32 devices in a mesh: expert: 16 (over z, y, core), dp: 2 (over x).
Axes of the slice: x: 2, y: 2, z: 4, core: 2. Of those that a mesh axis runs over, the one named last changes fastest.
Arguments:
- tokens: bfloat16 [768, 2048], P(('expert', 'dp')), may hold values from -6 to 6
- route_ids: int32 [768, 8], P(('expert', 'dp')), may hold values from 0 to 15, all different within a row; in each aligned block of 24 rows (0 to 23, 24 to 47, ...) at most 16 rows name the same one
- gates: float32 [768, 8], P(('expert', 'dp')), may hold values from 0.05 to 0.5
- cotangent: bfloat16 [768, 2048], P(('expert', 'dp')), may hold values from -1.5 to 1.5
- w_gate_up: bfloat16 [16, 2048, 768], P('expert', 'dp'), may hold values from -0.125 to 0.125
- w_down: bfloat16 [16, 2048, 384], P('expert', 'dp'), may hold values from -0.3125 to 0.3125
Outputs:
- mixed: bfloat16 [768, 2048], P(('expert', 'dp'))
- grad_tokens: bfloat16 [768, 2048], P(('expert', 'dp'))
- grad_gates: float32 [768, 8], P(('expert', 'dp'))
- grad_gate_up: bfloat16 [16, 2048, 768], P('expert', 'dp')
- grad_down: bfloat16 [16, 2048, 384], P('expert', 'dp')
The draws below stay inside these ranges and needn't reach their ends.
Inputs may be any that keep to these rules, and one draw needn't show every extreme that they name: `route_ids`: each row names 8 different experts. Among the 24 rows of one device no expert is named by more than 16 rows, and in every draw some device's rows name some expert exactly 16 times.
All inputs are finite; a program needn't handle non-finite values.
Results may differ from the reference program's by a relative error of at most 0.0064.
Values may be sent and summed in bfloat16 or wider, within the bound.
No kernel may reach another device: no remote copies, remote signals or barrier semaphores. Data moves between devices by JAX's collectives and lax.ppermute only.
A program may use at most 64 MiB of HBM per device.

```python
import math
import jax
import jax.numpy as jnp
import numpy as np
from jax import lax

D = 2048
TOP = 8
FFW = 384
TOK_DEV = 24
EXPERTS = 16
CAP = 16
TOKENS = 768
N_EXPERT = 16
N_DP = 2


def shard_levels(key, dims, cuts, low, top_value):
    def one(dim, blocks):
        heights = jax.random.uniform(jax.random.fold_in(jax.random.fold_in(key, 6), dim), (blocks,), jnp.float32, low / len(cuts), top_value / len(cuts))
        return jnp.repeat(jnp.exp(heights), dims[dim] // blocks).reshape((-1,) + (1,) * (len(dims) - dim - 1))

    gain = one(*cuts[0])
    for cut in cuts[1:]:
        gain = gain * one(*cut)
    return gain


def routed_block(rng, own, number, rows, count, top, reach, lean):
    order = jax.random.permutation(rng, count)
    heavy_load, usual = shares(count, rows * top, reach, lean, True), shares(count, rows * top, reach, lean, False)
    places = jnp.arange(count)

    def named(tallies, turn):
        used = int((tallies > 0).sum())
        fixed = max(1, used // 4)
        passed = fixed + (places - fixed + turn * (used - fixed)) % max(1, count - fixed)
        return jnp.zeros((count,), jnp.int32).at[order[jnp.where(places < fixed, places, passed)]].set(jnp.asarray(tallies, jnp.int32))

    tallies = jnp.where(number % 4 == 0, named(heavy_load, number // 4), named(usual, number - number // 4 - 1))
    mixed = jax.random.permutation(jax.random.fold_in(own, 3), count)
    giver, taker = mixed[0:count // 2 * 2:2], mixed[1:count // 2 * 2:2]
    slack = jnp.minimum(tallies[giver] - 1, reach - tallies[taker]) // 2
    slack = jnp.where((giver == order[0]) | (taker == order[0]) | (tallies[taker] == 0), 0, jnp.maximum(slack, 0))
    passed = jax.random.randint(jax.random.fold_in(own, 4), (count // 2,), 0, 1 << 20) % (slack + 1)
    tallies = tallies.at[giver].add(-passed).at[taker].add(passed)
    items = jnp.searchsorted(jnp.cumsum(tallies), jnp.arange(rows * top), side="right").astype(jnp.int32)
    table = items.reshape(top, rows).T
    table = table[jax.random.permutation(jax.random.fold_in(own, 1), rows)]
    turn = jax.random.randint(jax.random.fold_in(own, 2), (rows, 1), 0, top)
    return jnp.take_along_axis(table, (jnp.arange(top)[None, :] + turn) % top, axis=1)


def shares(count, total, bound, skew, full):
    loads = [(1 << 20) // math.isqrt(rank ** skew) + 1 for rank in range(1, count + 1)]
    largest = bound if full else min(bound, max(-(-total // count), total * loads[0] // sum(loads)))
    least = 1 if total - largest >= count - 1 else 0
    counts, rest = [largest] + [least] * (count - 1), total - largest - least * (count - 1)
    while rest > 0:
        candidates = [i for i in range(1, count) if counts[i] < largest] or [i for i in range(1, count) if counts[i] < bound]
        whole, budget = sum([loads[i] for i in candidates]), rest
        for i in candidates:
            more = min(bound - counts[i], max(1, budget * loads[i] // whole), rest)
            counts[i] = counts[i] + more
            rest = rest - more
    return np.array(counts)


def centred(own_key, extent, deviation, reach, shards=(), kind=jnp.bfloat16):
    loudness = shard_levels(own_key, extent, shards, -0.22, 0.18) if shards else 1.0
    values = jax.random.normal(own_key, extent, jnp.float32) * deviation * loudness
    return jnp.minimum(jnp.maximum(values, -reach), reach).astype(kind)


def setup_inputs(seed: int = 0) -> dict:
    key_of = jax.random.split(jax.random.key(seed), 7)
    tokens = centred(key_of[0], (TOKENS, D), 1.0, 6.0, ((0, 32),))
    route_ids_keys = jax.random.split(jax.random.fold_in(key_of[1], 1), TOKENS // TOK_DEV)
    route_ids_turns = jax.random.permutation(jax.random.fold_in(key_of[1], 3), TOKENS // TOK_DEV)
    route_ids = jax.vmap(lambda own, number: routed_block(jax.random.fold_in(key_of[1], 2), own, number, TOK_DEV, EXPERTS, TOP, CAP, 2))(route_ids_keys, route_ids_turns).reshape((TOKENS, TOP))
    gates = jnp.clip(0.05 + 0.45 * jax.random.uniform(key_of[2], (TOKENS, TOP), jnp.float32) ** shard_levels(key_of[2], (TOKENS, TOP), ((0, 32),), -0.2, 0.2), 0.05, 0.5)
    cotangent = centred(key_of[3], (TOKENS, D), 0.25, 1.5, ((0, 32),))
    w_gate_up = centred(key_of[4], (EXPERTS, D, 2 * FFW), D ** -0.5, 0.125, ((0, 16), (1, 2)))
    w_down = centred(key_of[5], (EXPERTS, D, FFW), FFW ** -0.5, 0.3125, ((0, 16), (1, 2)))
    return dict(tokens=tokens, route_ids=route_ids, gates=gates, cotangent=cotangent, w_gate_up=w_gate_up, w_down=w_down)


def reference(tokens, route_ids, gates, cotangent, w_gate_up, w_down):
    blocks = N_EXPERT * N_DP
    per_block = TOK_DEV * TOP
    slot_count = N_EXPERT * CAP
    expert_ids = route_ids.reshape(blocks, per_block)
    onehot = (expert_ids[:, :, None] == jnp.arange(EXPERTS, dtype=jnp.int32)[None, None, :]).astype(jnp.int32)
    earlier = jnp.sum((jnp.cumsum(onehot, axis=1, dtype=jnp.int32) - onehot) * onehot, axis=2, dtype=jnp.int32)
    block_index = jnp.arange(blocks, dtype=jnp.int32)
    position = (block_index // N_DP)[:, None] * CAP + earlier
    replica_of = jnp.broadcast_to((block_index % N_DP)[:, None], (blocks, per_block)).astype(jnp.int32)
    assign = jnp.arange(blocks * per_block, dtype=jnp.int32).reshape(blocks, per_block)
    slot_table = jnp.full((EXPERTS, N_DP, slot_count), blocks * per_block, jnp.int32)
    slot_table = slot_table.at[expert_ids, replica_of, position].set(assign)

    tok_pad = jnp.concatenate([tokens, jnp.zeros((1, D), jnp.bfloat16)], axis=0)
    cot_pad = jnp.concatenate([cotangent, jnp.zeros((1, D), jnp.bfloat16)], axis=0)
    gate_pad = jnp.concatenate([gates.reshape(-1), jnp.zeros((1,), jnp.float32)], axis=0)

    def expert_step(totals, inputs):
        mixed_acc, back_acc, score_acc = totals
        slots, weight_in, weight_out = inputs
        sum_gate_up = jnp.zeros((D, 2 * FFW), jnp.float32)
        sum_down = jnp.zeros((D, FFW), jnp.float32)
        for replica in range(N_DP):
            slot_index = slots[replica]
            token_row = slot_index // TOP
            x_rows = tok_pad[token_row]
            dy_rows = cot_pad[token_row]
            weight = gate_pad[slot_index]
            row_grad = (weight[:, None] * dy_rows.astype(jnp.float32)).astype(jnp.bfloat16)
            pre_act = jnp.dot(x_rows, weight_in, preferred_element_type=jnp.float32)
            gate_pre = pre_act[:, :FFW]
            up_pre = pre_act[:, FFW:]
            sigmoid_gate = jax.nn.sigmoid(gate_pre)
            activation = gate_pre * sigmoid_gate
            hidden = (activation * up_pre).astype(jnp.bfloat16)
            expert_out = jnp.dot(hidden, weight_out.T, preferred_element_type=jnp.float32).astype(jnp.bfloat16)
            hidden_grad = jnp.dot(row_grad, weight_out, preferred_element_type=jnp.float32)
            gate_grad = (hidden_grad * up_pre * (sigmoid_gate * (1.0 + gate_pre * (1.0 - sigmoid_gate)))).astype(jnp.bfloat16)
            up_grad = (hidden_grad * activation).astype(jnp.bfloat16)
            pair_grad = jnp.concatenate([gate_grad, up_grad], axis=1)
            input_grad = jnp.dot(pair_grad, weight_in.T, preferred_element_type=jnp.float32).astype(jnp.bfloat16)
            part_gate_up = jnp.dot(x_rows.T, pair_grad, preferred_element_type=jnp.float32).astype(jnp.bfloat16)
            part_down = jnp.dot(row_grad.T, hidden, preferred_element_type=jnp.float32).astype(jnp.bfloat16)
            sum_gate_up = sum_gate_up + lax.optimization_barrier(part_gate_up).astype(jnp.float32)
            sum_down = sum_down + lax.optimization_barrier(part_down).astype(jnp.float32)
            out_wide = expert_out.astype(jnp.float32)
            mixed_acc = mixed_acc.at[token_row].add(weight[:, None] * out_wide)
            back_acc = back_acc.at[token_row].add(input_grad.astype(jnp.float32))
            score_acc = score_acc.at[slot_index].add(jnp.sum(dy_rows.astype(jnp.float32) * out_wide, axis=1))
        return (mixed_acc, back_acc, score_acc), (sum_gate_up.astype(jnp.bfloat16), sum_down.astype(jnp.bfloat16))

    start = (jnp.zeros((TOKENS + 1, D), jnp.float32), jnp.zeros((TOKENS + 1, D), jnp.float32), jnp.zeros((TOKENS * TOP + 1,), jnp.float32))
    totals, grads = lax.scan(expert_step, start, (slot_table, w_gate_up, w_down))
    mixed_acc, back_acc, score_acc = totals
    mixed = mixed_acc[:TOKENS].astype(jnp.bfloat16)
    grad_tokens = back_acc[:TOKENS].astype(jnp.bfloat16)
    grad_gates = score_acc[:TOKENS * TOP].reshape(TOKENS, TOP)
    return (mixed, grad_tokens, grad_gates, grads[0], grads[1])
```

```python
import jax
import jax.numpy as jnp
from jax import lax
from jax.sharding import PartitionSpec as P


def expert_forward(x_rows, weight_in, weight_out, hidden_units):
    pre_act = jnp.dot(x_rows, weight_in, preferred_element_type=jnp.float32)
    gate_pre = pre_act[:, :hidden_units]
    up_pre = pre_act[:, hidden_units:]
    sigmoid_gate = jax.nn.sigmoid(gate_pre)
    activation = gate_pre * sigmoid_gate
    hidden = (activation * up_pre).astype(jnp.bfloat16)
    expert_out = lax.dot_general(
        hidden, weight_out, (((1,), (1,)), ((), ())), preferred_element_type=jnp.float32
    ).astype(jnp.bfloat16)
    return (gate_pre, up_pre, sigmoid_gate, activation, hidden, expert_out)


def expert_backward(saved, grad_rows, weight_in, weight_out):
    gate_pre, up_pre, sigmoid_gate, activation, hidden, expert_out = saved
    hidden_grad = jnp.dot(grad_rows, weight_out, preferred_element_type=jnp.float32)
    gate_grad = (
        hidden_grad * up_pre * (sigmoid_gate * (1.0 + gate_pre * (1.0 - sigmoid_gate)))
    ).astype(jnp.bfloat16)
    up_grad = (hidden_grad * activation).astype(jnp.bfloat16)
    pair_grad = jnp.concatenate([gate_grad, up_grad], axis=1)
    input_grad = lax.dot_general(
        pair_grad, weight_in, (((1,), (1,)), ((), ())), preferred_element_type=jnp.float32
    ).astype(jnp.bfloat16)
    return (pair_grad, input_grad)


def outer_blocks(left, right, pieces):
    span = left.shape[1] // pieces
    results = []
    for piece in range(pieces):
        product = lax.dot_general(
            left[:, piece * span : (piece + 1) * span],
            right,
            (((0,), (0,)), ((), ())),
            preferred_element_type=jnp.float32,
        )
        results.append(product.astype(jnp.bfloat16))
    return jnp.stack(results, axis=0)


def replica_total(received):
    return jnp.sum(received.astype(jnp.float32), axis=0).astype(jnp.bfloat16)


def body_by_slots(tokens, route_ids, gates, cotangent, w_gate_up, w_down):
    tok_dev, model_width = tokens.shape
    top_count = route_ids.shape[1]
    groups = lax.axis_size("expert")
    replicas = lax.axis_size("dp")
    local_experts = w_gate_up.shape[0]
    hidden_units = w_down.shape[2]
    experts = groups * local_experts
    assignments = tok_dev * top_count
    capacity = min(tok_dev, max(2, assignments // experts + max(1, assignments // (3 * experts))))
    flat_ids = route_ids.reshape(assignments)
    onehot = (flat_ids[:, None] == jnp.arange(experts, dtype=jnp.int32)[None, :]).astype(jnp.int32)
    earlier = jnp.sum(
        (jnp.cumsum(onehot, axis=0, dtype=jnp.int32) - onehot) * onehot, axis=1, dtype=jnp.int32
    )
    position = flat_ids * capacity + earlier
    source = (
        jnp.full((experts * capacity,), assignments, jnp.int32)
        .at[position]
        .set(jnp.arange(assignments, dtype=jnp.int32))
    )
    token_row = source // top_count
    tok_pad = jnp.concatenate([tokens, jnp.zeros((1, model_width), jnp.bfloat16)], axis=0)
    cot_pad = jnp.concatenate([cotangent, jnp.zeros((1, model_width), jnp.bfloat16)], axis=0)
    gate_pad = jnp.concatenate([gates.reshape(assignments), jnp.zeros((1,), jnp.float32)], axis=0)
    send_rows = tok_pad[token_row].reshape(experts, capacity, model_width)
    send_grads = (gate_pad[source][:, None] * cot_pad[token_row].astype(jnp.float32)).astype(
        jnp.bfloat16
    )
    send_grads = send_grads.reshape(experts, capacity, model_width)
    weights_in, weights_out = (
        lax.all_gather(w_gate_up, "dp", axis=1, tiled=True),
        lax.all_gather(w_down, "dp", axis=1, tiled=True),
    )
    rows_in, grads_in = (
        lax.all_to_all(send_rows, "expert", split_axis=0, concat_axis=1, tiled=True),
        lax.all_to_all(send_grads, "expert", split_axis=0, concat_axis=1, tiled=True),
    )
    local = 0
    forward_parts = expert_forward(
        rows_in[local], weights_in[local], weights_out[local], hidden_units
    )
    saved_all = [forward_parts]
    out_list = [forward_parts[5]]
    down_list = [outer_blocks(grads_in[local], forward_parts[4], replicas)]
    expert_outs = jnp.stack(out_list, axis=0)
    down_stack = jnp.stack(down_list, axis=1)
    outs_back = lax.all_to_all(expert_outs, "expert", split_axis=1, concat_axis=0, tiled=True)
    local = 0
    pair_grad, input_grad = expert_backward(
        saved_all[local], grads_in[local], weights_in[local], weights_out[local]
    )
    input_list = [input_grad]
    gate_up_list = [outer_blocks(rows_in[local], pair_grad, replicas)]
    input_grads = jnp.stack(input_list, axis=0)
    gate_up_stack = jnp.stack(gate_up_list, axis=1)
    grads_back = lax.all_to_all(input_grads, "expert", split_axis=1, concat_axis=0, tiled=True)
    gate_up_received, down_received = (
        lax.all_to_all(gate_up_stack, "dp", split_axis=0, concat_axis=0, tiled=True),
        lax.all_to_all(down_stack, "dp", split_axis=0, concat_axis=0, tiled=True),
    )
    grad_gate_up = replica_total(gate_up_received)
    grad_down = replica_total(down_received)
    out_rows = outs_back.reshape(experts * capacity, model_width)[position].reshape(
        tok_dev, top_count, model_width
    )
    mixed = jnp.sum(gates[:, :, None] * out_rows.astype(jnp.float32), axis=1).astype(jnp.bfloat16)
    grad_gates = jnp.einsum("td,tkd->tk", cotangent, out_rows, preferred_element_type=jnp.float32)
    back_rows = grads_back.reshape(experts * capacity, model_width)[position].reshape(
        tok_dev, top_count, model_width
    )
    grad_tokens = jnp.sum(back_rows.astype(jnp.float32), axis=1).astype(jnp.bfloat16)
    return (mixed, grad_tokens, grad_gates, grad_gate_up, grad_down)


def split_gates(route_ids, gates, experts):
    named = route_ids[:, :, None] == jnp.arange(experts, dtype=jnp.int32)[None, None, :]
    dense = jnp.sum(jnp.where(named, gates[:, :, None], 0.0), axis=1)
    terms = []
    rest = dense
    for _ in range(3):
        term = rest.astype(jnp.bfloat16)
        rest = rest - term.astype(jnp.float32)
        terms.append(term)
    return jnp.concatenate(terms, axis=1)


def swap_pair(value):
    return lax.ppermute(value, "dp", [(0, 1), (1, 0)])


def by_replica(own, other, replica):
    return jnp.where(replica == 0, jnp.stack([own, other]), jnp.stack([other, own]))


def body_by_width(tokens, route_ids, gates, cotangent, w_gate_up, w_down):
    tok_dev, model_width = tokens.shape
    top_count = route_ids.shape[1]
    groups = lax.axis_size("expert")
    replica = lax.axis_index("dp")
    expert = lax.axis_index("expert")
    half = w_gate_up.shape[1]
    hidden_units = w_down.shape[2]
    capacity = slot_capacity(tok_dev, top_count, groups)
    slots = 2 * groups * capacity
    rows = 2 * groups * tok_dev
    weight_in, weight_out = w_gate_up[0], w_down[0]
    f32, bf16 = jnp.float32, jnp.bfloat16

    meta = split_gates(route_ids, gates, groups)
    meta = jnp.pad(meta, ((0, 0), (0, -meta.shape[1] % 128)))

    def halves(value):
        return (
            lax.dynamic_slice_in_dim(value, replica * half, half, 1),
            lax.dynamic_slice_in_dim(value, (1 - replica) * half, half, 1),
        )

    tok_keep, tok_send = halves(tokens)
    cot_keep, cot_send = halves(cotangent)
    tok_other = swap_pair(jnp.concatenate([tok_send, meta], axis=1))
    cot_other = swap_pair(cot_send)
    tok_pair = by_replica(jnp.concatenate([tok_keep, meta], axis=1), tok_other, replica)
    cot_pair = by_replica(cot_keep, cot_other, replica)
    tok_all = lax.all_gather(tok_pair, "expert", axis=0).reshape(rows, -1)
    cot_all = lax.all_gather(cot_pair, "expert", axis=0).reshape(rows, half)

    column = lax.rem(jnp.arange(meta.shape[1], dtype=jnp.int32), groups) == expert
    column = column & (jnp.arange(meta.shape[1]) < 3 * groups)
    gate = jnp.sum(jnp.where(column[None, :], tok_all[:, half:].astype(f32), 0.0), axis=1)
    routed = gate > 0.0
    rank = jnp.cumsum(routed.astype(jnp.int32)) - 1
    pick = (rank[None, :] == jnp.arange(slots, dtype=jnp.int32)[:, None]) & routed[None, :]
    pick_b = pick.astype(bf16)
    gate_slot = jnp.sum(jnp.where(pick, gate[None, :], 0.0), axis=1)

    x_rows = jnp.dot(pick_b, tok_all[:, :half], preferred_element_type=f32).astype(bf16)
    pre_part = jnp.dot(x_rows, weight_in, preferred_element_type=f32)
    pre = pre_part + swap_pair(pre_part.astype(bf16)).astype(f32)

    scaled = (gate[:, None] * cot_all.astype(f32)).astype(bf16)
    grad_rows = jnp.dot(pick_b, scaled, preferred_element_type=f32).astype(bf16)
    hg_part = jnp.dot(grad_rows, weight_out, preferred_element_type=f32)
    hidden_grad = hg_part + swap_pair(hg_part.astype(bf16)).astype(f32)

    gate_pre, up_pre = pre[:, :hidden_units], pre[:, hidden_units:]
    sig = jax.nn.sigmoid(gate_pre)
    act = gate_pre * sig
    hidden = (act * up_pre).astype(bf16)
    out = lax.dot_general(hidden, weight_out, (((1,), (1,)), ((), ())), preferred_element_type=f32)
    out = (gate_slot[:, None] * out).astype(bf16)
    score = jnp.sum(hidden.astype(f32) * hidden_grad, axis=1) / jnp.where(gate_slot > 0, gate_slot, 1.0)

    def spread(value):
        return lax.dot_general(pick_b, value, (((0,), (0,)), ((), ())), preferred_element_type=f32).astype(bf16)

    score_row = jnp.sum(jnp.where(pick, score[:, None], 0.0), axis=0)
    score_hi = score_row.astype(bf16)
    score_lo = (score_row - score_hi.astype(f32)).astype(bf16)
    lane = jnp.arange(128)
    score_cols = jnp.where(lane[None, :] == expert, score_hi[:, None], 0) + jnp.where(
        lane[None, :] == expert + groups, score_lo[:, None], 0
    )
    mixed_part = jnp.concatenate([spread(out), score_cols.astype(bf16)], axis=1)

    gate_grad = (hidden_grad * up_pre * (sig * (1.0 + gate_pre * (1.0 - sig)))).astype(bf16)
    up_grad = (hidden_grad * act).astype(bf16)
    pair_grad = jnp.concatenate([gate_grad, up_grad], axis=1)
    back = lax.dot_general(pair_grad, weight_in, (((1,), (1,)), ((), ())), preferred_element_type=f32)
    back_part = spread(back.astype(bf16))

    def outer(left, right):
        return lax.dot_general(left, right, (((0,), (0,)), ((), ())), preferred_element_type=f32).astype(bf16)

    grad_gate_up = outer(x_rows, pair_grad)[None]
    grad_down = outer(grad_rows, hidden)[None]

    def total(value):
        return lax.psum_scatter(
            value.reshape(groups, 2, tok_dev, value.shape[1]), "expert", scatter_dimension=0
        )

    def rows_home(value):
        own = lax.dynamic_index_in_dim(value, replica, 0, keepdims=False)
        other = swap_pair(lax.dynamic_index_in_dim(value, 1 - replica, 0, keepdims=False))
        both = by_replica(own, other, replica)
        return jnp.concatenate([both[0], both[1]], axis=1)

    mixed_sum = total(mixed_part)
    back_sum = total(back_part)
    mixed = rows_home(mixed_sum[:, :, :half])
    grad_tokens = rows_home(back_sum)
    own_scores = lax.dynamic_index_in_dim(mixed_sum, replica, 0, keepdims=False)[:, half:].astype(f32)
    own_scores = own_scores[:, :groups] + own_scores[:, groups : 2 * groups]
    named = route_ids[:, :, None] == jnp.arange(groups, dtype=jnp.int32)[None, None, :]
    grad_gates = jnp.sum(jnp.where(named, own_scores[:, None, :], 0.0), axis=2)
    return (mixed, grad_tokens, grad_gates, grad_gate_up, grad_down)


def slot_capacity(tok_dev, top_count, experts):
    assignments = tok_dev * top_count
    return min(tok_dev, max(2, assignments // experts + max(1, assignments // (3 * experts))))


def body(tokens, route_ids, gates, cotangent, w_gate_up, w_down):
    groups, replicas = lax.axis_size("expert"), lax.axis_size("dp")
    gathered = 2 * groups * tokens.shape[0] * replicas * w_gate_up.shape[1] * 2
    small = gathered <= 8 * 1024 * 1024 and 3 * groups <= 128
    if replicas == 2 and w_gate_up.shape[0] == 1 and small:
        return body_by_width(tokens, route_ids, gates, cotangent, w_gate_up, w_down)
    return body_by_slots(tokens, route_ids, gates, cotangent, w_gate_up, w_down)


def solution(mesh):
    placed = (
        P(("expert", "dp"), None),
        P(("expert", "dp"), None),
        P(("expert", "dp"), None),
        P(("expert", "dp"), None),
        P("expert", "dp", None),
        P("expert", "dp", None),
    )
    return jax.shard_map(
        body,
        mesh=mesh,
        in_specs=placed,
        out_specs=(
            P(("expert", "dp"), None),
            P(("expert", "dp"), None),
            P(("expert", "dp"), None),
            P("expert", "dp", None),
            P("expert", "dp", None),
        ),
        check_vma=False,
    )
```

```python
import jax
import jax.numpy as jnp
from jax import lax
from jax.sharding import PartitionSpec as P


def expert_forward(x_rows, weight_in, weight_out, hidden_units):
    pre_act = jnp.dot(x_rows, weight_in, preferred_element_type=jnp.float32)
    gate_pre = pre_act[:, :hidden_units]
    up_pre = pre_act[:, hidden_units:]
    sigmoid_gate = jax.nn.sigmoid(gate_pre)
    activation = gate_pre * sigmoid_gate
    hidden = (activation * up_pre).astype(jnp.bfloat16)
    expert_out = lax.dot_general(
        hidden, weight_out, (((1,), (1,)), ((), ())), preferred_element_type=jnp.float32
    ).astype(jnp.bfloat16)
    return (gate_pre, up_pre, sigmoid_gate, activation, hidden, expert_out)


def expert_backward(saved, grad_rows, weight_in, weight_out):
    gate_pre, up_pre, sigmoid_gate, activation, hidden, expert_out = saved
    hidden_grad = jnp.dot(grad_rows, weight_out, preferred_element_type=jnp.float32)
    gate_grad = (
        hidden_grad * up_pre * (sigmoid_gate * (1.0 + gate_pre * (1.0 - sigmoid_gate)))
    ).astype(jnp.bfloat16)
    up_grad = (hidden_grad * activation).astype(jnp.bfloat16)
    pair_grad = jnp.concatenate([gate_grad, up_grad], axis=1)
    input_grad = lax.dot_general(
        pair_grad, weight_in, (((1,), (1,)), ((), ())), preferred_element_type=jnp.float32
    ).astype(jnp.bfloat16)
    return (pair_grad, input_grad)


def outer_blocks(left, right, pieces):
    span = left.shape[1] // pieces
    results = []
    for piece in range(pieces):
        product = lax.dot_general(
            left[:, piece * span : (piece + 1) * span],
            right,
            (((0,), (0,)), ((), ())),
            preferred_element_type=jnp.float32,
        )
        results.append(product.astype(jnp.bfloat16))
    return jnp.stack(results, axis=0)


def replica_total(received):
    return jnp.sum(received.astype(jnp.float32), axis=0).astype(jnp.bfloat16)


def body_by_slots(tokens, route_ids, gates, cotangent, w_gate_up, w_down):
    tok_dev, model_width = tokens.shape
    top_count = route_ids.shape[1]
    groups = lax.axis_size("expert")
    replicas = lax.axis_size("dp")
    local_experts = w_gate_up.shape[0]
    hidden_units = w_down.shape[2]
    experts = groups * local_experts
    assignments = tok_dev * top_count
    capacity = min(tok_dev, max(2, assignments // experts + max(1, assignments // (3 * experts))))
    flat_ids = route_ids.reshape(assignments)
    onehot = (flat_ids[:, None] == jnp.arange(experts, dtype=jnp.int32)[None, :]).astype(jnp.int32)
    earlier = jnp.sum(
        (jnp.cumsum(onehot, axis=0, dtype=jnp.int32) - onehot) * onehot, axis=1, dtype=jnp.int32
    )
    position = flat_ids * capacity + earlier
    source = (
        jnp.full((experts * capacity,), assignments, jnp.int32)
        .at[position]
        .set(jnp.arange(assignments, dtype=jnp.int32))
    )
    token_row = source // top_count
    tok_pad = jnp.concatenate([tokens, jnp.zeros((1, model_width), jnp.bfloat16)], axis=0)
    cot_pad = jnp.concatenate([cotangent, jnp.zeros((1, model_width), jnp.bfloat16)], axis=0)
    gate_pad = jnp.concatenate([gates.reshape(assignments), jnp.zeros((1,), jnp.float32)], axis=0)
    send_rows = tok_pad[token_row].reshape(experts, capacity, model_width)
    send_grads = (gate_pad[source][:, None] * cot_pad[token_row].astype(jnp.float32)).astype(
        jnp.bfloat16
    )
    send_grads = send_grads.reshape(experts, capacity, model_width)
    weights_in, weights_out = (
        lax.all_gather(w_gate_up, "dp", axis=1, tiled=True),
        lax.all_gather(w_down, "dp", axis=1, tiled=True),
    )
    rows_in, grads_in = (
        lax.all_to_all(send_rows, "expert", split_axis=0, concat_axis=1, tiled=True),
        lax.all_to_all(send_grads, "expert", split_axis=0, concat_axis=1, tiled=True),
    )
    local = 0
    forward_parts = expert_forward(
        rows_in[local], weights_in[local], weights_out[local], hidden_units
    )
    saved_all = [forward_parts]
    out_list = [forward_parts[5]]
    down_list = [outer_blocks(grads_in[local], forward_parts[4], replicas)]
    expert_outs = jnp.stack(out_list, axis=0)
    down_stack = jnp.stack(down_list, axis=1)
    outs_back = lax.all_to_all(expert_outs, "expert", split_axis=1, concat_axis=0, tiled=True)
    local = 0
    pair_grad, input_grad = expert_backward(
        saved_all[local], grads_in[local], weights_in[local], weights_out[local]
    )
    input_list = [input_grad]
    gate_up_list = [outer_blocks(rows_in[local], pair_grad, replicas)]
    input_grads = jnp.stack(input_list, axis=0)
    gate_up_stack = jnp.stack(gate_up_list, axis=1)
    grads_back = lax.all_to_all(input_grads, "expert", split_axis=1, concat_axis=0, tiled=True)
    gate_up_received, down_received = (
        lax.all_to_all(gate_up_stack, "dp", split_axis=0, concat_axis=0, tiled=True),
        lax.all_to_all(down_stack, "dp", split_axis=0, concat_axis=0, tiled=True),
    )
    grad_gate_up = replica_total(gate_up_received)
    grad_down = replica_total(down_received)
    out_rows = outs_back.reshape(experts * capacity, model_width)[position].reshape(
        tok_dev, top_count, model_width
    )
    mixed = jnp.sum(gates[:, :, None] * out_rows.astype(jnp.float32), axis=1).astype(jnp.bfloat16)
    grad_gates = jnp.einsum("td,tkd->tk", cotangent, out_rows, preferred_element_type=jnp.float32)
    back_rows = grads_back.reshape(experts * capacity, model_width)[position].reshape(
        tok_dev, top_count, model_width
    )
    grad_tokens = jnp.sum(back_rows.astype(jnp.float32), axis=1).astype(jnp.bfloat16)
    return (mixed, grad_tokens, grad_gates, grad_gate_up, grad_down)


def split_gates(route_ids, gates, experts):
    named = route_ids[:, :, None] == jnp.arange(experts, dtype=jnp.int32)[None, None, :]
    dense = jnp.sum(jnp.where(named, gates[:, :, None], 0.0), axis=1)
    terms = []
    rest = dense
    for _ in range(3):
        term = rest.astype(jnp.bfloat16)
        rest = rest - term.astype(jnp.float32)
        terms.append(term)
    return jnp.concatenate(terms, axis=1)


def swap_pair(value):
    return lax.ppermute(value, "dp", [(0, 1), (1, 0)])


def by_replica(own, other, replica):
    return jnp.where(replica == 0, jnp.stack([own, other]), jnp.stack([other, own]))


def ring_pairs(groups):
    chips = groups // 2
    levels = chips // 2
    order = [2 * z for z in range(levels)] + [2 * z + 1 for z in reversed(range(levels))]
    forward = []
    for place in range(chips):
        forward.append((2 * order[place], 2 * order[(place + 1) % chips]))
        forward.append((2 * order[(place + 1) % chips] + 1, 2 * order[place] + 1))
    backward = [(to, source) for source, to in forward]
    cores = [(index, index ^ 1) for index in range(groups)]
    return forward, backward, cores


def body_by_width(tokens, route_ids, gates, cotangent, w_gate_up, w_down):
    tok_dev, model_width = tokens.shape
    top_count = route_ids.shape[1]
    groups = lax.axis_size("expert")
    replica = lax.axis_index("dp")
    expert = lax.axis_index("expert")
    half = w_gate_up.shape[1]
    hidden_units = w_down.shape[2]
    capacity = slot_capacity(tok_dev, top_count, groups)
    devices = 2 * groups
    rows = devices * tok_dev
    steps = groups // 4
    weight_in, weight_out = w_gate_up[0], w_down[0]
    f32, bf16 = jnp.float32, jnp.bfloat16
    forward, backward, cores = ring_pairs(groups)
    unit = 2 * tok_dev

    def swap_cores(value):
        return lax.ppermute(value, "expert", cores)

    meta = split_gates(route_ids, gates, groups)
    meta = jnp.pad(meta, ((0, 0), (0, -meta.shape[1] % 128)))

    def halves(value):
        return (
            lax.dynamic_slice_in_dim(value, replica * half, half, 1),
            lax.dynamic_slice_in_dim(value, (1 - replica) * half, half, 1),
        )

    def gather_rows(pair):
        block = jnp.concatenate([pair, swap_cores(pair)], axis=0)
        own, mine = block, []
        for step in range(steps):
            block = lax.ppermute(block if step < steps - 1 else block[:unit], "expert", forward)
            mine.append(block)
        mine = jnp.concatenate(mine, axis=0)
        return jnp.concatenate([own, mine, swap_cores(mine)], axis=0)

    def scatter_sum(part):
        far = (rows - 2 * unit) // 2
        own = part[: 2 * unit].astype(f32)
        mine = part[2 * unit : 2 * unit + far].astype(f32)
        mine = mine + swap_cores(part[2 * unit + far :].astype(bf16)).astype(f32)
        total = mine[(steps - 1) * 2 * unit :]
        for step in reversed(range(steps)):
            came = lax.ppermute(total.astype(bf16), "expert", backward).astype(f32)
            base = own if step == 0 else mine[(step - 1) * 2 * unit : step * 2 * unit]
            if came.shape[0] == unit:
                total = jnp.concatenate([base[:unit] + came, base[unit:]], axis=0)
            else:
                total = base + came
        return total[:unit] + swap_cores(total[unit:].astype(bf16)).astype(f32)

    def rows_home(value):
        value = value.reshape(2, tok_dev, half)
        own = lax.dynamic_index_in_dim(value, replica, 0, keepdims=False).astype(bf16)
        other = swap_pair(lax.dynamic_index_in_dim(value, 1 - replica, 0, keepdims=False).astype(bf16))
        both = by_replica(own, other, replica)
        return jnp.concatenate([both[0], both[1]], axis=1)

    tok_keep, tok_send = halves(tokens)
    cot_keep, cot_send = halves(cotangent)
    tok_other = swap_pair(jnp.concatenate([tok_send, meta], axis=1))
    cot_other = swap_pair(cot_send)
    tok_pair = by_replica(jnp.concatenate([tok_keep, meta], axis=1), tok_other, replica).reshape(unit, -1)
    cot_pair = by_replica(cot_keep, cot_other, replica).reshape(unit, half)
    tok_all = gather_rows(tok_pair)
    cot_all = gather_rows(cot_pair)

    lane = jnp.arange(meta.shape[1], dtype=jnp.int32)
    column = (lax.rem(lane, groups) == expert) & (lane < 3 * groups)
    gate = jnp.sum(jnp.where(column[None, :], tok_all[:, half:].astype(f32), 0.0), axis=1)
    routed = gate > 0.0
    batch = 8 if devices % 8 == 0 else devices
    blocks = devices // batch
    by_device = routed.reshape(devices, tok_dev)
    earlier = jnp.arange(tok_dev)[:, None] < jnp.arange(tok_dev)[None, :]
    rank = jnp.sum(jnp.where(earlier[None] & by_device[:, :, None], 1, 0), axis=1, dtype=jnp.int32)
    place = rank + (jnp.arange(devices, dtype=jnp.int32) % batch * capacity)[:, None]
    place = jnp.where(by_device, place, -1).reshape(blocks, 1, batch * tok_dev)
    pick = place == jnp.arange(batch * capacity, dtype=jnp.int32)[None, :, None]
    pick_b = pick.astype(bf16)
    gate_blocks = gate.reshape(blocks, 1, batch * tok_dev)
    gate_slot = jnp.sum(jnp.where(pick, gate_blocks, 0.0), axis=2).reshape(-1)

    def to_slots(value):
        value = value.reshape(blocks, batch * tok_dev, value.shape[1])
        return jnp.einsum("bsr,brd->bsd", pick_b, value, preferred_element_type=f32).astype(bf16).reshape(-1, value.shape[2])

    def to_rows(value):
        value = value.reshape(blocks, batch * capacity, value.shape[1])
        return jnp.einsum("bsr,bsd->brd", pick_b, value, preferred_element_type=f32).astype(bf16).reshape(rows, -1)

    x_rows = to_slots(tok_all[:, :half])
    pre_part = jnp.dot(x_rows, weight_in, preferred_element_type=f32)
    pre = pre_part + swap_pair(pre_part.astype(bf16)).astype(f32)

    grad_rows = to_slots(cot_all)
    grad_rows = (gate_slot[:, None] * grad_rows.astype(f32)).astype(bf16)
    hg_part = jnp.dot(grad_rows, weight_out, preferred_element_type=f32)
    hidden_grad = hg_part + swap_pair(hg_part.astype(bf16)).astype(f32)

    gate_pre, up_pre = pre[:, :hidden_units], pre[:, hidden_units:]
    sig = jax.nn.sigmoid(gate_pre)
    act = gate_pre * sig
    hidden = (act * up_pre).astype(bf16)
    out = lax.dot_general(hidden, weight_out, (((1,), (1,)), ((), ())), preferred_element_type=f32)
    out = (gate_slot[:, None] * out).astype(bf16)
    mixed = rows_home(scatter_sum(to_rows(out)))

    gate_grad = (hidden_grad * up_pre * (sig * (1.0 + gate_pre * (1.0 - sig)))).astype(bf16)
    up_grad = (hidden_grad * act).astype(bf16)
    pair_grad = jnp.concatenate([gate_grad, up_grad], axis=1)
    back = lax.dot_general(pair_grad, weight_in, (((1,), (1,)), ((), ())), preferred_element_type=f32)

    score = jnp.sum(hidden.astype(f32) * hidden_grad, axis=1) / jnp.where(gate_slot > 0, gate_slot, 1.0)
    score = jnp.sum(jnp.where(pick, score.reshape(blocks, -1, 1), 0.0), axis=1).reshape(rows, 1)
    score_hi = score.astype(bf16)
    score_lo = (score - score_hi.astype(f32)).astype(bf16)
    lane = jnp.arange(128)[None, :]
    score_cols = jnp.where(lane == expert, score_hi, 0) + jnp.where(lane == expert + groups, score_lo, 0)
    back_sum = scatter_sum(jnp.concatenate([to_rows(back.astype(bf16)), score_cols.astype(bf16)], axis=1))
    grad_tokens = rows_home(back_sum[:, :half])

    def outer(left, right):
        return lax.dot_general(left, right, (((0,), (0,)), ((), ())), preferred_element_type=f32).astype(bf16)

    grad_gate_up = outer(x_rows, pair_grad)[None]
    grad_down = outer(grad_rows, hidden)[None]

    own_scores = back_sum[:, half:].reshape(2, tok_dev, -1)
    own_scores = lax.dynamic_index_in_dim(own_scores, replica, 0, keepdims=False)
    own_scores = own_scores[:, :groups] + own_scores[:, groups : 2 * groups]
    named = route_ids[:, :, None] == jnp.arange(groups, dtype=jnp.int32)[None, None, :]
    grad_gates = jnp.sum(jnp.where(named, own_scores[:, None, :], 0.0), axis=2)
    return (mixed, grad_tokens, grad_gates, grad_gate_up, grad_down)


def slot_capacity(tok_dev, top_count, experts):
    assignments = tok_dev * top_count
    return min(tok_dev, max(2, assignments // experts + max(1, assignments // (3 * experts))))


def body(tokens, route_ids, gates, cotangent, w_gate_up, w_down):
    groups, replicas = lax.axis_size("expert"), lax.axis_size("dp")
    gathered = 2 * groups * tokens.shape[0] * replicas * w_gate_up.shape[1] * 2
    small = gathered <= 8 * 1024 * 1024 and 3 * groups <= 128 and groups % 4 == 0
    if replicas == 2 and w_gate_up.shape[0] == 1 and small:
        return body_by_width(tokens, route_ids, gates, cotangent, w_gate_up, w_down)
    return body_by_slots(tokens, route_ids, gates, cotangent, w_gate_up, w_down)


def solution(mesh):
    placed = (
        P(("expert", "dp"), None),
        P(("expert", "dp"), None),
        P(("expert", "dp"), None),
        P(("expert", "dp"), None),
        P("expert", "dp", None),
        P("expert", "dp", None),
    )
    return jax.shard_map(
        body,
        mesh=mesh,
        in_specs=placed,
        out_specs=(
            P(("expert", "dp"), None),
            P(("expert", "dp"), None),
            P(("expert", "dp"), None),
            P("expert", "dp", None),
            P("expert", "dp", None),
        ),
        check_vma=False,
    )
```

```python
import jax
import jax.numpy as jnp
from jax import lax
from jax.sharding import PartitionSpec as P


def expert_forward(x_rows, weight_in, weight_out, hidden_units):
    pre_act = jnp.dot(x_rows, weight_in, preferred_element_type=jnp.float32)
    gate_pre = pre_act[:, :hidden_units]
    up_pre = pre_act[:, hidden_units:]
    sigmoid_gate = jax.nn.sigmoid(gate_pre)
    activation = gate_pre * sigmoid_gate
    hidden = (activation * up_pre).astype(jnp.bfloat16)
    expert_out = lax.dot_general(
        hidden, weight_out, (((1,), (1,)), ((), ())), preferred_element_type=jnp.float32
    ).astype(jnp.bfloat16)
    return (gate_pre, up_pre, sigmoid_gate, activation, hidden, expert_out)


def expert_backward(saved, grad_rows, weight_in, weight_out):
    gate_pre, up_pre, sigmoid_gate, activation, hidden, expert_out = saved
    hidden_grad = jnp.dot(grad_rows, weight_out, preferred_element_type=jnp.float32)
    gate_grad = (
        hidden_grad * up_pre * (sigmoid_gate * (1.0 + gate_pre * (1.0 - sigmoid_gate)))
    ).astype(jnp.bfloat16)
    up_grad = (hidden_grad * activation).astype(jnp.bfloat16)
    pair_grad = jnp.concatenate([gate_grad, up_grad], axis=1)
    input_grad = lax.dot_general(
        pair_grad, weight_in, (((1,), (1,)), ((), ())), preferred_element_type=jnp.float32
    ).astype(jnp.bfloat16)
    return (pair_grad, input_grad)


def outer_blocks(left, right, pieces):
    span = left.shape[1] // pieces
    results = []
    for piece in range(pieces):
        product = lax.dot_general(
            left[:, piece * span : (piece + 1) * span],
            right,
            (((0,), (0,)), ((), ())),
            preferred_element_type=jnp.float32,
        )
        results.append(product.astype(jnp.bfloat16))
    return jnp.stack(results, axis=0)


def replica_total(received):
    return jnp.sum(received.astype(jnp.float32), axis=0).astype(jnp.bfloat16)


def body_by_slots(tokens, route_ids, gates, cotangent, w_gate_up, w_down):
    tok_dev, model_width = tokens.shape
    top_count = route_ids.shape[1]
    groups = lax.axis_size("expert")
    replicas = lax.axis_size("dp")
    local_experts = w_gate_up.shape[0]
    hidden_units = w_down.shape[2]
    experts = groups * local_experts
    assignments = tok_dev * top_count
    capacity = min(tok_dev, max(2, assignments // experts + max(1, assignments // (3 * experts))))
    flat_ids = route_ids.reshape(assignments)
    onehot = (flat_ids[:, None] == jnp.arange(experts, dtype=jnp.int32)[None, :]).astype(jnp.int32)
    earlier = jnp.sum(
        (jnp.cumsum(onehot, axis=0, dtype=jnp.int32) - onehot) * onehot, axis=1, dtype=jnp.int32
    )
    position = flat_ids * capacity + earlier
    source = (
        jnp.full((experts * capacity,), assignments, jnp.int32)
        .at[position]
        .set(jnp.arange(assignments, dtype=jnp.int32))
    )
    token_row = source // top_count
    tok_pad = jnp.concatenate([tokens, jnp.zeros((1, model_width), jnp.bfloat16)], axis=0)
    cot_pad = jnp.concatenate([cotangent, jnp.zeros((1, model_width), jnp.bfloat16)], axis=0)
    gate_pad = jnp.concatenate([gates.reshape(assignments), jnp.zeros((1,), jnp.float32)], axis=0)
    send_rows = tok_pad[token_row].reshape(experts, capacity, model_width)
    send_grads = (gate_pad[source][:, None] * cot_pad[token_row].astype(jnp.float32)).astype(
        jnp.bfloat16
    )
    send_grads = send_grads.reshape(experts, capacity, model_width)
    weights_in, weights_out = (
        lax.all_gather(w_gate_up, "dp", axis=1, tiled=True),
        lax.all_gather(w_down, "dp", axis=1, tiled=True),
    )
    rows_in, grads_in = (
        lax.all_to_all(send_rows, "expert", split_axis=0, concat_axis=1, tiled=True),
        lax.all_to_all(send_grads, "expert", split_axis=0, concat_axis=1, tiled=True),
    )
    local = 0
    forward_parts = expert_forward(
        rows_in[local], weights_in[local], weights_out[local], hidden_units
    )
    saved_all = [forward_parts]
    out_list = [forward_parts[5]]
    down_list = [outer_blocks(grads_in[local], forward_parts[4], replicas)]
    expert_outs = jnp.stack(out_list, axis=0)
    down_stack = jnp.stack(down_list, axis=1)
    outs_back = lax.all_to_all(expert_outs, "expert", split_axis=1, concat_axis=0, tiled=True)
    local = 0
    pair_grad, input_grad = expert_backward(
        saved_all[local], grads_in[local], weights_in[local], weights_out[local]
    )
    input_list = [input_grad]
    gate_up_list = [outer_blocks(rows_in[local], pair_grad, replicas)]
    input_grads = jnp.stack(input_list, axis=0)
    gate_up_stack = jnp.stack(gate_up_list, axis=1)
    grads_back = lax.all_to_all(input_grads, "expert", split_axis=1, concat_axis=0, tiled=True)
    gate_up_received, down_received = (
        lax.all_to_all(gate_up_stack, "dp", split_axis=0, concat_axis=0, tiled=True),
        lax.all_to_all(down_stack, "dp", split_axis=0, concat_axis=0, tiled=True),
    )
    grad_gate_up = replica_total(gate_up_received)
    grad_down = replica_total(down_received)
    out_rows = outs_back.reshape(experts * capacity, model_width)[position].reshape(
        tok_dev, top_count, model_width
    )
    mixed = jnp.sum(gates[:, :, None] * out_rows.astype(jnp.float32), axis=1).astype(jnp.bfloat16)
    grad_gates = jnp.einsum("td,tkd->tk", cotangent, out_rows, preferred_element_type=jnp.float32)
    back_rows = grads_back.reshape(experts * capacity, model_width)[position].reshape(
        tok_dev, top_count, model_width
    )
    grad_tokens = jnp.sum(back_rows.astype(jnp.float32), axis=1).astype(jnp.bfloat16)
    return (mixed, grad_tokens, grad_gates, grad_gate_up, grad_down)


def split_gates(route_ids, gates, experts):
    named = route_ids[:, :, None] == jnp.arange(experts, dtype=jnp.int32)[None, None, :]
    dense = jnp.sum(jnp.where(named, gates[:, :, None], 0.0), axis=1)
    terms = []
    rest = dense
    for _ in range(3):
        term = rest.astype(jnp.bfloat16)
        rest = rest - term.astype(jnp.float32)
        terms.append(term)
    return jnp.concatenate(terms, axis=1)


def ring_pairs(groups):
    chips = groups // 2
    levels = chips // 2
    order = [2 * z for z in range(levels)] + [2 * z + 1 for z in reversed(range(levels))]
    forward = []
    for place in range(chips):
        forward.append((2 * order[place], 2 * order[(place + 1) % chips]))
        forward.append((2 * order[(place + 1) % chips] + 1, 2 * order[place] + 1))
    backward = [(to, source) for source, to in forward]
    cores = [(index, index ^ 1) for index in range(groups)]
    return forward, backward, cores


def swap_pair(value):
    return lax.ppermute(value, "dp", [(0, 1), (1, 0)])


def swap_both(value):
    groups = lax.axis_size("expert")
    pairs = [(2 * e + r, 2 * (e ^ 1) + 1 - r) for e in range(groups) for r in range(2)]
    return lax.ppermute(value, ("expert", "dp"), pairs)


def by_replica(own, other, replica):
    return jnp.where(replica == 0, jnp.stack([own, other]), jnp.stack([other, own]))


def body_by_width(tokens, route_ids, gates, cotangent, w_gate_up, w_down):
    tok_dev, model_width = tokens.shape
    top_count = route_ids.shape[1]
    groups = lax.axis_size("expert")
    replica = lax.axis_index("dp")
    expert = lax.axis_index("expert")
    half = w_gate_up.shape[1]
    hidden_units = w_down.shape[2]
    capacity = slot_capacity(tok_dev, top_count, groups)
    steps = groups // 4
    near_steps = steps // 2
    weight_in, weight_out = w_gate_up[0], w_down[0]
    f32, bf16 = jnp.float32, jnp.bfloat16
    forward, backward, cores = ring_pairs(groups)
    unit = 2 * tok_dev
    chip = 2 * unit

    def swap_cores(value):
        return lax.ppermute(value, "expert", cores)

    meta = split_gates(route_ids, gates, groups)
    meta = jnp.pad(meta, ((0, 0), (0, -meta.shape[1] % 128)))

    def halves(value):
        return (
            lax.dynamic_slice_in_dim(value, replica * half, half, 1),
            lax.dynamic_slice_in_dim(value, (1 - replica) * half, half, 1),
        )

    def chip_rows(keep, send):
        across, diagonal, beside = swap_pair(send), swap_both(send), swap_cores(keep)
        return jnp.concatenate(
            [by_replica(keep, across, replica), by_replica(beside, diagonal, replica)], axis=0
        ).reshape(chip, -1)

    def gather_rows(block):
        own, mine = block, []
        for step in range(steps):
            block = lax.ppermute(block if step < steps - 1 else block[:unit], "expert", forward)
            mine.append(block)
        near = jnp.concatenate(mine[:near_steps], axis=0)
        far = jnp.concatenate(mine[near_steps:], axis=0)
        return (
            jnp.concatenate([own, near, swap_cores(near)], axis=0),
            jnp.concatenate([far, swap_cores(far)], axis=0),
        )

    def scatter_sum(near, far):
        def both(value):
            return value[: value.shape[0] // 2].astype(f32) + swap_cores(value[value.shape[0] // 2 :]).astype(f32)

        far, own, near = both(far), near[:chip].astype(f32), both(near[chip:])
        terms = [own]
        terms += [near[step * chip : (step + 1) * chip] for step in range(near_steps)]
        terms += [far[step * chip : (step + 1) * chip] for step in range(steps - near_steps)]
        total = terms.pop()
        while terms:
            came = lax.ppermute(total.astype(bf16), "expert", backward).astype(f32)
            base = terms.pop()
            if came.shape[0] < chip:
                total = jnp.concatenate([base[:unit] + came, base[unit:]], axis=0)
            else:
                total = base + came
        return total

    def rows_home(value):
        value = value.reshape(2, 2, tok_dev, half).astype(bf16)
        mine = lax.dynamic_index_in_dim(value, replica, 1, keepdims=False)
        theirs = lax.dynamic_index_in_dim(value, 1 - replica, 1, keepdims=False)
        kept = mine[0].astype(f32) + swap_cores(mine[1]).astype(f32)
        other = swap_pair(theirs[0]).astype(f32) + swap_both(theirs[1]).astype(f32)
        both = by_replica(kept, other, replica)
        return jnp.concatenate([both[0], both[1]], axis=1).astype(bf16)

    tok_keep, tok_send = halves(tokens)
    cot_keep, cot_send = halves(cotangent)
    tok_near, tok_far = gather_rows(
        chip_rows(jnp.concatenate([tok_keep, meta], axis=1), jnp.concatenate([tok_send, meta], axis=1))
    )
    cot_near, cot_far = gather_rows(chip_rows(cot_keep, cot_send))

    lane = jnp.arange(meta.shape[1], dtype=jnp.int32)
    column = (lax.rem(lane, groups) == expert) & (lane < 3 * groups)

    def first_half(tok, cot):
        rows = tok.shape[0]
        devices = rows // tok_dev
        blocks = 2
        batch = devices // blocks
        gate = jnp.sum(jnp.where(column[None, :], tok[:, half:].astype(f32), 0.0), axis=1)
        routed = (gate > 0.0).reshape(devices, tok_dev)
        earlier = jnp.arange(tok_dev)[:, None] < jnp.arange(tok_dev)[None, :]
        rank = jnp.sum(jnp.where(earlier[None] & routed[:, :, None], 1, 0), axis=1, dtype=jnp.int32)
        place = rank + (jnp.arange(devices, dtype=jnp.int32) % batch * capacity)[:, None]
        place = jnp.where(routed, place, -1).reshape(blocks, 1, batch * tok_dev)
        pick = place == jnp.arange(batch * capacity, dtype=jnp.int32)[None, :, None]
        gate_slot = jnp.sum(jnp.where(pick, gate.reshape(blocks, 1, -1), 0.0), axis=2).reshape(-1)

        def to_slots(value):
            value = value.reshape(blocks, batch * tok_dev, value.shape[1])
            value = jnp.einsum("bsr,brd->bsd", pick.astype(bf16), value, preferred_element_type=f32)
            return value.astype(bf16).reshape(-1, value.shape[2])

        x_rows = to_slots(tok[:, :half])
        pre_part = jnp.dot(x_rows, weight_in, preferred_element_type=f32)
        grad_rows = to_slots(cot)
        grad_rows = (gate_slot[:, None] * grad_rows.astype(f32)).astype(bf16)
        hg_part = jnp.dot(grad_rows, weight_out, preferred_element_type=f32)
        return pick, gate_slot, x_rows, grad_rows, pre_part, hg_part

    def second_half(pick, gate_slot, pre, hidden_grad):
        blocks = pick.shape[0]

        def to_rows(value):
            value = value.reshape(blocks, -1, value.shape[1])
            value = jnp.einsum("bsr,bsd->brd", pick.astype(bf16), value, preferred_element_type=f32)
            return value.astype(bf16).reshape(-1, value.shape[2])

        gate_pre, up_pre = pre[:, :hidden_units], pre[:, hidden_units:]
        sig = jax.nn.sigmoid(gate_pre)
        act = gate_pre * sig
        hidden = (act * up_pre).astype(bf16)
        out = lax.dot_general(hidden, weight_out, (((1,), (1,)), ((), ())), preferred_element_type=f32)
        out = to_rows((gate_slot[:, None] * out).astype(bf16))
        gate_grad = (hidden_grad * up_pre * (sig * (1.0 + gate_pre * (1.0 - sig)))).astype(bf16)
        up_grad = (hidden_grad * act).astype(bf16)
        pair_grad = jnp.concatenate([gate_grad, up_grad], axis=1)
        back = lax.dot_general(pair_grad, weight_in, (((1,), (1,)), ((), ())), preferred_element_type=f32)
        score = jnp.sum(hidden.astype(f32) * hidden_grad, axis=1) / jnp.where(gate_slot > 0, gate_slot, 1.0)
        score = jnp.sum(jnp.where(pick, score.reshape(blocks, -1, 1), 0.0), axis=1).reshape(-1, 1)
        score_hi = score.astype(bf16)
        score_lo = (score - score_hi.astype(f32)).astype(bf16)
        lane = jnp.arange(128)[None, :]
        score_cols = jnp.where(lane == expert, score_hi, 0) + jnp.where(lane == expert + groups, score_lo, 0)
        return hidden, pair_grad, out, jnp.concatenate([to_rows(back.astype(bf16)), score_cols.astype(bf16)], axis=1)

    pick_n, gate_n, x_n, g_n, pre_n, hg_n = first_half(tok_near, cot_near)
    pick_f, gate_f, x_f, g_f, pre_f, hg_f = first_half(tok_far, cot_far)

    def pair_sum(part):
        return part + swap_pair(part.astype(bf16)).astype(f32)

    hidden_n, pair_n, out_n, back_n = second_half(pick_n, gate_n, pair_sum(pre_n), pair_sum(hg_n))
    hidden_f, pair_f, out_f, back_f = second_half(pick_f, gate_f, pair_sum(pre_f), pair_sum(hg_f))

    mixed = rows_home(scatter_sum(out_n, out_f))
    back_sum = scatter_sum(back_n, back_f)
    grad_tokens = rows_home(back_sum[:, :half])

    def outer(left_n, right_n, left_f, right_f):
        left, right = jnp.concatenate([left_n, left_f]), jnp.concatenate([right_n, right_f])
        return lax.dot_general(left, right, (((0,), (0,)), ((), ())), preferred_element_type=f32).astype(bf16)[None]

    grad_gate_up = outer(x_n, pair_n, x_f, pair_f)
    grad_down = outer(g_n, hidden_n, g_f, hidden_f)

    scores = back_sum[:, half:].astype(bf16).reshape(2, 2, tok_dev, -1)
    scores = lax.dynamic_index_in_dim(scores, replica, 1, keepdims=False)
    scores = scores[0].astype(f32) + swap_cores(scores[1]).astype(f32)
    scores = scores[:, :groups] + scores[:, groups : 2 * groups]
    named = route_ids[:, :, None] == jnp.arange(groups, dtype=jnp.int32)[None, None, :]
    grad_gates = jnp.sum(jnp.where(named, scores[:, None, :], 0.0), axis=2)
    return (mixed, grad_tokens, grad_gates, grad_gate_up, grad_down)


def slot_capacity(tok_dev, top_count, experts):
    assignments = tok_dev * top_count
    return min(tok_dev, max(2, assignments // experts + max(1, assignments // (3 * experts))))


def body(tokens, route_ids, gates, cotangent, w_gate_up, w_down):
    groups, replicas = lax.axis_size("expert"), lax.axis_size("dp")
    gathered = 2 * groups * tokens.shape[0] * replicas * w_gate_up.shape[1] * 2
    small = gathered <= 8 * 1024 * 1024 and 3 * groups <= 128 and groups % 8 == 0
    if replicas == 2 and w_gate_up.shape[0] == 1 and small:
        return body_by_width(tokens, route_ids, gates, cotangent, w_gate_up, w_down)
    return body_by_slots(tokens, route_ids, gates, cotangent, w_gate_up, w_down)


def solution(mesh):
    placed = (
        P(("expert", "dp"), None),
        P(("expert", "dp"), None),
        P(("expert", "dp"), None),
        P(("expert", "dp"), None),
        P("expert", "dp", None),
        P("expert", "dp", None),
    )
    return jax.shard_map(
        body,
        mesh=mesh,
        in_specs=placed,
        out_specs=(
            P(("expert", "dp"), None),
            P(("expert", "dp"), None),
            P(("expert", "dp"), None),
            P("expert", "dp", None),
            P("expert", "dp", None),
        ),
        check_vma=False,
    )
```

```python
import jax
import jax.numpy as jnp
from jax import lax
from jax.experimental import pallas as pl
from jax.experimental.pallas import tpu as pltpu
from jax.sharding import PartitionSpec as P


def expert_forward(x_rows, weight_in, weight_out, hidden_units):
    pre_act = jnp.dot(x_rows, weight_in, preferred_element_type=jnp.float32)
    gate_pre = pre_act[:, :hidden_units]
    up_pre = pre_act[:, hidden_units:]
    sigmoid_gate = jax.nn.sigmoid(gate_pre)
    activation = gate_pre * sigmoid_gate
    hidden = (activation * up_pre).astype(jnp.bfloat16)
    expert_out = lax.dot_general(
        hidden, weight_out, (((1,), (1,)), ((), ())), preferred_element_type=jnp.float32
    ).astype(jnp.bfloat16)
    return (gate_pre, up_pre, sigmoid_gate, activation, hidden, expert_out)


def expert_backward(saved, grad_rows, weight_in, weight_out):
    gate_pre, up_pre, sigmoid_gate, activation, hidden, expert_out = saved
    hidden_grad = jnp.dot(grad_rows, weight_out, preferred_element_type=jnp.float32)
    gate_grad = (
        hidden_grad * up_pre * (sigmoid_gate * (1.0 + gate_pre * (1.0 - sigmoid_gate)))
    ).astype(jnp.bfloat16)
    up_grad = (hidden_grad * activation).astype(jnp.bfloat16)
    pair_grad = jnp.concatenate([gate_grad, up_grad], axis=1)
    input_grad = lax.dot_general(
        pair_grad, weight_in, (((1,), (1,)), ((), ())), preferred_element_type=jnp.float32
    ).astype(jnp.bfloat16)
    return (pair_grad, input_grad)


def outer_blocks(left, right, pieces):
    span = left.shape[1] // pieces
    results = []
    for piece in range(pieces):
        product = lax.dot_general(
            left[:, piece * span : (piece + 1) * span],
            right,
            (((0,), (0,)), ((), ())),
            preferred_element_type=jnp.float32,
        )
        results.append(product.astype(jnp.bfloat16))
    return jnp.stack(results, axis=0)


def replica_total(received):
    return jnp.sum(received.astype(jnp.float32), axis=0).astype(jnp.bfloat16)


def body_by_slots(tokens, route_ids, gates, cotangent, w_gate_up, w_down):
    tok_dev, model_width = tokens.shape
    top_count = route_ids.shape[1]
    groups = lax.axis_size("expert")
    replicas = lax.axis_size("dp")
    local_experts = w_gate_up.shape[0]
    hidden_units = w_down.shape[2]
    experts = groups * local_experts
    assignments = tok_dev * top_count
    capacity = min(tok_dev, max(2, assignments // experts + max(1, assignments // (3 * experts))))
    flat_ids = route_ids.reshape(assignments)
    onehot = (flat_ids[:, None] == jnp.arange(experts, dtype=jnp.int32)[None, :]).astype(jnp.int32)
    earlier = jnp.sum(
        (jnp.cumsum(onehot, axis=0, dtype=jnp.int32) - onehot) * onehot, axis=1, dtype=jnp.int32
    )
    position = flat_ids * capacity + earlier
    source = (
        jnp.full((experts * capacity,), assignments, jnp.int32)
        .at[position]
        .set(jnp.arange(assignments, dtype=jnp.int32))
    )
    token_row = source // top_count
    tok_pad = jnp.concatenate([tokens, jnp.zeros((1, model_width), jnp.bfloat16)], axis=0)
    cot_pad = jnp.concatenate([cotangent, jnp.zeros((1, model_width), jnp.bfloat16)], axis=0)
    gate_pad = jnp.concatenate([gates.reshape(assignments), jnp.zeros((1,), jnp.float32)], axis=0)
    send_rows = tok_pad[token_row].reshape(experts, capacity, model_width)
    send_grads = (gate_pad[source][:, None] * cot_pad[token_row].astype(jnp.float32)).astype(
        jnp.bfloat16
    )
    send_grads = send_grads.reshape(experts, capacity, model_width)
    weights_in, weights_out = (
        lax.all_gather(w_gate_up, "dp", axis=1, tiled=True),
        lax.all_gather(w_down, "dp", axis=1, tiled=True),
    )
    rows_in, grads_in = (
        lax.all_to_all(send_rows, "expert", split_axis=0, concat_axis=1, tiled=True),
        lax.all_to_all(send_grads, "expert", split_axis=0, concat_axis=1, tiled=True),
    )
    local = 0
    forward_parts = expert_forward(
        rows_in[local], weights_in[local], weights_out[local], hidden_units
    )
    saved_all = [forward_parts]
    out_list = [forward_parts[5]]
    down_list = [outer_blocks(grads_in[local], forward_parts[4], replicas)]
    expert_outs = jnp.stack(out_list, axis=0)
    down_stack = jnp.stack(down_list, axis=1)
    outs_back = lax.all_to_all(expert_outs, "expert", split_axis=1, concat_axis=0, tiled=True)
    local = 0
    pair_grad, input_grad = expert_backward(
        saved_all[local], grads_in[local], weights_in[local], weights_out[local]
    )
    input_list = [input_grad]
    gate_up_list = [outer_blocks(rows_in[local], pair_grad, replicas)]
    input_grads = jnp.stack(input_list, axis=0)
    gate_up_stack = jnp.stack(gate_up_list, axis=1)
    grads_back = lax.all_to_all(input_grads, "expert", split_axis=1, concat_axis=0, tiled=True)
    gate_up_received, down_received = (
        lax.all_to_all(gate_up_stack, "dp", split_axis=0, concat_axis=0, tiled=True),
        lax.all_to_all(down_stack, "dp", split_axis=0, concat_axis=0, tiled=True),
    )
    grad_gate_up = replica_total(gate_up_received)
    grad_down = replica_total(down_received)
    out_rows = outs_back.reshape(experts * capacity, model_width)[position].reshape(
        tok_dev, top_count, model_width
    )
    mixed = jnp.sum(gates[:, :, None] * out_rows.astype(jnp.float32), axis=1).astype(jnp.bfloat16)
    grad_gates = jnp.einsum("td,tkd->tk", cotangent, out_rows, preferred_element_type=jnp.float32)
    back_rows = grads_back.reshape(experts * capacity, model_width)[position].reshape(
        tok_dev, top_count, model_width
    )
    grad_tokens = jnp.sum(back_rows.astype(jnp.float32), axis=1).astype(jnp.bfloat16)
    return (mixed, grad_tokens, grad_gates, grad_gate_up, grad_down)


F32, BF16 = jnp.float32, jnp.bfloat16
LANES = 128


def run(kernel, outs, args, flops, scalars=0):
    moved = sum(x.size * x.dtype.itemsize for x in (*args, *outs))
    spaces = [pltpu.SMEM] * scalars + [pltpu.VMEM] * (len(args) - scalars)
    return pl.pallas_call(
        kernel,
        out_shape=outs,
        in_specs=[pl.BlockSpec(memory_space=space) for space in spaces],
        out_specs=[pl.BlockSpec(memory_space=pltpu.VMEM) for _ in outs],
        compiler_params=pltpu.CompilerParams(vmem_limit_bytes=28 * 1024 * 1024),
        cost_estimate=pl.CostEstimate(flops=flops, bytes_accessed=moved, transcendentals=0),
    )(*args)


def dot_nn(left, right):
    return jnp.dot(left, right, preferred_element_type=F32)


def dot_nt(left, right):
    return lax.dot_general(left, right, (((1,), (1,)), ((), ())), preferred_element_type=F32)


def own_column(expert, groups):
    lane = lax.broadcasted_iota(jnp.int32, (1, LANES), 1)
    hit = (lane == expert) | (lane == expert + groups) | (lane == expert + 2 * groups)
    return jnp.where(hit, 1.0, 0.0)


def prepare(tokens, route_ids, gates, cotangent, replica, groups):
    rows, width = tokens.shape
    half = width // 2

    def kernel(replica_ref, tok_ref, id_ref, gate_ref, cot_ref, tok_keep, tok_send, cot_keep, cot_send):
        low = replica_ref[0] == 0
        lane = lax.broadcasted_iota(jnp.int32, (rows, LANES), 1)
        term = lax.div(lane, groups)
        named = lane - term * groups
        dense = jnp.zeros((rows, LANES), F32)
        for k in range(id_ref.shape[1]):
            dense = dense + jnp.where(id_ref[:, k : k + 1] == named, gate_ref[:, k : k + 1], 0.0)
        first = dense.astype(BF16).astype(F32)
        second = (dense - first).astype(BF16).astype(F32)
        third = dense - first - second
        meta = jnp.where(term == 0, first, jnp.where(term == 1, second, jnp.where(term == 2, third, 0.0))).astype(BF16)
        for ref, keep, send in ((tok_ref, tok_keep, tok_send), (cot_ref, cot_keep, cot_send)):
            left, right = ref[:, :half], ref[:, half:]
            keep[:, :half] = jnp.where(low, left, right)
            send[:, :half] = jnp.where(low, right, left)
        tok_keep[:, half:] = meta
        tok_send[:, half:] = meta

    wide = jax.ShapeDtypeStruct((rows, half + LANES), BF16)
    slim = jax.ShapeDtypeStruct((rows, half), BF16)
    return run(kernel, [wide, wide, slim, slim], [replica, tokens, route_ids, gates, cotangent], 1 << 20, 1)


def slot_counts(pieces, tok_dev, capacity):
    return [piece.shape[0] // tok_dev * capacity for piece in pieces]


def gate_up_half(pieces, weight_in, expert, groups, tok_dev, capacity):
    counts = slot_counts(pieces, tok_dev, capacity)
    total, width = sum(counts), pieces[0].shape[1]
    half, columns = weight_in.shape
    number = len(pieces)

    def kernel(expert_ref, *refs):
        toks, refs = refs[:number], refs[number:]
        w_ref, x_ref, gate_ref, own_ref, send_ref = refs[:5]
        picks, places = refs[5 : 5 + number], refs[5 + number :]
        column = own_column(expert_ref[0], groups)
        column_rows = jnp.broadcast_to(column, (8, LANES)).astype(BF16)
        start = 0
        for piece in range(number):
            rows, count = toks[piece].shape[0], counts[piece]
            meta = toks[piece][:, half:]
            gate_row = dot_nt(column_rows, meta)
            gate_col = jnp.sum(meta.astype(F32) * column, axis=1, keepdims=True)
            down = lax.broadcasted_iota(jnp.int32, (rows, rows), 0)
            along = lax.broadcasted_iota(jnp.int32, (rows, rows), 1)
            first_down, first_along = jnp.zeros_like(down), jnp.zeros_like(along)
            for device in range(1, rows // tok_dev):
                first_down += jnp.where(down >= device * tok_dev, tok_dev, 0)
                first_along += jnp.where(along >= device * tok_dev, tok_dev, 0)
            lower = ((along < down) & (along >= first_down)).astype(F32).astype(BF16)
            upper = ((down < along) & (down >= first_along)).astype(F32).astype(BF16)
            base_col = (first_down[:, :1] // tok_dev * capacity).astype(F32)
            base_row = (first_along[:1, :] // tok_dev * capacity).astype(F32)
            on_row = jnp.where(gate_row > 0.0, 1.0, 0.0)
            on_col = jnp.where(gate_col > 0.0, 1.0, 0.0)
            rank_row = dot_nn(on_row.astype(BF16), upper)
            rank_col = dot_nn(lower, jnp.broadcast_to(on_col, (rows, LANES)).astype(BF16))
            place_row = jnp.where(on_row > 0.0, rank_row + base_row, -1.0)[:1, :]
            place_col = jnp.where(on_col > 0.0, rank_col[:, :1] + base_col, -1.0)
            slot_down = lax.broadcasted_iota(jnp.int32, (count, rows), 0).astype(F32)
            slot_along = lax.broadcasted_iota(jnp.int32, (rows, count), 1).astype(F32)
            pick = jnp.where(place_row == slot_down, 1.0, 0.0).astype(BF16)
            picks[piece][...] = pick
            places[piece][...] = jnp.where(place_col == slot_along, 1.0, 0.0).astype(BF16)
            picked = dot_nn(pick, toks[piece][...])
            x_ref[start : start + count, :] = picked[:, :half].astype(BF16)
            gate = jnp.sum(picked[:, half:] * column, axis=1, keepdims=True)
            gate_ref[start : start + count, :] = jnp.broadcast_to(gate, (count, LANES))
            start += count
        part = dot_nn(x_ref[...], w_ref[...])
        own_ref[...] = part
        send_ref[...] = part.astype(BF16)

    shape = jax.ShapeDtypeStruct
    outs = [shape((total, half), BF16), shape((total, LANES), F32), shape((total, columns), F32), shape((total, columns), BF16)]
    outs += [shape((count, piece.shape[0]), BF16) for piece, count in zip(pieces, counts)]
    outs += [shape((piece.shape[0], count), BF16) for piece, count in zip(pieces, counts)]
    flops = 2 * total * half * columns + sum(2 * c * p.shape[0] * width for p, c in zip(pieces, counts))
    got = run(kernel, outs, [expert, *pieces, weight_in], flops, 1)
    return (*got[:4], got[4 : 4 + number], got[4 + number :])


def down_half(pieces, picks, gate, weight_out):
    counts = [pick.shape[0] for pick in picks]
    total, number = sum(counts), len(pieces)
    half, columns = weight_out.shape

    def kernel(*refs):
        cots, picked, refs = refs[:number], refs[number : 2 * number], refs[2 * number :]
        gate_ref, w_ref, rows_ref, own_ref, send_ref = refs
        start = 0
        for piece in range(number):
            count = counts[piece]
            rows = dot_nn(picked[piece][...], cots[piece][...])
            rows_ref[start : start + count, :] = (gate_ref[start : start + count, :1] * rows).astype(BF16)
            start += count
        part = dot_nn(rows_ref[...], w_ref[...])
        own_ref[...] = part
        send_ref[...] = part.astype(BF16)

    shape = jax.ShapeDtypeStruct
    outs = [shape((total, half), BF16), shape((total, columns), F32), shape((total, columns), BF16)]
    flops = 2 * total * half * columns + sum(2 * p.size * half for p in picks)
    return run(kernel, outs, [*pieces, *picks, gate, weight_out], flops)


def forward_rows(own, came, gate, places, weight_out):
    total, columns = own.shape
    hidden_units, half, number = columns // 2, weight_out.shape[0], len(places)

    def kernel(own_ref, came_ref, gate_ref, w_ref, *refs):
        put, hidden_ref, outs = refs[:number], refs[number], refs[number + 1 :]
        pre = own_ref[...] + came_ref[...].astype(F32)
        gate_pre, up_pre = pre[:, :hidden_units], pre[:, hidden_units:]
        hidden = (gate_pre * jax.nn.sigmoid(gate_pre) * up_pre).astype(BF16)
        hidden_ref[...] = hidden
        rows = (gate_ref[:, :1] * dot_nt(hidden, w_ref[...])).astype(BF16)
        start = 0
        for piece in range(number):
            count = put[piece].shape[1]
            outs[piece][...] = dot_nn(put[piece][...], rows[start : start + count, :]).astype(BF16)
            start += count

    shape = jax.ShapeDtypeStruct
    outs = [shape((total, hidden_units), BF16)] + [shape((place.shape[0], half), BF16) for place in places]
    flops = 2 * total * half * hidden_units + sum(2 * p.size * half for p in places)
    got = run(kernel, outs, [own, came, gate, weight_out, *places], flops)
    return got[0], got[1:]


def backward_rows(pre_own, pre_came, own, came, gate, places, weight_in, expert, groups):
    total, columns = pre_own.shape
    hidden_units, half, number = columns // 2, weight_in.shape[0], len(places)

    def kernel(expert_ref, pre_ref, pre_came_ref, own_ref, came_ref, gate_ref, w_ref, *refs):
        put, pair_ref, outs = refs[:number], refs[number], refs[number + 1 :]
        pre = pre_ref[...] + pre_came_ref[...].astype(F32)
        hidden_grad = own_ref[...] + came_ref[...].astype(F32)
        gate_pre, up_pre = pre[:, :hidden_units], pre[:, hidden_units:]
        sig = jax.nn.sigmoid(gate_pre)
        act = gate_pre * sig
        gate = gate_ref[...]
        score = jnp.sum((act * up_pre).astype(BF16).astype(F32) * hidden_grad, axis=1, keepdims=True)
        score = score / jnp.where(gate > 0.0, gate, 1.0)
        first = score.astype(BF16).astype(F32)
        lane = lax.broadcasted_iota(jnp.int32, (total, LANES), 1)
        expert = expert_ref[0]
        score = jnp.where(lane == expert, first, jnp.where(lane == expert + groups, score - first, 0.0)).astype(BF16)
        pair_ref[:, :hidden_units] = (hidden_grad * up_pre * (sig * (1.0 + gate_pre * (1.0 - sig)))).astype(BF16)
        pair_ref[:, hidden_units:] = (hidden_grad * act).astype(BF16)
        rows = dot_nt(pair_ref[...], w_ref[...]).astype(BF16)
        start = 0
        for piece in range(number):
            count = put[piece].shape[1]
            place = put[piece][...]
            outs[piece][:, :half] = dot_nn(place, rows[start : start + count, :]).astype(BF16)
            outs[piece][:, half:] = dot_nn(place, score[start : start + count, :]).astype(BF16)
            start += count

    shape = jax.ShapeDtypeStruct
    outs = [shape((total, columns), BF16)] + [shape((place.shape[0], half + LANES), BF16) for place in places]
    flops = 2 * total * half * columns + sum(2 * p.size * half for p in places)
    got = run(kernel, outs, [expert, pre_own, pre_came, own, came, gate, weight_in, *places], flops, 1)
    return got[0], got[1:]


def ring_pairs(groups):
    chips = groups // 2
    levels = chips // 2
    order = [2 * z for z in range(levels)] + [2 * z + 1 for z in reversed(range(levels))]
    forward = []
    for place in range(chips):
        forward.append((2 * order[place], 2 * order[(place + 1) % chips]))
        forward.append((2 * order[(place + 1) % chips] + 1, 2 * order[place] + 1))
    backward = [(to, source) for source, to in forward]
    cores = [(index, index ^ 1) for index in range(groups)]
    return forward, backward, cores


def swap_pair(value):
    return lax.ppermute(value, "dp", [(0, 1), (1, 0)])


def swap_both(value):
    groups = lax.axis_size("expert")
    pairs = [(2 * e + r, 2 * (e ^ 1) + 1 - r) for e in range(groups) for r in range(2)]
    return lax.ppermute(value, ("expert", "dp"), pairs)


def by_replica(own, other, replica):
    return jnp.where(replica == 0, jnp.stack([own, other]), jnp.stack([other, own]))


def body_by_width(tokens, route_ids, gates, cotangent, w_gate_up, w_down):
    tok_dev, model_width = tokens.shape
    top_count = route_ids.shape[1]
    groups = lax.axis_size("expert")
    replica = lax.axis_index("dp")
    expert = lax.axis_index("expert").astype(jnp.int32).reshape(1)
    half = w_gate_up.shape[1]
    capacity = slot_capacity(tok_dev, top_count, groups)
    steps = groups // 4
    near_steps = steps // 2
    weight_in, weight_out = w_gate_up[0], w_down[0]
    forward, backward, cores = ring_pairs(groups)
    unit = 2 * tok_dev
    chip = 2 * unit

    def swap_cores(value):
        return lax.ppermute(value, "expert", cores)

    def chip_rows(keep, send):
        across, diagonal, beside = swap_pair(send), swap_both(send), swap_cores(keep)
        return jnp.concatenate(
            [by_replica(keep, across, replica), by_replica(beside, diagonal, replica)], axis=0
        ).reshape(chip, -1)

    def gather_rows(block):
        own, mine = block, []
        for step in range(steps):
            block = lax.ppermute(block if step < steps - 1 else block[:unit], "expert", forward)
            mine.append(block)
        near = jnp.concatenate(mine[:near_steps], axis=0)
        far = jnp.concatenate(mine[near_steps:], axis=0)
        return [own, near, swap_cores(near)], [far, swap_cores(far)]

    def scatter_sum(near, far):
        own, near_mine, near_other = near
        far_mine, far_other = far
        far_other, near_other = swap_cores(far_other), swap_cores(near_other)
        terms = [own.astype(F32)]
        for step in range(steps):
            mine, other = (near_mine, near_other) if step < near_steps else (far_mine, far_other)
            start = (step if step < near_steps else step - near_steps) * chip
            terms.append(mine[start : start + chip].astype(F32) + other[start : start + chip].astype(F32))
        total = terms.pop()
        while terms:
            came = lax.ppermute(total.astype(BF16), "expert", backward).astype(F32)
            base = terms.pop()
            if came.shape[0] < chip:
                total = jnp.concatenate([base[:unit] + came, base[unit:]], axis=0)
            else:
                total = base + came
        return total

    def rows_home(value):
        value = value.reshape(2, 2, tok_dev, half).astype(BF16)
        mine = lax.dynamic_index_in_dim(value, replica, 1, keepdims=False)
        theirs = lax.dynamic_index_in_dim(value, 1 - replica, 1, keepdims=False)
        kept = mine[0].astype(F32) + swap_cores(mine[1]).astype(F32)
        other = swap_pair(theirs[0]).astype(F32) + swap_both(theirs[1]).astype(F32)
        both = by_replica(kept, other, replica)
        return jnp.concatenate([both[0], both[1]], axis=1).astype(BF16)

    tok_keep, tok_send, cot_keep, cot_send = prepare(
        tokens, route_ids, gates, cotangent, replica.astype(jnp.int32).reshape(1), groups
    )
    tok_chunks = gather_rows(chip_rows(tok_keep, tok_send))
    cot_chunks = gather_rows(chip_rows(cot_keep, cot_send))

    saved, outs, backs = [], [], []
    for toks, cots in zip(tok_chunks, cot_chunks):
        x_rows, gate, pre_own, pre_send, picks, places = gate_up_half(
            toks, weight_in, expert, groups, tok_dev, capacity
        )
        grad_rows, hg_own, hg_send = down_half(cots, picks, gate, weight_out)
        saved.append((x_rows, gate, pre_own, swap_pair(pre_send), places, grad_rows, hg_own, swap_pair(hg_send)))
    grads = []
    for x_rows, gate, pre_own, pre_came, places, grad_rows, hg_own, hg_came in saved:
        hidden, out = forward_rows(pre_own, pre_came, gate, places, weight_out)
        pair_grad, back = backward_rows(
            pre_own, pre_came, hg_own, hg_came, gate, places, weight_in, expert, groups
        )
        outs.append(out)
        backs.append(back)
        grads.append((x_rows, pair_grad, grad_rows, hidden))

    mixed = rows_home(scatter_sum(*outs))
    back_sum = scatter_sum(*backs)
    grad_tokens = rows_home(back_sum[:, :half])

    def outer(left, right):
        left = jnp.concatenate([chunk[left] for chunk in grads])
        right = jnp.concatenate([chunk[right] for chunk in grads])
        return lax.dot_general(left, right, (((0,), (0,)), ((), ())), preferred_element_type=F32).astype(BF16)[None]

    grad_gate_up = outer(0, 1)
    grad_down = outer(2, 3)

    scores = back_sum[:, half:].astype(BF16).reshape(2, 2, tok_dev, -1)
    scores = lax.dynamic_index_in_dim(scores, replica, 1, keepdims=False)
    scores = scores[0].astype(F32) + swap_cores(scores[1]).astype(F32)
    scores = scores[:, :groups] + scores[:, groups : 2 * groups]
    named = route_ids[:, :, None] == jnp.arange(groups, dtype=jnp.int32)[None, None, :]
    grad_gates = jnp.sum(jnp.where(named, scores[:, None, :], 0.0), axis=2)
    return (mixed, grad_tokens, grad_gates, grad_gate_up, grad_down)


def slot_capacity(tok_dev, top_count, experts):
    assignments = tok_dev * top_count
    return min(tok_dev, max(2, assignments // experts + max(1, assignments // (3 * experts))))


def body(tokens, route_ids, gates, cotangent, w_gate_up, w_down):
    groups, replicas = lax.axis_size("expert"), lax.axis_size("dp")
    gathered = 2 * groups * tokens.shape[0] * replicas * w_gate_up.shape[1] * 2
    small = gathered <= 8 * 1024 * 1024 and 3 * groups <= 128 and groups % 8 == 0
    if replicas == 2 and w_gate_up.shape[0] == 1 and small:
        return body_by_width(tokens, route_ids, gates, cotangent, w_gate_up, w_down)
    return body_by_slots(tokens, route_ids, gates, cotangent, w_gate_up, w_down)


def solution(mesh):
    placed = (
        P(("expert", "dp"), None),
        P(("expert", "dp"), None),
        P(("expert", "dp"), None),
        P(("expert", "dp"), None),
        P("expert", "dp", None),
        P("expert", "dp", None),
    )
    return jax.shard_map(
        body,
        mesh=mesh,
        in_specs=placed,
        out_specs=(
            P(("expert", "dp"), None),
            P(("expert", "dp"), None),
            P(("expert", "dp"), None),
            P("expert", "dp", None),
            P("expert", "dp", None),
        ),
        check_vma=False,
    )
```

```python
import jax
import jax.numpy as jnp
from jax import lax
from jax.experimental import pallas as pl
from jax.experimental.pallas import tpu as pltpu
from jax.sharding import PartitionSpec as P


def expert_forward(x_rows, weight_in, weight_out, hidden_units):
    pre_act = jnp.dot(x_rows, weight_in, preferred_element_type=jnp.float32)
    gate_pre = pre_act[:, :hidden_units]
    up_pre = pre_act[:, hidden_units:]
    sigmoid_gate = jax.nn.sigmoid(gate_pre)
    activation = gate_pre * sigmoid_gate
    hidden = (activation * up_pre).astype(jnp.bfloat16)
    expert_out = lax.dot_general(
        hidden, weight_out, (((1,), (1,)), ((), ())), preferred_element_type=jnp.float32
    ).astype(jnp.bfloat16)
    return (gate_pre, up_pre, sigmoid_gate, activation, hidden, expert_out)


def expert_backward(saved, grad_rows, weight_in, weight_out):
    gate_pre, up_pre, sigmoid_gate, activation, hidden, expert_out = saved
    hidden_grad = jnp.dot(grad_rows, weight_out, preferred_element_type=jnp.float32)
    gate_grad = (
        hidden_grad * up_pre * (sigmoid_gate * (1.0 + gate_pre * (1.0 - sigmoid_gate)))
    ).astype(jnp.bfloat16)
    up_grad = (hidden_grad * activation).astype(jnp.bfloat16)
    pair_grad = jnp.concatenate([gate_grad, up_grad], axis=1)
    input_grad = lax.dot_general(
        pair_grad, weight_in, (((1,), (1,)), ((), ())), preferred_element_type=jnp.float32
    ).astype(jnp.bfloat16)
    return (pair_grad, input_grad)


def outer_blocks(left, right, pieces):
    span = left.shape[1] // pieces
    results = []
    for piece in range(pieces):
        product = lax.dot_general(
            left[:, piece * span : (piece + 1) * span],
            right,
            (((0,), (0,)), ((), ())),
            preferred_element_type=jnp.float32,
        )
        results.append(product.astype(jnp.bfloat16))
    return jnp.stack(results, axis=0)


def replica_total(received):
    return jnp.sum(received.astype(jnp.float32), axis=0).astype(jnp.bfloat16)


def body_by_slots(tokens, route_ids, gates, cotangent, w_gate_up, w_down):
    tok_dev, model_width = tokens.shape
    top_count = route_ids.shape[1]
    groups = lax.axis_size("expert")
    replicas = lax.axis_size("dp")
    local_experts = w_gate_up.shape[0]
    hidden_units = w_down.shape[2]
    experts = groups * local_experts
    assignments = tok_dev * top_count
    capacity = min(tok_dev, max(2, assignments // experts + max(1, assignments // (3 * experts))))
    flat_ids = route_ids.reshape(assignments)
    onehot = (flat_ids[:, None] == jnp.arange(experts, dtype=jnp.int32)[None, :]).astype(jnp.int32)
    earlier = jnp.sum(
        (jnp.cumsum(onehot, axis=0, dtype=jnp.int32) - onehot) * onehot, axis=1, dtype=jnp.int32
    )
    position = flat_ids * capacity + earlier
    source = (
        jnp.full((experts * capacity,), assignments, jnp.int32)
        .at[position]
        .set(jnp.arange(assignments, dtype=jnp.int32))
    )
    token_row = source // top_count
    tok_pad = jnp.concatenate([tokens, jnp.zeros((1, model_width), jnp.bfloat16)], axis=0)
    cot_pad = jnp.concatenate([cotangent, jnp.zeros((1, model_width), jnp.bfloat16)], axis=0)
    gate_pad = jnp.concatenate([gates.reshape(assignments), jnp.zeros((1,), jnp.float32)], axis=0)
    send_rows = tok_pad[token_row].reshape(experts, capacity, model_width)
    send_grads = (gate_pad[source][:, None] * cot_pad[token_row].astype(jnp.float32)).astype(
        jnp.bfloat16
    )
    send_grads = send_grads.reshape(experts, capacity, model_width)
    weights_in, weights_out = (
        lax.all_gather(w_gate_up, "dp", axis=1, tiled=True),
        lax.all_gather(w_down, "dp", axis=1, tiled=True),
    )
    rows_in, grads_in = (
        lax.all_to_all(send_rows, "expert", split_axis=0, concat_axis=1, tiled=True),
        lax.all_to_all(send_grads, "expert", split_axis=0, concat_axis=1, tiled=True),
    )
    local = 0
    forward_parts = expert_forward(
        rows_in[local], weights_in[local], weights_out[local], hidden_units
    )
    saved_all = [forward_parts]
    out_list = [forward_parts[5]]
    down_list = [outer_blocks(grads_in[local], forward_parts[4], replicas)]
    expert_outs = jnp.stack(out_list, axis=0)
    down_stack = jnp.stack(down_list, axis=1)
    outs_back = lax.all_to_all(expert_outs, "expert", split_axis=1, concat_axis=0, tiled=True)
    local = 0
    pair_grad, input_grad = expert_backward(
        saved_all[local], grads_in[local], weights_in[local], weights_out[local]
    )
    input_list = [input_grad]
    gate_up_list = [outer_blocks(rows_in[local], pair_grad, replicas)]
    input_grads = jnp.stack(input_list, axis=0)
    gate_up_stack = jnp.stack(gate_up_list, axis=1)
    grads_back = lax.all_to_all(input_grads, "expert", split_axis=1, concat_axis=0, tiled=True)
    gate_up_received, down_received = (
        lax.all_to_all(gate_up_stack, "dp", split_axis=0, concat_axis=0, tiled=True),
        lax.all_to_all(down_stack, "dp", split_axis=0, concat_axis=0, tiled=True),
    )
    grad_gate_up = replica_total(gate_up_received)
    grad_down = replica_total(down_received)
    out_rows = outs_back.reshape(experts * capacity, model_width)[position].reshape(
        tok_dev, top_count, model_width
    )
    mixed = jnp.sum(gates[:, :, None] * out_rows.astype(jnp.float32), axis=1).astype(jnp.bfloat16)
    grad_gates = jnp.einsum("td,tkd->tk", cotangent, out_rows, preferred_element_type=jnp.float32)
    back_rows = grads_back.reshape(experts * capacity, model_width)[position].reshape(
        tok_dev, top_count, model_width
    )
    grad_tokens = jnp.sum(back_rows.astype(jnp.float32), axis=1).astype(jnp.bfloat16)
    return (mixed, grad_tokens, grad_gates, grad_gate_up, grad_down)


F32, BF16 = jnp.float32, jnp.bfloat16
LANES = 128
FREE = pl.CostEstimate(flops=0, bytes_accessed=0, transcendentals=0)


def run(kernel, outs, args, scalars=0):
    spaces = [pltpu.SMEM] * scalars + [pltpu.VMEM] * (len(args) - scalars)
    return pl.pallas_call(
        kernel,
        out_shape=outs,
        in_specs=[pl.BlockSpec(memory_space=space) for space in spaces],
        out_specs=[pl.BlockSpec(memory_space=pltpu.VMEM) for _ in outs],
        compiler_params=pltpu.CompilerParams(vmem_limit_bytes=16 * 1024 * 1024),
        cost_estimate=FREE,
    )(*args)


def dot_nn(left, right):
    return jnp.dot(left, right, preferred_element_type=F32)


def dot_nt(left, right):
    return lax.dot_general(left, right, (((1,), (1,)), ((), ())), preferred_element_type=F32)


def own_column(expert, groups):
    lane = lax.broadcasted_iota(jnp.int32, (1, LANES), 1)
    hit = (lane == expert) | (lane == expert + groups) | (lane == expert + 2 * groups)
    return jnp.where(hit, 1.0, 0.0)


def prepare(tokens, route_ids, gates, cotangent, replica, groups):
    rows, width = tokens.shape
    half = width // 2

    def kernel(replica_ref, tok_ref, id_ref, gate_ref, cot_ref, keep_ref, send_ref):
        low = replica_ref[0] == 0
        lane = lax.broadcasted_iota(jnp.int32, (rows, LANES), 1)
        term = lax.div(lane, groups)
        named = lane - term * groups
        dense = jnp.zeros((rows, LANES), F32)
        for k in range(id_ref.shape[1]):
            dense = dense + jnp.where(id_ref[:, k : k + 1] == named, gate_ref[:, k : k + 1], 0.0)
        first = dense.astype(BF16).astype(F32)
        second = (dense - first).astype(BF16).astype(F32)
        third = dense - first - second
        meta = jnp.where(term == 0, first, jnp.where(term == 1, second, jnp.where(term == 2, third, 0.0))).astype(BF16)
        for ref, start in ((tok_ref, 0), (cot_ref, half + LANES)):
            left, right = ref[:, :half], ref[:, half:]
            keep_ref[:, start : start + half] = jnp.where(low, left, right)
            send_ref[:, start : start + half] = jnp.where(low, right, left)
        keep_ref[:, half : half + LANES] = meta
        send_ref[:, half : half + LANES] = meta

    out = jax.ShapeDtypeStruct((rows, width + LANES), BF16)
    return run(kernel, [out, out], [replica, tokens, route_ids, gates, cotangent], 1)


def partial_products(pieces, weight_in, weight_out, expert, groups, tok_dev, capacity):
    counts = [piece.shape[0] // tok_dev * capacity for piece in pieces]
    total, number = sum(counts), len(pieces)
    half, columns = weight_in.shape
    hidden_units = weight_out.shape[1]

    def kernel(expert_ref, *refs):
        rows_refs, refs = refs[:number], refs[number:]
        in_ref, out_ref, x_ref, grad_ref, gate_ref, own_ref, send_ref = refs[:7]
        places = refs[7:]
        column = own_column(expert_ref[0], groups)
        column_rows = jnp.broadcast_to(column, (8, LANES)).astype(BF16)
        start = 0
        for piece in range(number):
            rows, count = rows_refs[piece].shape[0], counts[piece]
            meta = rows_refs[piece][:, half : half + LANES]
            gate_row = dot_nt(column_rows, meta)
            gate_col = jnp.sum(meta.astype(F32) * column, axis=1, keepdims=True)
            down = lax.broadcasted_iota(jnp.int32, (rows, rows), 0)
            along = lax.broadcasted_iota(jnp.int32, (rows, rows), 1)
            first_down, first_along = jnp.zeros_like(down), jnp.zeros_like(along)
            base_down, base_along = jnp.zeros_like(down), jnp.zeros_like(along)
            for device in range(1, rows // tok_dev):
                first_down += jnp.where(down >= device * tok_dev, tok_dev, 0)
                first_along += jnp.where(along >= device * tok_dev, tok_dev, 0)
                base_down += jnp.where(down >= device * tok_dev, capacity, 0)
                base_along += jnp.where(along >= device * tok_dev, capacity, 0)
            lower = jnp.where((along < down) & (along >= first_down), 1.0, 0.0).astype(BF16)
            upper = jnp.where((down < along) & (down >= first_along), 1.0, 0.0).astype(BF16)
            on_row = jnp.where(gate_row > 0.0, 1.0, 0.0)
            on_col = jnp.where(gate_col > 0.0, 1.0, 0.0)
            rank_row = dot_nn(on_row.astype(BF16), upper)
            rank_col = dot_nn(lower, jnp.broadcast_to(on_col, (rows, LANES)).astype(BF16))
            place_row = jnp.where(on_row > 0.0, rank_row + base_along[:8].astype(F32), -1.0)[:1, :]
            place_col = jnp.where(on_col > 0.0, rank_col[:, :1] + base_down[:, :1].astype(F32), -1.0)
            slot_down = lax.broadcasted_iota(jnp.int32, (count, rows), 0).astype(F32)
            slot_along = lax.broadcasted_iota(jnp.int32, (rows, count), 1).astype(F32)
            pick = jnp.where(place_row == slot_down, 1.0, 0.0).astype(BF16)
            places[piece][...] = jnp.where(place_col == slot_along, 1.0, 0.0).astype(BF16)
            picked = dot_nn(pick, rows_refs[piece][...])
            x_ref[start : start + count, :] = picked[:, :half].astype(BF16)
            gate = jnp.sum(picked[:, half : half + LANES] * column, axis=1, keepdims=True)
            gate_ref[start : start + count, :] = jnp.broadcast_to(gate, (count, LANES))
            grad_ref[start : start + count, :] = (gate * picked[:, half + LANES :]).astype(BF16)
            start += count
        for left, right, at in ((x_ref, in_ref, 0), (grad_ref, out_ref, columns)):
            part = dot_nn(left[...], right[...])
            own_ref[:, at : at + part.shape[1]] = part
            send_ref[:, at : at + part.shape[1]] = part.astype(BF16)

    shape = jax.ShapeDtypeStruct
    outs = [shape((total, half), BF16), shape((total, half), BF16), shape((total, LANES), F32)]
    outs += [shape((total, columns + hidden_units), F32), shape((total, columns + hidden_units), BF16)]
    outs += [shape((piece.shape[0], count), BF16) for piece, count in zip(pieces, counts)]
    got = run(kernel, outs, [expert, *pieces, weight_in, weight_out], 1)
    return (*got[:5], got[5:])


def expert_rows(own, came, gate, places, weight_in, weight_out, expert, groups):
    total = own.shape[0]
    half, columns = weight_in.shape
    hidden_units, number = columns // 2, len(places)

    def kernel(expert_ref, own_ref, came_ref, gate_ref, in_ref, out_ref, *refs):
        put, hidden_ref, pair_ref, flag_ref, outs = refs[:number], *refs[number : number + 3], refs[number + 3 :]
        gate_pre = own_ref[:, :hidden_units] + came_ref[:, :hidden_units].astype(F32)
        up_pre = own_ref[:, hidden_units:columns] + came_ref[:, hidden_units:columns].astype(F32)
        hidden_grad = own_ref[:, columns:] + came_ref[:, columns:].astype(F32)
        sig = jax.nn.sigmoid(gate_pre)
        act = gate_pre * sig
        hidden = (act * up_pre).astype(BF16)
        hidden_ref[...] = hidden
        pair_ref[:, :hidden_units] = (hidden_grad * up_pre * (sig * (1.0 + gate_pre * (1.0 - sig)))).astype(BF16)
        pair_ref[:, hidden_units:] = (hidden_grad * act).astype(BF16)
        gate = gate_ref[...]
        flag_ref[...] = gate[:8]
        score = jnp.sum(hidden.astype(F32) * hidden_grad, axis=1, keepdims=True)
        score = score / jnp.where(gate > 0.0, gate, 1.0)
        first = score.astype(BF16).astype(F32)
        lane = lax.broadcasted_iota(jnp.int32, (total, LANES), 1)
        expert = expert_ref[0]
        score = jnp.where(lane == expert, first, jnp.where(lane == expert + groups, score - first, 0.0)).astype(BF16)
        forth = (gate[:, :1] * dot_nt(hidden, out_ref[...])).astype(BF16)
        back = dot_nt(pair_ref[...], in_ref[...]).astype(BF16)
        start = 0
        for piece in range(number):
            count = put[piece].shape[1]
            place = put[piece][...]
            for rows, at in ((forth, 0), (back, half), (score, 2 * half)):
                rows = rows[start : start + count, :]
                outs[piece][:, at : at + rows.shape[1]] = dot_nn(place, rows).astype(BF16)
            start += count

    shape = jax.ShapeDtypeStruct
    outs = [shape((total, hidden_units), BF16), shape((total, columns), BF16), shape((8, LANES), F32)]
    outs += [shape((place.shape[0], 2 * half + LANES), BF16) for place in places]
    got = run(kernel, outs, [expert, own, came, gate, weight_in, weight_out, *places], 1)
    return got[0], got[1], got[2], got[3:]


def ring_pairs(groups):
    chips = groups // 2
    levels = chips // 2
    order = [2 * z for z in range(levels)] + [2 * z + 1 for z in reversed(range(levels))]
    forward = []
    for place in range(chips):
        forward.append((2 * order[place], 2 * order[(place + 1) % chips]))
        forward.append((2 * order[(place + 1) % chips] + 1, 2 * order[place] + 1))
    backward = [(to, source) for source, to in forward]
    cores = [(index, index ^ 1) for index in range(groups)]
    return forward, backward, cores


def swap_pair(value):
    return lax.ppermute(value, "dp", [(0, 1), (1, 0)])


def swap_both(value):
    groups = lax.axis_size("expert")
    pairs = [(2 * e + r, 2 * (e ^ 1) + 1 - r) for e in range(groups) for r in range(2)]
    return lax.ppermute(value, ("expert", "dp"), pairs)


def by_replica(own, other, replica):
    return jnp.where(replica == 0, jnp.stack([own, other]), jnp.stack([other, own]))


def after(value, *anchors):
    anywhere = pl.BlockSpec(memory_space=pl.ANY)
    return pl.pallas_call(
        lambda *refs: None,
        out_shape=jax.ShapeDtypeStruct(value.shape, value.dtype),
        in_specs=[anywhere] * (1 + len(anchors)),
        out_specs=anywhere,
        input_output_aliases={0: 0},
        compiler_params=pltpu.CompilerParams(vmem_limit_bytes=1024 * 1024),
        cost_estimate=FREE,
    )(value, *anchors)


def body_by_width(tokens, route_ids, gates, cotangent, w_gate_up, w_down):
    tok_dev, model_width = tokens.shape
    top_count = route_ids.shape[1]
    groups = lax.axis_size("expert")
    replica = lax.axis_index("dp")
    expert = lax.axis_index("expert").astype(jnp.int32).reshape(1)
    half = w_gate_up.shape[1]
    capacity = slot_capacity(tok_dev, top_count, groups)
    steps = groups // 4
    weight_in, weight_out = w_gate_up[0], w_down[0]
    forward, backward, cores = ring_pairs(groups)
    unit = 2 * tok_dev
    chip = 2 * unit

    def swap_cores(value):
        return lax.ppermute(value, "expert", cores)

    def products(pieces):
        *kept, own, send, places = partial_products(
            pieces, weight_in, weight_out, expert, groups, tok_dev, capacity
        )
        return kept, own, send, places, swap_pair(send)

    keep, send = prepare(tokens, route_ids, gates, cotangent, replica.astype(jnp.int32).reshape(1), groups)
    across, diagonal, beside = swap_pair(send), swap_both(send), swap_cores(keep)
    block = jnp.concatenate(
        [by_replica(keep, across, replica), by_replica(beside, diagonal, replica)], axis=0
    ).reshape(chip, -1)

    chunks, pieces = [], [block]
    for step in range(steps):
        block = lax.ppermute(block if step < steps - 1 else block[:unit], "expert", forward)
        if chunks and step < steps - 1:
            block = after(block, chunks[-1][2])
        pieces += [block, swap_cores(block)]
        if step != steps - 2:
            chunks.append(products(pieces))
            pieces = []

    outs, grads = [], []
    for number, ((x_rows, grad_rows, gate), own, _, places, came) in enumerate(chunks):
        if number:
            came = after(came, flag)
        hidden, pair_grad, flag, out = expert_rows(own, came, gate, places, weight_in, weight_out, expert, groups)
        outs += out
        grads.append((x_rows, pair_grad, grad_rows, hidden))

    terms = [outs[0].astype(F32)]
    for mine, other in zip(outs[1::2], outs[2::2]):
        terms.append(mine.astype(F32) + swap_cores(other).astype(F32))
    total = terms.pop()
    while terms:
        total = total.astype(BF16)
        if len(terms) == steps - 2:
            total = after(total, grad_gate_up, grad_down)
        came = lax.ppermute(total, "expert", backward)
        if len(terms) == steps:
            x_rows, pair_grad, grad_rows, hidden = grads[-1]
            grads[-1] = (x_rows, after(pair_grad, came), grad_rows, after(hidden, came))

            def outer(left, right):
                left = jnp.concatenate([chunk[left] for chunk in grads])
                right = jnp.concatenate([chunk[right] for chunk in grads])
                return lax.dot_general(
                    left, right, (((0,), (0,)), ((), ())), preferred_element_type=F32
                ).astype(BF16)[None]

            grad_gate_up, grad_down = outer(0, 1), outer(2, 3)
        base, came = terms.pop(), came.astype(F32)
        if came.shape[0] < chip:
            total = jnp.concatenate([base[:unit] + came, base[unit:]], axis=0)
        else:
            total = base + came

    total = total.astype(BF16).reshape(2, 2, tok_dev, -1)
    mine = lax.dynamic_index_in_dim(total, replica, 1, keepdims=False)
    theirs = lax.dynamic_index_in_dim(total, 1 - replica, 1, keepdims=False)[:, :, : 2 * half]
    kept = mine[0].astype(F32) + swap_cores(mine[1]).astype(F32)
    other = swap_pair(theirs[0]).astype(F32) + swap_both(theirs[1]).astype(F32)
    both = by_replica(kept[:, : 2 * half], other, replica).astype(BF16)
    mixed = jnp.concatenate([both[0, :, :half], both[1, :, :half]], axis=1)
    grad_tokens = jnp.concatenate([both[0, :, half:], both[1, :, half:]], axis=1)
    scores = kept[:, 2 * half :]
    scores = scores[:, :groups] + scores[:, groups : 2 * groups]
    named = route_ids[:, :, None] == jnp.arange(groups, dtype=jnp.int32)[None, None, :]
    grad_gates = jnp.sum(jnp.where(named, scores[:, None, :], 0.0), axis=2)
    return (mixed, grad_tokens, grad_gates, grad_gate_up, grad_down)


def slot_capacity(tok_dev, top_count, experts):
    assignments = tok_dev * top_count
    return min(tok_dev, max(2, assignments // experts + max(1, assignments // (3 * experts))))


def body(tokens, route_ids, gates, cotangent, w_gate_up, w_down):
    groups, replicas = lax.axis_size("expert"), lax.axis_size("dp")
    gathered = 2 * groups * tokens.shape[0] * replicas * w_gate_up.shape[1] * 2
    small = gathered <= 8 * 1024 * 1024 and 3 * groups <= 128 and groups % 4 == 0 and groups >= 16
    if replicas == 2 and w_gate_up.shape[0] == 1 and small:
        return body_by_width(tokens, route_ids, gates, cotangent, w_gate_up, w_down)
    return body_by_slots(tokens, route_ids, gates, cotangent, w_gate_up, w_down)


def solution(mesh):
    placed = (
        P(("expert", "dp"), None),
        P(("expert", "dp"), None),
        P(("expert", "dp"), None),
        P(("expert", "dp"), None),
        P("expert", "dp", None),
        P("expert", "dp", None),
    )
    return jax.shard_map(
        body,
        mesh=mesh,
        in_specs=placed,
        out_specs=(
            P(("expert", "dp"), None),
            P(("expert", "dp"), None),
            P(("expert", "dp"), None),
            P("expert", "dp", None),
            P("expert", "dp", None),
        ),
        check_vma=False,
    )
```

```python
import jax
import jax.numpy as jnp
from jax import lax
from jax.experimental import pallas as pl
from jax.experimental.pallas import tpu as pltpu
from jax.sharding import PartitionSpec as P


def expert_forward(x_rows, weight_in, weight_out, hidden_units):
    pre_act = jnp.dot(x_rows, weight_in, preferred_element_type=jnp.float32)
    gate_pre = pre_act[:, :hidden_units]
    up_pre = pre_act[:, hidden_units:]
    sigmoid_gate = jax.nn.sigmoid(gate_pre)
    activation = gate_pre * sigmoid_gate
    hidden = (activation * up_pre).astype(jnp.bfloat16)
    expert_out = lax.dot_general(
        hidden, weight_out, (((1,), (1,)), ((), ())), preferred_element_type=jnp.float32
    ).astype(jnp.bfloat16)
    return (gate_pre, up_pre, sigmoid_gate, activation, hidden, expert_out)


def expert_backward(saved, grad_rows, weight_in, weight_out):
    gate_pre, up_pre, sigmoid_gate, activation, hidden, expert_out = saved
    hidden_grad = jnp.dot(grad_rows, weight_out, preferred_element_type=jnp.float32)
    gate_grad = (
        hidden_grad * up_pre * (sigmoid_gate * (1.0 + gate_pre * (1.0 - sigmoid_gate)))
    ).astype(jnp.bfloat16)
    up_grad = (hidden_grad * activation).astype(jnp.bfloat16)
    pair_grad = jnp.concatenate([gate_grad, up_grad], axis=1)
    input_grad = lax.dot_general(
        pair_grad, weight_in, (((1,), (1,)), ((), ())), preferred_element_type=jnp.float32
    ).astype(jnp.bfloat16)
    return (pair_grad, input_grad)


def outer_blocks(left, right, pieces):
    span = left.shape[1] // pieces
    results = []
    for piece in range(pieces):
        product = lax.dot_general(
            left[:, piece * span : (piece + 1) * span],
            right,
            (((0,), (0,)), ((), ())),
            preferred_element_type=jnp.float32,
        )
        results.append(product.astype(jnp.bfloat16))
    return jnp.stack(results, axis=0)


def replica_total(received):
    return jnp.sum(received.astype(jnp.float32), axis=0).astype(jnp.bfloat16)


def body_by_slots(tokens, route_ids, gates, cotangent, w_gate_up, w_down):
    tok_dev, model_width = tokens.shape
    top_count = route_ids.shape[1]
    groups = lax.axis_size("expert")
    replicas = lax.axis_size("dp")
    local_experts = w_gate_up.shape[0]
    hidden_units = w_down.shape[2]
    experts = groups * local_experts
    assignments = tok_dev * top_count
    capacity = min(tok_dev, max(2, assignments // experts + max(1, assignments // (3 * experts))))
    flat_ids = route_ids.reshape(assignments)
    onehot = (flat_ids[:, None] == jnp.arange(experts, dtype=jnp.int32)[None, :]).astype(jnp.int32)
    earlier = jnp.sum(
        (jnp.cumsum(onehot, axis=0, dtype=jnp.int32) - onehot) * onehot, axis=1, dtype=jnp.int32
    )
    position = flat_ids * capacity + earlier
    source = (
        jnp.full((experts * capacity,), assignments, jnp.int32)
        .at[position]
        .set(jnp.arange(assignments, dtype=jnp.int32))
    )
    token_row = source // top_count
    tok_pad = jnp.concatenate([tokens, jnp.zeros((1, model_width), jnp.bfloat16)], axis=0)
    cot_pad = jnp.concatenate([cotangent, jnp.zeros((1, model_width), jnp.bfloat16)], axis=0)
    gate_pad = jnp.concatenate([gates.reshape(assignments), jnp.zeros((1,), jnp.float32)], axis=0)
    send_rows = tok_pad[token_row].reshape(experts, capacity, model_width)
    send_grads = (gate_pad[source][:, None] * cot_pad[token_row].astype(jnp.float32)).astype(
        jnp.bfloat16
    )
    send_grads = send_grads.reshape(experts, capacity, model_width)
    weights_in, weights_out = (
        lax.all_gather(w_gate_up, "dp", axis=1, tiled=True),
        lax.all_gather(w_down, "dp", axis=1, tiled=True),
    )
    rows_in, grads_in = (
        lax.all_to_all(send_rows, "expert", split_axis=0, concat_axis=1, tiled=True),
        lax.all_to_all(send_grads, "expert", split_axis=0, concat_axis=1, tiled=True),
    )
    local = 0
    forward_parts = expert_forward(
        rows_in[local], weights_in[local], weights_out[local], hidden_units
    )
    saved_all = [forward_parts]
    out_list = [forward_parts[5]]
    down_list = [outer_blocks(grads_in[local], forward_parts[4], replicas)]
    expert_outs = jnp.stack(out_list, axis=0)
    down_stack = jnp.stack(down_list, axis=1)
    outs_back = lax.all_to_all(expert_outs, "expert", split_axis=1, concat_axis=0, tiled=True)
    local = 0
    pair_grad, input_grad = expert_backward(
        saved_all[local], grads_in[local], weights_in[local], weights_out[local]
    )
    input_list = [input_grad]
    gate_up_list = [outer_blocks(rows_in[local], pair_grad, replicas)]
    input_grads = jnp.stack(input_list, axis=0)
    gate_up_stack = jnp.stack(gate_up_list, axis=1)
    grads_back = lax.all_to_all(input_grads, "expert", split_axis=1, concat_axis=0, tiled=True)
    gate_up_received, down_received = (
        lax.all_to_all(gate_up_stack, "dp", split_axis=0, concat_axis=0, tiled=True),
        lax.all_to_all(down_stack, "dp", split_axis=0, concat_axis=0, tiled=True),
    )
    grad_gate_up = replica_total(gate_up_received)
    grad_down = replica_total(down_received)
    out_rows = outs_back.reshape(experts * capacity, model_width)[position].reshape(
        tok_dev, top_count, model_width
    )
    mixed = jnp.sum(gates[:, :, None] * out_rows.astype(jnp.float32), axis=1).astype(jnp.bfloat16)
    grad_gates = jnp.einsum("td,tkd->tk", cotangent, out_rows, preferred_element_type=jnp.float32)
    back_rows = grads_back.reshape(experts * capacity, model_width)[position].reshape(
        tok_dev, top_count, model_width
    )
    grad_tokens = jnp.sum(back_rows.astype(jnp.float32), axis=1).astype(jnp.bfloat16)
    return (mixed, grad_tokens, grad_gates, grad_gate_up, grad_down)


F32, BF16 = jnp.float32, jnp.bfloat16
LANES = 128
FREE = pl.CostEstimate(flops=0, bytes_accessed=0, transcendentals=0)


def run(kernel, outs, args, scalars=0):
    spaces = [pltpu.SMEM] * scalars + [pltpu.VMEM] * (len(args) - scalars)
    return pl.pallas_call(
        kernel,
        out_shape=outs,
        in_specs=[pl.BlockSpec(memory_space=space) for space in spaces],
        out_specs=[pl.BlockSpec(memory_space=pltpu.VMEM) for _ in outs],
        compiler_params=pltpu.CompilerParams(vmem_limit_bytes=16 * 1024 * 1024),
        cost_estimate=FREE,
    )(*args)


def dot_nn(left, right):
    return jnp.dot(left, right, preferred_element_type=F32)


def dot_nt(left, right):
    return lax.dot_general(left, right, (((1,), (1,)), ((), ())), preferred_element_type=F32)


def own_column(expert, groups):
    lane = lax.broadcasted_iota(jnp.int32, (1, LANES), 1)
    hit = (lane == expert) | (lane == expert + groups) | (lane == expert + 2 * groups)
    return jnp.where(hit, 1.0, 0.0)


def prepare(tokens, route_ids, gates, cotangent, replica, groups):
    rows, width = tokens.shape
    half = width // 2

    def kernel(replica_ref, tok_ref, id_ref, gate_ref, cot_ref, keep_ref, send_ref):
        low = replica_ref[0] == 0
        line = lax.broadcasted_iota(jnp.int32, (LANES, rows), 0)
        term = lax.div(line, groups)
        named = line - term * groups
        dense = jnp.zeros((LANES, rows), F32)
        for k in range(id_ref.shape[0]):
            dense = dense + jnp.where(id_ref[k : k + 1, :] == named, gate_ref[k : k + 1, :], 0.0)
        first = dense.astype(BF16).astype(F32)
        second = (dense - first).astype(BF16).astype(F32)
        third = dense - first - second
        meta = jnp.where(term == 0, first, jnp.where(term == 1, second, jnp.where(term == 2, third, 0.0))).astype(BF16)
        down = lax.broadcasted_iota(jnp.int32, (rows, rows), 0)
        along = lax.broadcasted_iota(jnp.int32, (rows, rows), 1)
        meta = dot_nt(jnp.where(down == along, 1.0, 0.0).astype(BF16), meta).astype(BF16)
        for ref, start in ((tok_ref, 0), (cot_ref, half + LANES)):
            left, right = ref[:, :half], ref[:, half:]
            keep_ref[:, start : start + half] = jnp.where(low, left, right)
            send_ref[:, start : start + half] = jnp.where(low, right, left)
        keep_ref[:, half : half + LANES] = meta
        send_ref[:, half : half + LANES] = meta

    out = jax.ShapeDtypeStruct((rows, width + LANES), BF16)
    args = [tokens, route_ids, gates, cotangent]
    return pl.pallas_call(
        kernel,
        grid=(1,),
        out_shape=[out, out],
        in_specs=[pl.BlockSpec(memory_space=pltpu.SMEM)] + [pl.BlockSpec(arg.shape, lambda i: (0, 0)) for arg in args],
        out_specs=[pl.BlockSpec(out.shape, lambda i: (0, 0))] * 2,
        compiler_params=pltpu.CompilerParams(vmem_limit_bytes=60 * 1024 * 1024),
        cost_estimate=FREE,
    )(replica, *args)


def partial_products(pieces, weight_in, weight_out, expert, groups, tok_dev, capacity):
    counts = [piece.shape[0] // tok_dev * capacity for piece in pieces]
    total, number = sum(counts), len(pieces)
    half, columns = weight_in.shape
    hidden_units = weight_out.shape[1]

    def kernel(expert_ref, *refs):
        rows_refs, refs = refs[:number], refs[number:]
        in_ref, out_ref, x_ref, grad_ref, gate_ref, own_ref, send_ref = refs[:7]
        places = refs[7:]
        column = own_column(expert_ref[0], groups)
        column_rows = jnp.broadcast_to(column, (8, LANES)).astype(BF16)
        start = 0
        for piece in range(number):
            rows, count = rows_refs[piece].shape[0], counts[piece]
            meta = rows_refs[piece][:, half : half + LANES]
            gate_row = dot_nt(column_rows, meta)
            gate_col = jnp.sum(meta.astype(F32) * column, axis=1, keepdims=True)
            down = lax.broadcasted_iota(jnp.int32, (rows, rows), 0)
            along = lax.broadcasted_iota(jnp.int32, (rows, rows), 1)
            first_down, first_along = jnp.zeros_like(down), jnp.zeros_like(along)
            base_down, base_along = jnp.zeros_like(down), jnp.zeros_like(along)
            for device in range(1, rows // tok_dev):
                first_down += jnp.where(down >= device * tok_dev, tok_dev, 0)
                first_along += jnp.where(along >= device * tok_dev, tok_dev, 0)
                base_down += jnp.where(down >= device * tok_dev, capacity, 0)
                base_along += jnp.where(along >= device * tok_dev, capacity, 0)
            lower = jnp.where((along < down) & (along >= first_down), 1.0, 0.0).astype(BF16)
            upper = jnp.where((down < along) & (down >= first_along), 1.0, 0.0).astype(BF16)
            on_row = jnp.where(gate_row > 0.0, 1.0, 0.0)
            on_col = jnp.where(gate_col > 0.0, 1.0, 0.0)
            rank_row = dot_nn(on_row.astype(BF16), upper)
            rank_col = dot_nn(lower, jnp.broadcast_to(on_col, (rows, LANES)).astype(BF16))
            place_row = jnp.where(on_row > 0.0, rank_row + base_along[:8].astype(F32), -1.0)[:1, :]
            place_col = jnp.where(on_col > 0.0, rank_col[:, :1] + base_down[:, :1].astype(F32), -1.0)
            slot_down = lax.broadcasted_iota(jnp.int32, (count, rows), 0).astype(F32)
            slot_along = lax.broadcasted_iota(jnp.int32, (rows, count), 1).astype(F32)
            pick = jnp.where(place_row == slot_down, 1.0, 0.0).astype(BF16)
            places[piece][...] = jnp.where(place_col == slot_along, 1.0, 0.0).astype(BF16)
            picked = dot_nn(pick, rows_refs[piece][...])
            x_ref[start : start + count, :] = picked[:, :half].astype(BF16)
            gate = jnp.sum(picked[:, half : half + LANES] * column, axis=1, keepdims=True)
            gate_ref[start : start + count, :] = jnp.broadcast_to(gate, (count, LANES))
            grad_ref[start : start + count, :] = (gate * picked[:, half + LANES :]).astype(BF16)
            start += count
        for left, right, at in ((x_ref, in_ref, 0), (grad_ref, out_ref, columns)):
            part = dot_nn(left[...], right[...])
            own_ref[:, at : at + part.shape[1]] = part
            part = part.astype(BF16)
            send_ref[: total // 2, at : at + part.shape[1]] = part[total // 2 :]
            send_ref[total // 2 :, at : at + part.shape[1]] = part[: total // 2]

    shape = jax.ShapeDtypeStruct
    outs = [shape((total, half), BF16), shape((total, half), BF16), shape((total, LANES), F32)]
    outs += [shape((total, columns + hidden_units), F32), shape((total, columns + hidden_units), BF16)]
    outs += [shape((piece.shape[0], count), BF16) for piece, count in zip(pieces, counts)]
    got = run(kernel, outs, [expert, *pieces, weight_in, weight_out], 1)
    return (*got[:5], got[5:])


def expert_rows(own, came, gate, places, weight_in, weight_out, expert, groups):
    total = own.shape[0]
    half, columns = weight_in.shape
    hidden_units, number = columns // 2, len(places)

    def kernel(expert_ref, own_ref, came_ref, gate_ref, in_ref, out_ref, *refs):
        put, hidden_ref, pair_ref, flag_ref, outs = refs[:number], *refs[number : number + 3], refs[number + 3 :]
        gate_pre = own_ref[:, :hidden_units] + came_ref[:, :hidden_units].astype(F32)
        up_pre = own_ref[:, hidden_units:columns] + came_ref[:, hidden_units:columns].astype(F32)
        hidden_grad = own_ref[:, columns:] + came_ref[:, columns:].astype(F32)
        sig = jax.nn.sigmoid(gate_pre)
        act = gate_pre * sig
        hidden = (act * up_pre).astype(BF16)
        hidden_ref[...] = hidden
        pair_ref[:, :hidden_units] = (hidden_grad * up_pre * (sig * (1.0 + gate_pre * (1.0 - sig)))).astype(BF16)
        pair_ref[:, hidden_units:] = (hidden_grad * act).astype(BF16)
        gate = gate_ref[...]
        flag_ref[...] = gate[:8]
        score = jnp.sum(hidden.astype(F32) * hidden_grad, axis=1, keepdims=True)
        score = score / jnp.where(gate > 0.0, gate, 1.0)
        first = score.astype(BF16).astype(F32)
        lane = lax.broadcasted_iota(jnp.int32, (total, LANES), 1)
        expert = expert_ref[0]
        score = jnp.where(lane == expert, first, jnp.where(lane == expert + groups, score - first, 0.0)).astype(BF16)
        forth = (gate[:, :1] * dot_nt(hidden, out_ref[...])).astype(BF16)
        back = dot_nt(pair_ref[...], in_ref[...]).astype(BF16)
        start = 0
        for piece in range(number):
            count = put[piece].shape[1]
            place = put[piece][...]
            for rows, at in ((forth, 0), (back, half), (score, 2 * half)):
                rows = rows[start : start + count, :]
                outs[piece][:, at : at + rows.shape[1]] = dot_nn(place, rows).astype(BF16)
            start += count

    shape = jax.ShapeDtypeStruct
    outs = [shape((total, hidden_units), BF16), shape((total, columns), BF16), shape((8, LANES), F32)]
    outs += [shape((place.shape[0], 2 * half + LANES), BF16) for place in places]
    got = run(kernel, outs, [expert, own, came, gate, weight_in, weight_out, *places], 1)
    return got[0], got[1], got[2], got[3:]


def ring_pairs(groups):
    chips = groups // 2
    levels = chips // 2
    order = [2 * z for z in range(levels)] + [2 * z + 1 for z in reversed(range(levels))]
    forward = []
    for place in range(chips):
        forward.append((2 * order[place], 2 * order[(place + 1) % chips]))
        forward.append((2 * order[(place + 1) % chips] + 1, 2 * order[place] + 1))
    backward = [(to, source) for source, to in forward]
    cores = [(index, index ^ 1) for index in range(groups)]
    return forward, backward, cores


def swap_pair(value):
    return lax.ppermute(value, "dp", [(0, 1), (1, 0)])


def swap_both(value):
    groups = lax.axis_size("expert")
    pairs = [(2 * e + r, 2 * (e ^ 1) + 1 - r) for e in range(groups) for r in range(2)]
    return lax.ppermute(value, ("expert", "dp"), pairs)


def by_replica(own, other, replica):
    return jnp.where(replica == 0, jnp.stack([own, other]), jnp.stack([other, own]))


def after(value, *anchors):
    anywhere = pl.BlockSpec(memory_space=pl.ANY)
    return pl.pallas_call(
        lambda *refs: None,
        out_shape=jax.ShapeDtypeStruct(value.shape, value.dtype),
        in_specs=[anywhere] * (1 + len(anchors)),
        out_specs=anywhere,
        input_output_aliases={0: 0},
        compiler_params=pltpu.CompilerParams(vmem_limit_bytes=1024 * 1024),
        cost_estimate=FREE,
    )(value, *anchors)


class Order:
    def __init__(self):
        self.last = None

    def __call__(self, value, *anchors):
        if self.last is not None:
            value = after(value, self.last, *anchors)
        self.last = value
        return value


def body_by_width(tokens, route_ids, gates, cotangent, w_gate_up, w_down):
    tok_dev, model_width = tokens.shape
    top_count = route_ids.shape[1]
    groups = lax.axis_size("expert")
    replica = lax.axis_index("dp")
    expert = lax.axis_index("expert").astype(jnp.int32).reshape(1)
    half = w_gate_up.shape[1]
    capacity = slot_capacity(tok_dev, top_count, groups)
    steps = groups // 4
    weight_in, weight_out = w_gate_up[0], w_down[0]
    forward, backward, cores = ring_pairs(groups)
    unit = 2 * tok_dev

    def swap_cores(value):
        return lax.ppermute(value, "expert", cores)

    def products(pieces):
        *kept, own, send, places = partial_products(
            pieces, weight_in, weight_out, expert, groups, tok_dev, capacity
        )
        return [kept, own, send, places, swap_pair(send)]

    def ring(block, step):
        return lax.ppermute(block if step < steps else block[:tok_dev], "expert", forward)

    order = Order()
    keep, send = prepare(tokens, route_ids.T, gates.T, cotangent, replica.astype(jnp.int32).reshape(1), groups)
    second = jnp.concatenate([order(swap_pair(send)), order(swap_both(send))], axis=0)
    first = jnp.concatenate([keep, order(swap_cores(keep))], axis=0)
    chunks = [products([first, second])]

    def wait_for(number):
        chunks[number][4] = order(chunks[number][4], chunks[-1][0][2])

    for step in range(1, steps + 1):
        first = order(ring(first, step))
        if 3 <= step < steps:
            wait_for(step - 2)
        second = order(ring(second, step), chunks[-1][0][2])
        if step == 1 or step == steps:
            wait_for(max(step - 2, 0))
        first_other, second_other = swap_cores(first), order(swap_cores(second))
        chunks.append(products([first, first_other, second, second_other]))

    outs, grads = ([], []), []
    for number, ((x_rows, grad_rows, gate), own, _, places, came) in enumerate(chunks):
        if number:
            came = after(came, flag)
        hidden, pair_grad, flag, out = expert_rows(own, came, gate, places, weight_in, weight_out, expert, groups)
        outs[0].extend(out[: len(out) // 2])
        outs[1].extend(out[len(out) // 2 :])
        grads.append((x_rows, pair_grad, grad_rows, hidden))

    terms = [[out[0].astype(F32)] for out in outs]
    for stream in (1, 0):
        for mine, other in zip(outs[stream][1::2], outs[stream][2::2]):
            terms[stream].append(mine.astype(F32) + swap_cores(other).astype(F32))
    totals = [term.pop() for term in terms]
    for step in reversed(range(steps)):
        for stream in (1, 0):
            total = totals[stream].astype(BF16)
            if step == steps - 3 and stream == 0:
                total = after(total, grad_gate_up, grad_down)
            came = order(lax.ppermute(total, "expert", backward))
            if step == steps - 1 and stream == 0:
                x_rows, pair_grad, grad_rows, hidden = grads[-1]
                grads[-1] = (x_rows, after(pair_grad, came), grad_rows, after(hidden, came))
                grad_gate_up, grad_down = outer_products(grads, 0, 1), outer_products(grads, 2, 3)
            base, came = terms[stream].pop(), came.astype(F32)
            if came.shape[0] < unit:
                totals[stream] = jnp.concatenate([base[:tok_dev] + came, base[tok_dev:]], axis=0)
            else:
                totals[stream] = base + came

    here, there = (total.astype(BF16) for total in totals)
    there = there[:, : 2 * half]
    other = swap_pair(there[:tok_dev]).astype(F32) + swap_both(there[tok_dev:]).astype(F32)
    kept = here[:tok_dev].astype(F32) + swap_cores(here[tok_dev:]).astype(F32)
    both = by_replica(kept[:, : 2 * half], other, replica).astype(BF16)
    mixed = jnp.concatenate([both[0, :, :half], both[1, :, :half]], axis=1)
    grad_tokens = jnp.concatenate([both[0, :, half:], both[1, :, half:]], axis=1)
    scores = kept[:, 2 * half :]
    scores = scores[:, :groups] + scores[:, groups : 2 * groups]
    named = route_ids[:, :, None] == jnp.arange(groups, dtype=jnp.int32)[None, None, :]
    grad_gates = jnp.sum(jnp.where(named, scores[:, None, :], 0.0), axis=2)
    return (mixed, grad_tokens, grad_gates, grad_gate_up, grad_down)


def outer_products(chunks, left, right):
    left = jnp.concatenate([chunk[left] for chunk in chunks])
    right = jnp.concatenate([chunk[right] for chunk in chunks])
    return lax.dot_general(left, right, (((0,), (0,)), ((), ())), preferred_element_type=F32).astype(BF16)[None]


def slot_capacity(tok_dev, top_count, experts):
    assignments = tok_dev * top_count
    return min(tok_dev, max(2, assignments // experts + max(1, assignments // (3 * experts))))


def body(tokens, route_ids, gates, cotangent, w_gate_up, w_down):
    groups, replicas = lax.axis_size("expert"), lax.axis_size("dp")
    gathered = 2 * groups * tokens.shape[0] * replicas * w_gate_up.shape[1] * 2
    small = gathered <= 8 * 1024 * 1024 and 3 * groups <= 128 and groups % 4 == 0 and groups >= 16
    if replicas == 2 and w_gate_up.shape[0] == 1 and small:
        return body_by_width(tokens, route_ids, gates, cotangent, w_gate_up, w_down)
    return body_by_slots(tokens, route_ids, gates, cotangent, w_gate_up, w_down)


def solution(mesh):
    placed = (
        P(("expert", "dp"), None),
        P(("expert", "dp"), None),
        P(("expert", "dp"), None),
        P(("expert", "dp"), None),
        P("expert", "dp", None),
        P("expert", "dp", None),
    )
    return jax.shard_map(
        body,
        mesh=mesh,
        in_specs=placed,
        out_specs=(
            P(("expert", "dp"), None),
            P(("expert", "dp"), None),
            P(("expert", "dp"), None),
            P("expert", "dp", None),
            P("expert", "dp", None),
        ),
        check_vma=False,
    )
```

```python
import jax
import jax.numpy as jnp
from jax import lax
from jax.experimental import pallas as pl
from jax.experimental.pallas import tpu as pltpu
from jax.sharding import PartitionSpec as P


def expert_forward(x_rows, weight_in, weight_out, hidden_units):
    pre_act = jnp.dot(x_rows, weight_in, preferred_element_type=jnp.float32)
    gate_pre = pre_act[:, :hidden_units]
    up_pre = pre_act[:, hidden_units:]
    sigmoid_gate = jax.nn.sigmoid(gate_pre)
    activation = gate_pre * sigmoid_gate
    hidden = (activation * up_pre).astype(jnp.bfloat16)
    expert_out = lax.dot_general(
        hidden, weight_out, (((1,), (1,)), ((), ())), preferred_element_type=jnp.float32
    ).astype(jnp.bfloat16)
    return (gate_pre, up_pre, sigmoid_gate, activation, hidden, expert_out)


def expert_backward(saved, grad_rows, weight_in, weight_out):
    gate_pre, up_pre, sigmoid_gate, activation, hidden, expert_out = saved
    hidden_grad = jnp.dot(grad_rows, weight_out, preferred_element_type=jnp.float32)
    gate_grad = (
        hidden_grad * up_pre * (sigmoid_gate * (1.0 + gate_pre * (1.0 - sigmoid_gate)))
    ).astype(jnp.bfloat16)
    up_grad = (hidden_grad * activation).astype(jnp.bfloat16)
    pair_grad = jnp.concatenate([gate_grad, up_grad], axis=1)
    input_grad = lax.dot_general(
        pair_grad, weight_in, (((1,), (1,)), ((), ())), preferred_element_type=jnp.float32
    ).astype(jnp.bfloat16)
    return (pair_grad, input_grad)


def outer_blocks(left, right, pieces):
    span = left.shape[1] // pieces
    results = []
    for piece in range(pieces):
        product = lax.dot_general(
            left[:, piece * span : (piece + 1) * span],
            right,
            (((0,), (0,)), ((), ())),
            preferred_element_type=jnp.float32,
        )
        results.append(product.astype(jnp.bfloat16))
    return jnp.stack(results, axis=0)


def replica_total(received):
    return jnp.sum(received.astype(jnp.float32), axis=0).astype(jnp.bfloat16)


def body_by_slots(tokens, route_ids, gates, cotangent, w_gate_up, w_down):
    tok_dev, model_width = tokens.shape
    top_count = route_ids.shape[1]
    groups = lax.axis_size("expert")
    replicas = lax.axis_size("dp")
    local_experts = w_gate_up.shape[0]
    hidden_units = w_down.shape[2]
    experts = groups * local_experts
    assignments = tok_dev * top_count
    capacity = min(tok_dev, max(2, assignments // experts + max(1, assignments // (3 * experts))))
    flat_ids = route_ids.reshape(assignments)
    onehot = (flat_ids[:, None] == jnp.arange(experts, dtype=jnp.int32)[None, :]).astype(jnp.int32)
    earlier = jnp.sum(
        (jnp.cumsum(onehot, axis=0, dtype=jnp.int32) - onehot) * onehot, axis=1, dtype=jnp.int32
    )
    position = flat_ids * capacity + earlier
    source = (
        jnp.full((experts * capacity,), assignments, jnp.int32)
        .at[position]
        .set(jnp.arange(assignments, dtype=jnp.int32))
    )
    token_row = source // top_count
    tok_pad = jnp.concatenate([tokens, jnp.zeros((1, model_width), jnp.bfloat16)], axis=0)
    cot_pad = jnp.concatenate([cotangent, jnp.zeros((1, model_width), jnp.bfloat16)], axis=0)
    gate_pad = jnp.concatenate([gates.reshape(assignments), jnp.zeros((1,), jnp.float32)], axis=0)
    send_rows = tok_pad[token_row].reshape(experts, capacity, model_width)
    send_grads = (gate_pad[source][:, None] * cot_pad[token_row].astype(jnp.float32)).astype(
        jnp.bfloat16
    )
    send_grads = send_grads.reshape(experts, capacity, model_width)
    weights_in, weights_out = (
        lax.all_gather(w_gate_up, "dp", axis=1, tiled=True),
        lax.all_gather(w_down, "dp", axis=1, tiled=True),
    )
    rows_in, grads_in = (
        lax.all_to_all(send_rows, "expert", split_axis=0, concat_axis=1, tiled=True),
        lax.all_to_all(send_grads, "expert", split_axis=0, concat_axis=1, tiled=True),
    )
    local = 0
    forward_parts = expert_forward(
        rows_in[local], weights_in[local], weights_out[local], hidden_units
    )
    saved_all = [forward_parts]
    out_list = [forward_parts[5]]
    down_list = [outer_blocks(grads_in[local], forward_parts[4], replicas)]
    expert_outs = jnp.stack(out_list, axis=0)
    down_stack = jnp.stack(down_list, axis=1)
    outs_back = lax.all_to_all(expert_outs, "expert", split_axis=1, concat_axis=0, tiled=True)
    local = 0
    pair_grad, input_grad = expert_backward(
        saved_all[local], grads_in[local], weights_in[local], weights_out[local]
    )
    input_list = [input_grad]
    gate_up_list = [outer_blocks(rows_in[local], pair_grad, replicas)]
    input_grads = jnp.stack(input_list, axis=0)
    gate_up_stack = jnp.stack(gate_up_list, axis=1)
    grads_back = lax.all_to_all(input_grads, "expert", split_axis=1, concat_axis=0, tiled=True)
    gate_up_received, down_received = (
        lax.all_to_all(gate_up_stack, "dp", split_axis=0, concat_axis=0, tiled=True),
        lax.all_to_all(down_stack, "dp", split_axis=0, concat_axis=0, tiled=True),
    )
    grad_gate_up = replica_total(gate_up_received)
    grad_down = replica_total(down_received)
    out_rows = outs_back.reshape(experts * capacity, model_width)[position].reshape(
        tok_dev, top_count, model_width
    )
    mixed = jnp.sum(gates[:, :, None] * out_rows.astype(jnp.float32), axis=1).astype(jnp.bfloat16)
    grad_gates = jnp.einsum("td,tkd->tk", cotangent, out_rows, preferred_element_type=jnp.float32)
    back_rows = grads_back.reshape(experts * capacity, model_width)[position].reshape(
        tok_dev, top_count, model_width
    )
    grad_tokens = jnp.sum(back_rows.astype(jnp.float32), axis=1).astype(jnp.bfloat16)
    return (mixed, grad_tokens, grad_gates, grad_gate_up, grad_down)


F32, BF16 = jnp.float32, jnp.bfloat16
LANES = 128
FREE = pl.CostEstimate(flops=0, bytes_accessed=0, transcendentals=0)


def run(kernel, outs, args, scalars=0):
    spaces = [pltpu.SMEM] * scalars + [pltpu.VMEM] * (len(args) - scalars)
    return pl.pallas_call(
        kernel,
        out_shape=outs,
        in_specs=[pl.BlockSpec(memory_space=space) for space in spaces],
        out_specs=[pl.BlockSpec(memory_space=pltpu.VMEM) for _ in outs],
        compiler_params=pltpu.CompilerParams(vmem_limit_bytes=10 * 1024 * 1024),
        cost_estimate=FREE,
    )(*args)


def dot_nn(left, right):
    return jnp.dot(left, right, preferred_element_type=F32)


def dot_nt(left, right):
    return lax.dot_general(left, right, (((1,), (1,)), ((), ())), preferred_element_type=F32)


def own_column(expert, groups):
    lane = lax.broadcasted_iota(jnp.int32, (1, LANES), 1)
    hit = (lane == expert) | (lane == expert + groups) | (lane == expert + 2 * groups)
    return jnp.where(hit, 1.0, 0.0)


def prepare(tokens, route_ids, gates, cotangent, replica, groups):
    rows, width = tokens.shape
    half = width // 2

    def kernel(replica_ref, tok_ref, id_ref, gate_ref, cot_ref, keep_ref, send_ref):
        low = replica_ref[0] == 0
        line = lax.broadcasted_iota(jnp.int32, (LANES, rows), 0)
        term = lax.div(line, groups)
        named = line - term * groups
        dense = jnp.zeros((LANES, rows), F32)
        for k in range(id_ref.shape[0]):
            dense = dense + jnp.where(id_ref[k : k + 1, :] == named, gate_ref[k : k + 1, :], 0.0)
        first = dense.astype(BF16).astype(F32)
        second = (dense - first).astype(BF16).astype(F32)
        third = dense - first - second
        meta = jnp.where(term == 0, first, jnp.where(term == 1, second, jnp.where(term == 2, third, 0.0))).astype(BF16)
        down = lax.broadcasted_iota(jnp.int32, (rows, rows), 0)
        along = lax.broadcasted_iota(jnp.int32, (rows, rows), 1)
        meta = dot_nt(jnp.where(down == along, 1.0, 0.0).astype(BF16), meta).astype(BF16)
        for ref, start in ((tok_ref, 0), (cot_ref, half + LANES)):
            left, right = ref[:, :half], ref[:, half:]
            keep_ref[:, start : start + half] = jnp.where(low, left, right)
            send_ref[:, start : start + half] = jnp.where(low, right, left)
        keep_ref[:, half : half + LANES] = meta
        send_ref[:, half : half + LANES] = meta

    out = jax.ShapeDtypeStruct((rows, width + LANES), BF16)
    args = [tokens, route_ids, gates, cotangent]
    return pl.pallas_call(
        kernel,
        grid=(1,),
        out_shape=[out, out],
        in_specs=[pl.BlockSpec(memory_space=pltpu.SMEM)] + [pl.BlockSpec(arg.shape, lambda i: (0, 0)) for arg in args],
        out_specs=[pl.BlockSpec(out.shape, lambda i: (0, 0))] * 2,
        compiler_params=pltpu.CompilerParams(vmem_limit_bytes=60 * 1024 * 1024),
        cost_estimate=FREE,
    )(replica, *args)


def partial_products(pieces, weight_in, weight_out, expert, groups, tok_dev, capacity):
    counts = [piece.shape[0] // tok_dev * capacity for piece in pieces]
    total, number = sum(counts), len(pieces)
    half, columns = weight_in.shape
    hidden_units = weight_out.shape[1]

    def kernel(expert_ref, *refs):
        rows_refs, refs = refs[:number], refs[number:]
        in_ref, out_ref, x_ref, grad_ref, gate_ref, own_ref, send_ref = refs[:7]
        places = refs[7:]
        column = own_column(expert_ref[0], groups)
        column_rows = jnp.broadcast_to(column, (8, LANES)).astype(BF16)
        start = 0
        for piece in range(number):
            rows, count = rows_refs[piece].shape[0], counts[piece]
            meta = rows_refs[piece][:, half : half + LANES]
            gate_row = dot_nt(column_rows, meta)
            gate_col = jnp.sum(meta.astype(F32) * column, axis=1, keepdims=True)
            down = lax.broadcasted_iota(jnp.int32, (rows, rows), 0)
            along = lax.broadcasted_iota(jnp.int32, (rows, rows), 1)
            first_down, first_along = jnp.zeros_like(down), jnp.zeros_like(along)
            base_down, base_along = jnp.zeros_like(down), jnp.zeros_like(along)
            for device in range(1, rows // tok_dev):
                first_down += jnp.where(down >= device * tok_dev, tok_dev, 0)
                first_along += jnp.where(along >= device * tok_dev, tok_dev, 0)
                base_down += jnp.where(down >= device * tok_dev, capacity, 0)
                base_along += jnp.where(along >= device * tok_dev, capacity, 0)
            lower = jnp.where((along < down) & (along >= first_down), 1.0, 0.0).astype(BF16)
            upper = jnp.where((down < along) & (down >= first_along), 1.0, 0.0).astype(BF16)
            on_row = jnp.where(gate_row > 0.0, 1.0, 0.0)
            on_col = jnp.where(gate_col > 0.0, 1.0, 0.0)
            rank_row = dot_nn(on_row.astype(BF16), upper)
            rank_col = dot_nn(lower, jnp.broadcast_to(on_col, (rows, LANES)).astype(BF16))
            place_row = jnp.where(on_row > 0.0, rank_row + base_along[:8].astype(F32), -1.0)[:1, :]
            place_col = jnp.where(on_col > 0.0, rank_col[:, :1] + base_down[:, :1].astype(F32), -1.0)
            slot_down = lax.broadcasted_iota(jnp.int32, (count, rows), 0).astype(F32)
            slot_along = lax.broadcasted_iota(jnp.int32, (rows, count), 1).astype(F32)
            pick = jnp.where(place_row == slot_down, 1.0, 0.0).astype(BF16)
            places[piece][...] = jnp.where(place_col == slot_along, 1.0, 0.0).astype(BF16)
            picked = dot_nn(pick, rows_refs[piece][...])
            x_ref[start : start + count, :] = picked[:, :half].astype(BF16)
            gate = jnp.sum(picked[:, half : half + LANES] * column, axis=1, keepdims=True)
            gate_ref[start : start + count, :] = jnp.broadcast_to(gate, (count, LANES))
            grad_ref[start : start + count, :] = (gate * picked[:, half + LANES :]).astype(BF16)
            start += count
        for left, right, at in ((x_ref, in_ref, 0), (grad_ref, out_ref, columns)):
            part = dot_nn(left[...], right[...])
            own_ref[:, at : at + part.shape[1]] = part
            part = part.astype(BF16)
            send_ref[: total // 2, at : at + part.shape[1]] = part[total // 2 :]
            send_ref[total // 2 :, at : at + part.shape[1]] = part[: total // 2]

    shape = jax.ShapeDtypeStruct
    outs = [shape((total, half), BF16), shape((total, half), BF16), shape((total, LANES), F32)]
    outs += [shape((total, columns + hidden_units), F32), shape((total, columns + hidden_units), BF16)]
    outs += [shape((piece.shape[0], count), BF16) for piece, count in zip(pieces, counts)]
    got = run(kernel, outs, [expert, *pieces, weight_in, weight_out], 1)
    return (*got[:5], got[5:])


def expert_rows(own, came, gate, places, weight_in, weight_out, expert, groups):
    total = own.shape[0]
    half, columns = weight_in.shape
    hidden_units, number = columns // 2, len(places)

    def kernel(expert_ref, own_ref, came_ref, gate_ref, in_ref, out_ref, *refs):
        put, hidden_ref, pair_ref, flag_ref, outs = refs[:number], *refs[number : number + 3], refs[number + 3 :]
        gate_pre = own_ref[:, :hidden_units] + came_ref[:, :hidden_units].astype(F32)
        up_pre = own_ref[:, hidden_units:columns] + came_ref[:, hidden_units:columns].astype(F32)
        hidden_grad = own_ref[:, columns:] + came_ref[:, columns:].astype(F32)
        sig = jax.nn.sigmoid(gate_pre)
        act = gate_pre * sig
        hidden = (act * up_pre).astype(BF16)
        hidden_ref[...] = hidden
        pair_ref[:, :hidden_units] = (hidden_grad * up_pre * (sig * (1.0 + gate_pre * (1.0 - sig)))).astype(BF16)
        pair_ref[:, hidden_units:] = (hidden_grad * act).astype(BF16)
        gate = gate_ref[...]
        flag_ref[...] = gate[:8]
        score = jnp.sum(hidden.astype(F32) * hidden_grad, axis=1, keepdims=True)
        score = score / jnp.where(gate > 0.0, gate, 1.0)
        first = score.astype(BF16).astype(F32)
        lane = lax.broadcasted_iota(jnp.int32, (total, LANES), 1)
        expert = expert_ref[0]
        score = jnp.where(lane == expert, first, jnp.where(lane == expert + groups, score - first, 0.0)).astype(BF16)
        forth = (gate[:, :1] * dot_nt(hidden, out_ref[...])).astype(BF16)
        back = dot_nt(pair_ref[...], in_ref[...]).astype(BF16)
        start = 0
        for piece in range(number):
            count = put[piece].shape[1]
            place = put[piece][...]
            for rows, at in ((forth, 0), (back, half), (score, 2 * half)):
                rows = rows[start : start + count, :]
                outs[piece][:, at : at + rows.shape[1]] = dot_nn(place, rows).astype(BF16)
            start += count

    shape = jax.ShapeDtypeStruct
    outs = [shape((total, hidden_units), BF16), shape((total, columns), BF16), shape((8, LANES), F32)]
    outs += [shape((place.shape[0], 2 * half + LANES), BF16) for place in places]
    got = run(kernel, outs, [expert, own, came, gate, weight_in, weight_out, *places], 1)
    return got[0], got[1], got[2], got[3:]


def ring_pairs(groups):
    chips = groups // 2
    levels = chips // 2
    order = [2 * z for z in range(levels)] + [2 * z + 1 for z in reversed(range(levels))]
    forward = []
    for place in range(chips):
        forward.append((2 * order[place], 2 * order[(place + 1) % chips]))
        forward.append((2 * order[(place + 1) % chips] + 1, 2 * order[place] + 1))
    backward = [(to, source) for source, to in forward]
    cores = [(index, index ^ 1) for index in range(groups)]
    return forward, backward, cores


def swap_pair(value):
    return lax.ppermute(value, "dp", [(0, 1), (1, 0)])


def swap_both(value):
    groups = lax.axis_size("expert")
    pairs = [(2 * e + r, 2 * (e ^ 1) + 1 - r) for e in range(groups) for r in range(2)]
    return lax.ppermute(value, ("expert", "dp"), pairs)


def by_replica(own, other, replica):
    return jnp.where(replica == 0, jnp.stack([own, other]), jnp.stack([other, own]))


def after(value, *anchors):
    anywhere = pl.BlockSpec(memory_space=pl.ANY)
    return pl.pallas_call(
        lambda *refs: None,
        out_shape=jax.ShapeDtypeStruct(value.shape, value.dtype),
        in_specs=[anywhere] * (1 + len(anchors)),
        out_specs=anywhere,
        input_output_aliases={0: 0},
        compiler_params=pltpu.CompilerParams(vmem_limit_bytes=1024 * 1024),
        cost_estimate=FREE,
    )(value, *anchors)


class Order:
    def __init__(self):
        self.last = None

    def __call__(self, value, *anchors):
        if self.last is not None:
            value = after(value, self.last, *anchors)
        self.last = value
        return value


def body_by_width(tokens, route_ids, gates, cotangent, w_gate_up, w_down):
    tok_dev, model_width = tokens.shape
    top_count = route_ids.shape[1]
    groups = lax.axis_size("expert")
    replica = lax.axis_index("dp")
    expert = lax.axis_index("expert").astype(jnp.int32).reshape(1)
    half = w_gate_up.shape[1]
    capacity = slot_capacity(tok_dev, top_count, groups)
    steps = groups // 4
    weight_in, weight_out = w_gate_up[0], w_down[0]
    forward, backward, cores = ring_pairs(groups)
    unit = 2 * tok_dev

    def swap_cores(value):
        return lax.ppermute(value, "expert", cores)

    def products(pieces):
        *kept, own, send, places = partial_products(
            pieces, weight_in, weight_out, expert, groups, tok_dev, capacity
        )
        return [kept, own, send, places, swap_pair(send)]

    def ring(block, step):
        return lax.ppermute(block if step < steps else block[:tok_dev], "expert", forward)

    order = Order()
    keep, send = prepare(tokens, route_ids.T, gates.T, cotangent, replica.astype(jnp.int32).reshape(1), groups)
    second = jnp.concatenate([order(swap_pair(send)), order(swap_both(send))], axis=0)
    first = jnp.concatenate([keep, order(swap_cores(keep))], axis=0)
    chunks = [products([first, second])]

    def wait_for(number):
        chunks[number][4] = order(chunks[number][4], chunks[-1][0][2])

    for step in range(1, steps + 1):
        if step == steps:
            wait_for(step - 2)
        first = order(ring(first, step), chunks[-1][0][2])
        if 3 <= step < steps:
            wait_for(step - 2)
        second = order(ring(second, step))
        if step == 1:
            wait_for(0)
        first_other, second_other = swap_cores(first), order(swap_cores(second))
        chunks.append(products([first, first_other, second, second_other]))

    terms, grads, swapped = ([], []), [], []
    for number, ((x_rows, grad_rows, gate), own, _, places, came) in enumerate(chunks):
        if number == steps:
            came = order(came)
        elif number == steps - 1:
            for stream, place, other in swapped:
                terms[stream][place] += (order(other),)
            swapped = []
            came = order(came, flag, chunks[-1][0][2])
        elif number:
            came = after(came, flag)
        hidden, pair_grad, flag, out = expert_rows(own, came, gate, places, weight_in, weight_out, expert, groups)
        for stream in (1, 0):
            mine = out[stream * len(out) // 2 :][: len(out) // 2]
            terms[stream].append((mine[0],))
            if number:
                swapped.append((stream, number, swap_cores(mine[1])))
        grads.append((x_rows, pair_grad, grad_rows, hidden))
    for stream, place, other in swapped:
        terms[stream][place] += (other,)

    def pop_term(stream):
        return sum(term.astype(F32) for term in terms[stream].pop())

    totals = [pop_term(0), pop_term(1)]
    for step in reversed(range(steps)):
        for stream in (1, 0):
            total = totals[stream].astype(BF16)
            came = lax.ppermute(total, "expert", backward)
            if step == steps - 3 and stream == 0:
                came = after(came, grad_gate_up, grad_down)
            if step == steps - 2 and stream == 1:
                grads[0] = tuple(after(array, came) for array in grads[0])
                grad_gate_up, grad_down = outer_products(grads, 0, 1), outer_products(grads, 2, 3)
            base, came = pop_term(stream), came.astype(F32)
            if came.shape[0] < unit:
                totals[stream] = jnp.concatenate([base[:tok_dev] + came, base[tok_dev:]], axis=0)
            else:
                totals[stream] = base + came

    there = totals[1][:, : 2 * half].astype(BF16)
    kept = totals[0][:tok_dev], swap_cores(totals[0][tok_dev:].astype(BF16))
    scores = kept[0][:, 2 * half :] + kept[1][:, 2 * half :].astype(F32)
    scores = scores[:, :groups] + scores[:, groups : 2 * groups]
    named = route_ids[:, :, None] == jnp.arange(groups, dtype=jnp.int32)[None, None, :]
    grad_gates = jnp.sum(jnp.where(named, scores[:, None, :], 0.0), axis=2)
    other = swap_pair(there[:tok_dev]), after(swap_both(there[tok_dev:]), scores)
    mixed, grad_tokens = join_halves(kept, other, half, replica.astype(jnp.int32).reshape(1))
    return (mixed, grad_tokens, grad_gates, grad_gate_up, grad_down)


def join_halves(kept, other, half, replica):
    rows = kept[0].shape[0]

    def kernel(replica_ref, mine_ref, beside_ref, across_ref, diagonal_ref, *outs):
        low = replica_ref[0] == 0
        for number, out in enumerate(outs):
            at = slice(number * half, (number + 1) * half)
            here = mine_ref[:, at] + beside_ref[:, at].astype(F32)
            there = across_ref[:, at].astype(F32) + diagonal_ref[:, at].astype(F32)
            out[:, :half] = jnp.where(low, here, there).astype(BF16)
            out[:, half:] = jnp.where(low, there, here).astype(BF16)

    out = jax.ShapeDtypeStruct((rows, 2 * half), BF16)
    return run(kernel, [out, out], [replica, *kept, *other], 1)


def outer_products(chunks, left, right):
    left = jnp.concatenate([chunk[left] for chunk in chunks])
    right = jnp.concatenate([chunk[right] for chunk in chunks])
    return lax.dot_general(left, right, (((0,), (0,)), ((), ())), preferred_element_type=F32).astype(BF16)[None]


def slot_capacity(tok_dev, top_count, experts):
    assignments = tok_dev * top_count
    return min(tok_dev, max(2, assignments // experts + max(1, assignments // (3 * experts))))


def body(tokens, route_ids, gates, cotangent, w_gate_up, w_down):
    groups, replicas = lax.axis_size("expert"), lax.axis_size("dp")
    gathered = 2 * groups * tokens.shape[0] * replicas * w_gate_up.shape[1] * 2
    small = gathered <= 8 * 1024 * 1024 and 3 * groups <= 128 and groups % 4 == 0 and groups >= 16
    if replicas == 2 and w_gate_up.shape[0] == 1 and small:
        return body_by_width(tokens, route_ids, gates, cotangent, w_gate_up, w_down)
    return body_by_slots(tokens, route_ids, gates, cotangent, w_gate_up, w_down)


def solution(mesh):
    placed = (
        P(("expert", "dp"), None),
        P(("expert", "dp"), None),
        P(("expert", "dp"), None),
        P(("expert", "dp"), None),
        P("expert", "dp", None),
        P("expert", "dp", None),
    )
    return jax.shard_map(
        body,
        mesh=mesh,
        in_specs=placed,
        out_specs=(
            P(("expert", "dp"), None),
            P(("expert", "dp"), None),
            P(("expert", "dp"), None),
            P("expert", "dp", None),
            P("expert", "dp", None),
        ),
        check_vma=False,
    )
```

```python
import jax
import jax.numpy as jnp
from jax import lax
from jax.experimental import pallas as pl
from jax.experimental.pallas import tpu as pltpu
from jax.sharding import PartitionSpec as P


def expert_forward(x_rows, weight_in, weight_out, hidden_units):
    pre_act = jnp.dot(x_rows, weight_in, preferred_element_type=jnp.float32)
    gate_pre = pre_act[:, :hidden_units]
    up_pre = pre_act[:, hidden_units:]
    sigmoid_gate = jax.nn.sigmoid(gate_pre)
    activation = gate_pre * sigmoid_gate
    hidden = (activation * up_pre).astype(jnp.bfloat16)
    expert_out = lax.dot_general(
        hidden, weight_out, (((1,), (1,)), ((), ())), preferred_element_type=jnp.float32
    ).astype(jnp.bfloat16)
    return (gate_pre, up_pre, sigmoid_gate, activation, hidden, expert_out)


def expert_backward(saved, grad_rows, weight_in, weight_out):
    gate_pre, up_pre, sigmoid_gate, activation, hidden, expert_out = saved
    hidden_grad = jnp.dot(grad_rows, weight_out, preferred_element_type=jnp.float32)
    gate_grad = (
        hidden_grad * up_pre * (sigmoid_gate * (1.0 + gate_pre * (1.0 - sigmoid_gate)))
    ).astype(jnp.bfloat16)
    up_grad = (hidden_grad * activation).astype(jnp.bfloat16)
    pair_grad = jnp.concatenate([gate_grad, up_grad], axis=1)
    input_grad = lax.dot_general(
        pair_grad, weight_in, (((1,), (1,)), ((), ())), preferred_element_type=jnp.float32
    ).astype(jnp.bfloat16)
    return (pair_grad, input_grad)


def outer_blocks(left, right, pieces):
    span = left.shape[1] // pieces
    results = []
    for piece in range(pieces):
        product = lax.dot_general(
            left[:, piece * span : (piece + 1) * span],
            right,
            (((0,), (0,)), ((), ())),
            preferred_element_type=jnp.float32,
        )
        results.append(product.astype(jnp.bfloat16))
    return jnp.stack(results, axis=0)


def replica_total(received):
    return jnp.sum(received.astype(jnp.float32), axis=0).astype(jnp.bfloat16)


def body_by_slots(tokens, route_ids, gates, cotangent, w_gate_up, w_down):
    tok_dev, model_width = tokens.shape
    top_count = route_ids.shape[1]
    groups = lax.axis_size("expert")
    replicas = lax.axis_size("dp")
    local_experts = w_gate_up.shape[0]
    hidden_units = w_down.shape[2]
    experts = groups * local_experts
    assignments = tok_dev * top_count
    capacity = min(tok_dev, max(2, assignments // experts + max(1, assignments // (3 * experts))))
    flat_ids = route_ids.reshape(assignments)
    onehot = (flat_ids[:, None] == jnp.arange(experts, dtype=jnp.int32)[None, :]).astype(jnp.int32)
    earlier = jnp.sum(
        (jnp.cumsum(onehot, axis=0, dtype=jnp.int32) - onehot) * onehot, axis=1, dtype=jnp.int32
    )
    position = flat_ids * capacity + earlier
    source = (
        jnp.full((experts * capacity,), assignments, jnp.int32)
        .at[position]
        .set(jnp.arange(assignments, dtype=jnp.int32))
    )
    token_row = source // top_count
    tok_pad = jnp.concatenate([tokens, jnp.zeros((1, model_width), jnp.bfloat16)], axis=0)
    cot_pad = jnp.concatenate([cotangent, jnp.zeros((1, model_width), jnp.bfloat16)], axis=0)
    gate_pad = jnp.concatenate([gates.reshape(assignments), jnp.zeros((1,), jnp.float32)], axis=0)
    send_rows = tok_pad[token_row].reshape(experts, capacity, model_width)
    send_grads = (gate_pad[source][:, None] * cot_pad[token_row].astype(jnp.float32)).astype(
        jnp.bfloat16
    )
    send_grads = send_grads.reshape(experts, capacity, model_width)
    weights_in, weights_out = (
        lax.all_gather(w_gate_up, "dp", axis=1, tiled=True),
        lax.all_gather(w_down, "dp", axis=1, tiled=True),
    )
    rows_in, grads_in = (
        lax.all_to_all(send_rows, "expert", split_axis=0, concat_axis=1, tiled=True),
        lax.all_to_all(send_grads, "expert", split_axis=0, concat_axis=1, tiled=True),
    )
    local = 0
    forward_parts = expert_forward(
        rows_in[local], weights_in[local], weights_out[local], hidden_units
    )
    saved_all = [forward_parts]
    out_list = [forward_parts[5]]
    down_list = [outer_blocks(grads_in[local], forward_parts[4], replicas)]
    expert_outs = jnp.stack(out_list, axis=0)
    down_stack = jnp.stack(down_list, axis=1)
    outs_back = lax.all_to_all(expert_outs, "expert", split_axis=1, concat_axis=0, tiled=True)
    local = 0
    pair_grad, input_grad = expert_backward(
        saved_all[local], grads_in[local], weights_in[local], weights_out[local]
    )
    input_list = [input_grad]
    gate_up_list = [outer_blocks(rows_in[local], pair_grad, replicas)]
    input_grads = jnp.stack(input_list, axis=0)
    gate_up_stack = jnp.stack(gate_up_list, axis=1)
    grads_back = lax.all_to_all(input_grads, "expert", split_axis=1, concat_axis=0, tiled=True)
    gate_up_received, down_received = (
        lax.all_to_all(gate_up_stack, "dp", split_axis=0, concat_axis=0, tiled=True),
        lax.all_to_all(down_stack, "dp", split_axis=0, concat_axis=0, tiled=True),
    )
    grad_gate_up = replica_total(gate_up_received)
    grad_down = replica_total(down_received)
    out_rows = outs_back.reshape(experts * capacity, model_width)[position].reshape(
        tok_dev, top_count, model_width
    )
    mixed = jnp.sum(gates[:, :, None] * out_rows.astype(jnp.float32), axis=1).astype(jnp.bfloat16)
    grad_gates = jnp.einsum("td,tkd->tk", cotangent, out_rows, preferred_element_type=jnp.float32)
    back_rows = grads_back.reshape(experts * capacity, model_width)[position].reshape(
        tok_dev, top_count, model_width
    )
    grad_tokens = jnp.sum(back_rows.astype(jnp.float32), axis=1).astype(jnp.bfloat16)
    return (mixed, grad_tokens, grad_gates, grad_gate_up, grad_down)


F32, BF16 = jnp.float32, jnp.bfloat16
LANES = 128
FREE = pl.CostEstimate(flops=0, bytes_accessed=0, transcendentals=0)


def run(kernel, outs, args, scalars=0):
    spaces = [pltpu.SMEM] * scalars + [pltpu.VMEM] * (len(args) - scalars)
    return pl.pallas_call(
        kernel,
        out_shape=outs,
        in_specs=[pl.BlockSpec(memory_space=space) for space in spaces],
        out_specs=[pl.BlockSpec(memory_space=pltpu.VMEM) for _ in outs],
        compiler_params=pltpu.CompilerParams(vmem_limit_bytes=10 * 1024 * 1024),
        cost_estimate=FREE,
    )(*args)


def dot_nn(left, right):
    return jnp.dot(left, right, preferred_element_type=F32)


def dot_nt(left, right):
    return lax.dot_general(left, right, (((1,), (1,)), ((), ())), preferred_element_type=F32)


def own_column(expert, groups):
    lane = lax.broadcasted_iota(jnp.int32, (1, LANES), 1)
    hit = (lane == expert) | (lane == expert + groups) | (lane == expert + 2 * groups)
    return jnp.where(hit, 1.0, 0.0)


def prepare(tokens, route_ids, gates, cotangent, replica, groups):
    rows, width = tokens.shape
    half = width // 2

    def kernel(replica_ref, tok_ref, id_ref, gate_ref, cot_ref, keep_ref, send_ref):
        low = replica_ref[0] == 0
        line = lax.broadcasted_iota(jnp.int32, (LANES, rows), 0)
        term = lax.div(line, groups)
        named = line - term * groups
        dense = jnp.zeros((LANES, rows), F32)
        for k in range(id_ref.shape[0]):
            dense = dense + jnp.where(id_ref[k : k + 1, :] == named, gate_ref[k : k + 1, :], 0.0)
        first = dense.astype(BF16).astype(F32)
        second = (dense - first).astype(BF16).astype(F32)
        third = dense - first - second
        meta = jnp.where(term == 0, first, jnp.where(term == 1, second, jnp.where(term == 2, third, 0.0))).astype(BF16)
        down = lax.broadcasted_iota(jnp.int32, (rows, rows), 0)
        along = lax.broadcasted_iota(jnp.int32, (rows, rows), 1)
        meta = dot_nt(jnp.where(down == along, 1.0, 0.0).astype(BF16), meta).astype(BF16)
        for ref, start in ((tok_ref, 0), (cot_ref, half + LANES)):
            left, right = ref[:, :half], ref[:, half:]
            keep_ref[:, start : start + half] = jnp.where(low, left, right)
            send_ref[:, start : start + half] = jnp.where(low, right, left)
        keep_ref[:, half : half + LANES] = meta
        send_ref[:, half : half + LANES] = meta

    out = jax.ShapeDtypeStruct((rows, width + LANES), BF16)
    args = [tokens, route_ids, gates, cotangent]
    return pl.pallas_call(
        kernel,
        grid=(1,),
        out_shape=[out, out],
        in_specs=[pl.BlockSpec(memory_space=pltpu.SMEM)] + [pl.BlockSpec(arg.shape, lambda i: (0, 0)) for arg in args],
        out_specs=[pl.BlockSpec(out.shape, lambda i: (0, 0))] * 2,
        compiler_params=pltpu.CompilerParams(vmem_limit_bytes=60 * 1024 * 1024),
        cost_estimate=FREE,
    )(replica, *args)


def partial_products(pieces, weight_in, weight_out, expert, groups, tok_dev, capacity):
    counts = [piece.shape[0] // tok_dev * capacity for piece in pieces]
    total, number = sum(counts), len(pieces)
    half, columns = weight_in.shape
    hidden_units = weight_out.shape[1]

    def kernel(expert_ref, *refs):
        rows_refs, refs = refs[:number], refs[number:]
        in_ref, out_ref, x_ref, grad_ref, gate_ref, own_ref, send_ref = refs[:7]
        places = refs[7:]
        column = own_column(expert_ref[0], groups)
        column_rows = jnp.broadcast_to(column, (8, LANES)).astype(BF16)
        start = 0
        for piece in range(number):
            rows, count = rows_refs[piece].shape[0], counts[piece]
            meta = rows_refs[piece][:, half : half + LANES]
            gate_row = dot_nt(column_rows, meta)
            gate_col = jnp.sum(meta.astype(F32) * column, axis=1, keepdims=True)
            down = lax.broadcasted_iota(jnp.int32, (rows, rows), 0)
            along = lax.broadcasted_iota(jnp.int32, (rows, rows), 1)
            first_down, first_along = jnp.zeros_like(down), jnp.zeros_like(along)
            base_down, base_along = jnp.zeros_like(down), jnp.zeros_like(along)
            for device in range(1, rows // tok_dev):
                first_down += jnp.where(down >= device * tok_dev, tok_dev, 0)
                first_along += jnp.where(along >= device * tok_dev, tok_dev, 0)
                base_down += jnp.where(down >= device * tok_dev, capacity, 0)
                base_along += jnp.where(along >= device * tok_dev, capacity, 0)
            lower = jnp.where((along < down) & (along >= first_down), 1.0, 0.0).astype(BF16)
            upper = jnp.where((down < along) & (down >= first_along), 1.0, 0.0).astype(BF16)
            on_row = jnp.where(gate_row > 0.0, 1.0, 0.0)
            on_col = jnp.where(gate_col > 0.0, 1.0, 0.0)
            rank_row = dot_nn(on_row.astype(BF16), upper)
            rank_col = dot_nn(lower, jnp.broadcast_to(on_col, (rows, LANES)).astype(BF16))
            place_row = jnp.where(on_row > 0.0, rank_row + base_along[:8].astype(F32), -1.0)[:1, :]
            place_col = jnp.where(on_col > 0.0, rank_col[:, :1] + base_down[:, :1].astype(F32), -1.0)
            slot_down = lax.broadcasted_iota(jnp.int32, (count, rows), 0).astype(F32)
            slot_along = lax.broadcasted_iota(jnp.int32, (rows, count), 1).astype(F32)
            pick = jnp.where(place_row == slot_down, 1.0, 0.0).astype(BF16)
            places[piece][...] = jnp.where(place_col == slot_along, 1.0, 0.0).astype(BF16)
            picked = dot_nn(pick, rows_refs[piece][...])
            x_ref[start : start + count, :] = picked[:, :half].astype(BF16)
            gate = jnp.sum(picked[:, half : half + LANES] * column, axis=1, keepdims=True)
            gate_ref[start : start + count, :] = jnp.broadcast_to(gate, (count, LANES))
            grad_ref[start : start + count, :] = (gate * picked[:, half + LANES :]).astype(BF16)
            start += count
        for left, right, at in ((x_ref, in_ref, 0), (grad_ref, out_ref, columns)):
            part = dot_nn(left[...], right[...])
            own_ref[:, at : at + part.shape[1]] = part
            part = part.astype(BF16)
            send_ref[: total // 2, at : at + part.shape[1]] = part[total // 2 :]
            send_ref[total // 2 :, at : at + part.shape[1]] = part[: total // 2]

    shape = jax.ShapeDtypeStruct
    outs = [shape((total, half), BF16), shape((total, half), BF16), shape((total, LANES), F32)]
    outs += [shape((total, columns + hidden_units), F32), shape((total, columns + hidden_units), BF16)]
    outs += [shape((piece.shape[0], count), BF16) for piece, count in zip(pieces, counts)]
    got = run(kernel, outs, [expert, *pieces, weight_in, weight_out], 1)
    return (*got[:5], got[5:])


def expert_rows(own, came, gate, places, weight_in, weight_out, expert, groups):
    total = own.shape[0]
    half, columns = weight_in.shape
    hidden_units, number = columns // 2, len(places)

    def kernel(expert_ref, own_ref, came_ref, gate_ref, in_ref, out_ref, *refs):
        put, hidden_ref, pair_ref, flag_ref, outs = refs[:number], *refs[number : number + 3], refs[number + 3 :]
        gate_pre = own_ref[:, :hidden_units] + came_ref[:, :hidden_units].astype(F32)
        up_pre = own_ref[:, hidden_units:columns] + came_ref[:, hidden_units:columns].astype(F32)
        hidden_grad = own_ref[:, columns:] + came_ref[:, columns:].astype(F32)
        sig = jax.nn.sigmoid(gate_pre)
        act = gate_pre * sig
        hidden = (act * up_pre).astype(BF16)
        hidden_ref[...] = hidden
        pair_ref[:, :hidden_units] = (hidden_grad * up_pre * (sig * (1.0 + gate_pre * (1.0 - sig)))).astype(BF16)
        pair_ref[:, hidden_units:] = (hidden_grad * act).astype(BF16)
        gate = gate_ref[...]
        flag_ref[...] = gate[:8]
        score = jnp.sum(hidden.astype(F32) * hidden_grad, axis=1, keepdims=True)
        score = score / jnp.where(gate > 0.0, gate, 1.0)
        first = score.astype(BF16).astype(F32)
        lane = lax.broadcasted_iota(jnp.int32, (total, LANES), 1)
        expert = expert_ref[0]
        score = jnp.where(lane == expert, first, jnp.where(lane == expert + groups, score - first, 0.0)).astype(BF16)
        forth = (gate[:, :1] * dot_nt(hidden, out_ref[...])).astype(BF16)
        back = dot_nt(pair_ref[...], in_ref[...]).astype(BF16)
        start = 0
        for piece in range(number):
            count = put[piece].shape[1]
            place = put[piece][...]
            for rows, at in ((forth, 0), (back, half), (score, 2 * half)):
                rows = rows[start : start + count, :]
                outs[piece][:, at : at + rows.shape[1]] = dot_nn(place, rows).astype(BF16)
            start += count

    shape = jax.ShapeDtypeStruct
    outs = [shape((total, hidden_units), BF16), shape((total, columns), BF16), shape((8, LANES), F32)]
    outs += [shape((place.shape[0], 2 * half + LANES), BF16) for place in places]
    got = run(kernel, outs, [expert, own, came, gate, weight_in, weight_out, *places], 1)
    return got[0], got[1], got[2], got[3:]


def ring_pairs(groups):
    chips = groups // 2
    levels = chips // 2
    order = [2 * z for z in range(levels)] + [2 * z + 1 for z in reversed(range(levels))]
    forward = []
    for place in range(chips):
        forward.append((2 * order[place], 2 * order[(place + 1) % chips]))
        forward.append((2 * order[(place + 1) % chips] + 1, 2 * order[place] + 1))
    backward = [(to, source) for source, to in forward]
    cores = [(index, index ^ 1) for index in range(groups)]
    return forward, backward, cores


def swap_pair(value):
    return lax.ppermute(value, "dp", [(0, 1), (1, 0)])


def swap_both(value):
    groups = lax.axis_size("expert")
    pairs = [(2 * e + r, 2 * (e ^ 1) + 1 - r) for e in range(groups) for r in range(2)]
    return lax.ppermute(value, ("expert", "dp"), pairs)


def by_replica(own, other, replica):
    return jnp.where(replica == 0, jnp.stack([own, other]), jnp.stack([other, own]))


def after(value, *anchors):
    anywhere = pl.BlockSpec(memory_space=pl.ANY)
    return pl.pallas_call(
        lambda *refs: None,
        out_shape=jax.ShapeDtypeStruct(value.shape, value.dtype),
        in_specs=[anywhere] * (1 + len(anchors)),
        out_specs=anywhere,
        input_output_aliases={0: 0},
        compiler_params=pltpu.CompilerParams(vmem_limit_bytes=1024 * 1024),
        cost_estimate=FREE,
    )(value, *anchors)


class Order:
    def __init__(self):
        self.last = None

    def __call__(self, value, *anchors):
        if self.last is not None:
            value = after(value, self.last, *anchors)
        self.last = value
        return value


def body_by_width(tokens, route_ids, gates, cotangent, w_gate_up, w_down):
    tok_dev, model_width = tokens.shape
    top_count = route_ids.shape[1]
    groups = lax.axis_size("expert")
    replica = lax.axis_index("dp")
    expert = lax.axis_index("expert").astype(jnp.int32).reshape(1)
    half = w_gate_up.shape[1]
    capacity = slot_capacity(tok_dev, top_count, groups)
    steps = groups // 4
    weight_in, weight_out = w_gate_up[0], w_down[0]
    forward, backward, cores = ring_pairs(groups)
    unit = 2 * tok_dev

    def swap_cores(value):
        return lax.ppermute(value, "expert", cores)

    def products(pieces):
        *kept, own, send, places = partial_products(
            pieces, weight_in, weight_out, expert, groups, tok_dev, capacity
        )
        return [kept, own, send, places, swap_pair(send)]

    def ring(block, step):
        return lax.ppermute(block if step < steps else block[:tok_dev], "expert", forward)

    order = Order()
    keep, send = prepare(tokens, route_ids.T, gates.T, cotangent, replica.astype(jnp.int32).reshape(1), groups)
    second = jnp.concatenate([order(swap_pair(send)), order(swap_both(send))], axis=0)
    first = jnp.concatenate([keep, order(swap_cores(keep))], axis=0)
    chunks, pieces = [], ([first], [second])

    def wait_for(number):
        chunks[number][4] = order(chunks[number][4], chunks[-1][0][2])

    for step in range(1, steps + 1):
        if step == steps:
            wait_for(step - 3)
        first = order(ring(first, step), *(chunk[0][2] for chunk in chunks[-1:]))
        if 3 <= step < steps:
            wait_for(step - 3)
        second = order(ring(second, step))
        pieces[0].extend([first, swap_cores(first)])
        pieces[1].extend([second, order(swap_cores(second))])
        chunks.append(products(pieces[0] + pieces[1]))
        pieces = ([], [])

    terms, grads = ([], []), []
    for number, ((x_rows, grad_rows, gate), own, _, places, came) in enumerate(chunks):
        if number == steps - 1:
            came = order(came)
        elif number == steps - 2:
            came = order(came, flag, chunks[-1][0][2])
        elif number:
            came = after(came, flag, chunks[-1][0][2])
        hidden, pair_grad, flag, out = expert_rows(own, came, gate, places, weight_in, weight_out, expert, groups)
        for stream in (1, 0):
            *own_terms, mine, other = out[stream * len(out) // 2 :][: len(out) // 2]
            terms[stream].extend([(term, None) for term in own_terms] + [(mine, other)])
        grads.append((x_rows, pair_grad, grad_rows, hidden))

    def pop_term(stream, arrived):
        mine, other = terms[stream].pop()
        if other is None:
            return mine.astype(F32)
        if arrived is not None:
            other = after(other, arrived)
        came_over.append(swap_cores(other))
        return mine.astype(F32) + came_over[-1].astype(F32)

    came_over = []
    totals, arrived = [pop_term(0, None), pop_term(1, None)], [[None, came_over[0]], [None, came_over[1]]]
    for step in reversed(range(steps)):
        for stream in (1, 0):
            came = lax.ppermute(totals[stream].astype(BF16), "expert", backward)
            if step == steps - 3 and stream == 0:
                came = after(came, grad_gate_up, grad_down)
            if step == steps - 2 and stream == 1:
                grads[0] = tuple(after(array, came) for array in grads[0])
                grad_gate_up, grad_down = outer_products(grads, 0, 1), outer_products(grads, 2, 3)
            base = pop_term(stream, arrived[stream].pop(0))
            arrived[stream].append(came)
            if came.shape[0] < unit:
                totals[stream] = jnp.concatenate([base[:tok_dev] + came.astype(F32), base[tok_dev:]], axis=0)
            else:
                totals[stream] = base + came.astype(F32)

    there = totals[1][:, : 2 * half].astype(BF16)
    kept = totals[0][:tok_dev], swap_cores(totals[0][tok_dev:].astype(BF16))
    scores = kept[0][:, 2 * half :] + kept[1][:, 2 * half :].astype(F32)
    scores = scores[:, :groups] + scores[:, groups : 2 * groups]
    named = route_ids[:, :, None] == jnp.arange(groups, dtype=jnp.int32)[None, None, :]
    grad_gates = jnp.sum(jnp.where(named, scores[:, None, :], 0.0), axis=2)
    other = swap_pair(there[:tok_dev]), after(swap_both(there[tok_dev:]), scores)
    mixed, grad_tokens = join_halves(kept, other, half, replica.astype(jnp.int32).reshape(1))
    return (mixed, grad_tokens, grad_gates, grad_gate_up, grad_down)


def join_halves(kept, other, half, replica):
    rows = kept[0].shape[0]

    def kernel(replica_ref, mine_ref, beside_ref, across_ref, diagonal_ref, *outs):
        low = replica_ref[0] == 0
        for number, out in enumerate(outs):
            at = slice(number * half, (number + 1) * half)
            here = mine_ref[:, at] + beside_ref[:, at].astype(F32)
            there = across_ref[:, at].astype(F32) + diagonal_ref[:, at].astype(F32)
            out[:, :half] = jnp.where(low, here, there).astype(BF16)
            out[:, half:] = jnp.where(low, there, here).astype(BF16)

    out = jax.ShapeDtypeStruct((rows, 2 * half), BF16)
    return run(kernel, [out, out], [replica, *kept, *other], 1)


def outer_products(chunks, left, right):
    left = jnp.concatenate([chunk[left] for chunk in chunks])
    right = jnp.concatenate([chunk[right] for chunk in chunks])
    return lax.dot_general(left, right, (((0,), (0,)), ((), ())), preferred_element_type=F32).astype(BF16)[None]


def slot_capacity(tok_dev, top_count, experts):
    assignments = tok_dev * top_count
    return min(tok_dev, max(2, assignments // experts + max(1, assignments // (3 * experts))))


def body(tokens, route_ids, gates, cotangent, w_gate_up, w_down):
    groups, replicas = lax.axis_size("expert"), lax.axis_size("dp")
    gathered = 2 * groups * tokens.shape[0] * replicas * w_gate_up.shape[1] * 2
    small = gathered <= 8 * 1024 * 1024 and 3 * groups <= 128 and groups % 4 == 0 and groups >= 16
    if replicas == 2 and w_gate_up.shape[0] == 1 and small:
        return body_by_width(tokens, route_ids, gates, cotangent, w_gate_up, w_down)
    return body_by_slots(tokens, route_ids, gates, cotangent, w_gate_up, w_down)


def solution(mesh):
    placed = (
        P(("expert", "dp"), None),
        P(("expert", "dp"), None),
        P(("expert", "dp"), None),
        P(("expert", "dp"), None),
        P("expert", "dp", None),
        P("expert", "dp", None),
    )
    return jax.shard_map(
        body,
        mesh=mesh,
        in_specs=placed,
        out_specs=(
            P(("expert", "dp"), None),
            P(("expert", "dp"), None),
            P(("expert", "dp"), None),
            P("expert", "dp", None),
            P("expert", "dp", None),
        ),
        check_vma=False,
    )
```

```python
import jax
import jax.numpy as jnp
from jax import lax
from jax.experimental import pallas as pl
from jax.experimental.pallas import tpu as pltpu
from jax.sharding import PartitionSpec as P


def expert_forward(x_rows, weight_in, weight_out, hidden_units):
    pre_act = jnp.dot(x_rows, weight_in, preferred_element_type=jnp.float32)
    gate_pre = pre_act[:, :hidden_units]
    up_pre = pre_act[:, hidden_units:]
    sigmoid_gate = jax.nn.sigmoid(gate_pre)
    activation = gate_pre * sigmoid_gate
    hidden = (activation * up_pre).astype(jnp.bfloat16)
    expert_out = lax.dot_general(
        hidden, weight_out, (((1,), (1,)), ((), ())), preferred_element_type=jnp.float32
    ).astype(jnp.bfloat16)
    return (gate_pre, up_pre, sigmoid_gate, activation, hidden, expert_out)


def expert_backward(saved, grad_rows, weight_in, weight_out):
    gate_pre, up_pre, sigmoid_gate, activation, hidden, expert_out = saved
    hidden_grad = jnp.dot(grad_rows, weight_out, preferred_element_type=jnp.float32)
    gate_grad = (
        hidden_grad * up_pre * (sigmoid_gate * (1.0 + gate_pre * (1.0 - sigmoid_gate)))
    ).astype(jnp.bfloat16)
    up_grad = (hidden_grad * activation).astype(jnp.bfloat16)
    pair_grad = jnp.concatenate([gate_grad, up_grad], axis=1)
    input_grad = lax.dot_general(
        pair_grad, weight_in, (((1,), (1,)), ((), ())), preferred_element_type=jnp.float32
    ).astype(jnp.bfloat16)
    return (pair_grad, input_grad)


def outer_blocks(left, right, pieces):
    span = left.shape[1] // pieces
    results = []
    for piece in range(pieces):
        product = lax.dot_general(
            left[:, piece * span : (piece + 1) * span],
            right,
            (((0,), (0,)), ((), ())),
            preferred_element_type=jnp.float32,
        )
        results.append(product.astype(jnp.bfloat16))
    return jnp.stack(results, axis=0)


def replica_total(received):
    return jnp.sum(received.astype(jnp.float32), axis=0).astype(jnp.bfloat16)


def body_by_slots(tokens, route_ids, gates, cotangent, w_gate_up, w_down):
    tok_dev, model_width = tokens.shape
    top_count = route_ids.shape[1]
    groups = lax.axis_size("expert")
    replicas = lax.axis_size("dp")
    local_experts = w_gate_up.shape[0]
    hidden_units = w_down.shape[2]
    experts = groups * local_experts
    assignments = tok_dev * top_count
    capacity = min(tok_dev, max(2, assignments // experts + max(1, assignments // (3 * experts))))
    flat_ids = route_ids.reshape(assignments)
    onehot = (flat_ids[:, None] == jnp.arange(experts, dtype=jnp.int32)[None, :]).astype(jnp.int32)
    earlier = jnp.sum(
        (jnp.cumsum(onehot, axis=0, dtype=jnp.int32) - onehot) * onehot, axis=1, dtype=jnp.int32
    )
    position = flat_ids * capacity + earlier
    source = (
        jnp.full((experts * capacity,), assignments, jnp.int32)
        .at[position]
        .set(jnp.arange(assignments, dtype=jnp.int32))
    )
    token_row = source // top_count
    tok_pad = jnp.concatenate([tokens, jnp.zeros((1, model_width), jnp.bfloat16)], axis=0)
    cot_pad = jnp.concatenate([cotangent, jnp.zeros((1, model_width), jnp.bfloat16)], axis=0)
    gate_pad = jnp.concatenate([gates.reshape(assignments), jnp.zeros((1,), jnp.float32)], axis=0)
    send_rows = tok_pad[token_row].reshape(experts, capacity, model_width)
    send_grads = (gate_pad[source][:, None] * cot_pad[token_row].astype(jnp.float32)).astype(
        jnp.bfloat16
    )
    send_grads = send_grads.reshape(experts, capacity, model_width)
    weights_in, weights_out = (
        lax.all_gather(w_gate_up, "dp", axis=1, tiled=True),
        lax.all_gather(w_down, "dp", axis=1, tiled=True),
    )
    rows_in, grads_in = (
        lax.all_to_all(send_rows, "expert", split_axis=0, concat_axis=1, tiled=True),
        lax.all_to_all(send_grads, "expert", split_axis=0, concat_axis=1, tiled=True),
    )
    local = 0
    forward_parts = expert_forward(
        rows_in[local], weights_in[local], weights_out[local], hidden_units
    )
    saved_all = [forward_parts]
    out_list = [forward_parts[5]]
    down_list = [outer_blocks(grads_in[local], forward_parts[4], replicas)]
    expert_outs = jnp.stack(out_list, axis=0)
    down_stack = jnp.stack(down_list, axis=1)
    outs_back = lax.all_to_all(expert_outs, "expert", split_axis=1, concat_axis=0, tiled=True)
    local = 0
    pair_grad, input_grad = expert_backward(
        saved_all[local], grads_in[local], weights_in[local], weights_out[local]
    )
    input_list = [input_grad]
    gate_up_list = [outer_blocks(rows_in[local], pair_grad, replicas)]
    input_grads = jnp.stack(input_list, axis=0)
    gate_up_stack = jnp.stack(gate_up_list, axis=1)
    grads_back = lax.all_to_all(input_grads, "expert", split_axis=1, concat_axis=0, tiled=True)
    gate_up_received, down_received = (
        lax.all_to_all(gate_up_stack, "dp", split_axis=0, concat_axis=0, tiled=True),
        lax.all_to_all(down_stack, "dp", split_axis=0, concat_axis=0, tiled=True),
    )
    grad_gate_up = replica_total(gate_up_received)
    grad_down = replica_total(down_received)
    out_rows = outs_back.reshape(experts * capacity, model_width)[position].reshape(
        tok_dev, top_count, model_width
    )
    mixed = jnp.sum(gates[:, :, None] * out_rows.astype(jnp.float32), axis=1).astype(jnp.bfloat16)
    grad_gates = jnp.einsum("td,tkd->tk", cotangent, out_rows, preferred_element_type=jnp.float32)
    back_rows = grads_back.reshape(experts * capacity, model_width)[position].reshape(
        tok_dev, top_count, model_width
    )
    grad_tokens = jnp.sum(back_rows.astype(jnp.float32), axis=1).astype(jnp.bfloat16)
    return (mixed, grad_tokens, grad_gates, grad_gate_up, grad_down)


F32, BF16 = jnp.float32, jnp.bfloat16
LANES = 128
FREE = pl.CostEstimate(flops=0, bytes_accessed=0, transcendentals=0)


def run(kernel, outs, args, scalars=0):
    spaces = [pltpu.SMEM] * scalars + [pltpu.VMEM] * (len(args) - scalars)
    return pl.pallas_call(
        kernel,
        out_shape=outs,
        in_specs=[pl.BlockSpec(memory_space=space) for space in spaces],
        out_specs=[pl.BlockSpec(memory_space=pltpu.VMEM) for _ in outs],
        compiler_params=pltpu.CompilerParams(vmem_limit_bytes=10 * 1024 * 1024),
        cost_estimate=FREE,
    )(*args)


def dot_nn(left, right):
    return jnp.dot(left, right, preferred_element_type=F32)


def dot_nt(left, right):
    return lax.dot_general(left, right, (((1,), (1,)), ((), ())), preferred_element_type=F32)


def own_column(expert, groups):
    lane = lax.broadcasted_iota(jnp.int32, (1, LANES), 1)
    hit = (lane == expert) | (lane == expert + groups) | (lane == expert + 2 * groups)
    return jnp.where(hit, 1.0, 0.0)


def prepare(tokens, route_ids, gates, cotangent, replica, groups):
    rows, width = tokens.shape
    half = width // 2

    def kernel(replica_ref, tok_ref, id_ref, gate_ref, cot_ref, keep_ref, send_ref):
        low = replica_ref[0] == 0
        line = lax.broadcasted_iota(jnp.int32, (LANES, rows), 0)
        term = lax.div(line, groups)
        named = line - term * groups
        dense = jnp.zeros((LANES, rows), F32)
        for k in range(id_ref.shape[0]):
            dense = dense + jnp.where(id_ref[k : k + 1, :] == named, gate_ref[k : k + 1, :], 0.0)
        first = dense.astype(BF16).astype(F32)
        second = (dense - first).astype(BF16).astype(F32)
        third = dense - first - second
        meta = jnp.where(term == 0, first, jnp.where(term == 1, second, jnp.where(term == 2, third, 0.0))).astype(BF16)
        down = lax.broadcasted_iota(jnp.int32, (rows, rows), 0)
        along = lax.broadcasted_iota(jnp.int32, (rows, rows), 1)
        meta = dot_nt(jnp.where(down == along, 1.0, 0.0).astype(BF16), meta).astype(BF16)
        for ref, start in ((tok_ref, 0), (cot_ref, half + LANES)):
            left, right = ref[:, :half], ref[:, half:]
            keep_ref[:, start : start + half] = jnp.where(low, left, right)
            send_ref[:, start : start + half] = jnp.where(low, right, left)
        keep_ref[:, half : half + LANES] = meta
        send_ref[:, half : half + LANES] = meta

    out = jax.ShapeDtypeStruct((rows, width + LANES), BF16)
    args = [tokens, route_ids, gates, cotangent]
    return pl.pallas_call(
        kernel,
        grid=(1,),
        out_shape=[out, out],
        in_specs=[pl.BlockSpec(memory_space=pltpu.SMEM)] + [pl.BlockSpec(arg.shape, lambda i: (0, 0)) for arg in args],
        out_specs=[pl.BlockSpec(out.shape, lambda i: (0, 0))] * 2,
        compiler_params=pltpu.CompilerParams(vmem_limit_bytes=60 * 1024 * 1024),
        cost_estimate=FREE,
    )(replica, *args)


def partial_products(pieces, weight_in, weight_out, expert, groups, tok_dev, capacity):
    counts = [piece.shape[0] // tok_dev * capacity for piece in pieces]
    total, number = sum(counts), len(pieces)
    half, columns = weight_in.shape
    hidden_units = weight_out.shape[1]

    def kernel(expert_ref, *refs):
        rows_refs, refs = refs[:number], refs[number:]
        in_ref, out_ref, x_ref, grad_ref, gate_ref, own_ref, send_ref = refs[:7]
        places = refs[7:]
        column = own_column(expert_ref[0], groups)
        column_rows = jnp.broadcast_to(column, (8, LANES)).astype(BF16)
        start = 0
        for piece in range(number):
            rows, count = rows_refs[piece].shape[0], counts[piece]
            meta = rows_refs[piece][:, half : half + LANES]
            gate_row = dot_nt(column_rows, meta)
            gate_col = jnp.sum(meta.astype(F32) * column, axis=1, keepdims=True)
            down = lax.broadcasted_iota(jnp.int32, (rows, rows), 0)
            along = lax.broadcasted_iota(jnp.int32, (rows, rows), 1)
            first_down, first_along = jnp.zeros_like(down), jnp.zeros_like(along)
            base_down, base_along = jnp.zeros_like(down), jnp.zeros_like(along)
            for device in range(1, rows // tok_dev):
                first_down += jnp.where(down >= device * tok_dev, tok_dev, 0)
                first_along += jnp.where(along >= device * tok_dev, tok_dev, 0)
                base_down += jnp.where(down >= device * tok_dev, capacity, 0)
                base_along += jnp.where(along >= device * tok_dev, capacity, 0)
            lower = jnp.where((along < down) & (along >= first_down), 1.0, 0.0).astype(BF16)
            upper = jnp.where((down < along) & (down >= first_along), 1.0, 0.0).astype(BF16)
            on_row = jnp.where(gate_row > 0.0, 1.0, 0.0)
            on_col = jnp.where(gate_col > 0.0, 1.0, 0.0)
            rank_row = dot_nn(on_row.astype(BF16), upper)
            rank_col = dot_nn(lower, jnp.broadcast_to(on_col, (rows, LANES)).astype(BF16))
            place_row = jnp.where(on_row > 0.0, rank_row + base_along[:8].astype(F32), -1.0)[:1, :]
            place_col = jnp.where(on_col > 0.0, rank_col[:, :1] + base_down[:, :1].astype(F32), -1.0)
            slot_down = lax.broadcasted_iota(jnp.int32, (count, rows), 0).astype(F32)
            slot_along = lax.broadcasted_iota(jnp.int32, (rows, count), 1).astype(F32)
            pick = jnp.where(place_row == slot_down, 1.0, 0.0).astype(BF16)
            places[piece][...] = jnp.where(place_col == slot_along, 1.0, 0.0).astype(BF16)
            picked = dot_nn(pick, rows_refs[piece][...])
            x_ref[start : start + count, :] = picked[:, :half].astype(BF16)
            gate = jnp.sum(picked[:, half : half + LANES] * column, axis=1, keepdims=True)
            gate_ref[start : start + count, :] = jnp.broadcast_to(gate, (count, LANES))
            grad_ref[start : start + count, :] = (gate * picked[:, half + LANES :]).astype(BF16)
            start += count
        for left, right, at in ((x_ref, in_ref, 0), (grad_ref, out_ref, columns)):
            part = dot_nn(left[...], right[...])
            own_ref[:, at : at + part.shape[1]] = part
            part = part.astype(BF16)
            send_ref[: total // 2, at : at + part.shape[1]] = part[total // 2 :]
            send_ref[total // 2 :, at : at + part.shape[1]] = part[: total // 2]

    shape = jax.ShapeDtypeStruct
    outs = [shape((total, half), BF16), shape((total, half), BF16), shape((total, LANES), F32)]
    outs += [shape((total, columns + hidden_units), F32), shape((total, columns + hidden_units), BF16)]
    outs += [shape((piece.shape[0], count), BF16) for piece, count in zip(pieces, counts)]
    got = run(kernel, outs, [expert, *pieces, weight_in, weight_out], 1)
    return (*got[:5], got[5:])


def expert_rows(own, came, gate, places, weight_in, weight_out, expert, groups):
    total = own.shape[0]
    half, columns = weight_in.shape
    hidden_units, number = columns // 2, len(places)

    def kernel(expert_ref, own_ref, came_ref, gate_ref, in_ref, out_ref, *refs):
        put, hidden_ref, pair_ref, flag_ref, outs = refs[:number], *refs[number : number + 3], refs[number + 3 :]
        gate_pre = own_ref[:, :hidden_units] + came_ref[:, :hidden_units].astype(F32)
        up_pre = own_ref[:, hidden_units:columns] + came_ref[:, hidden_units:columns].astype(F32)
        hidden_grad = own_ref[:, columns:] + came_ref[:, columns:].astype(F32)
        sig = jax.nn.sigmoid(gate_pre)
        act = gate_pre * sig
        hidden = (act * up_pre).astype(BF16)
        hidden_ref[...] = hidden
        pair_ref[:, :hidden_units] = (hidden_grad * up_pre * (sig * (1.0 + gate_pre * (1.0 - sig)))).astype(BF16)
        pair_ref[:, hidden_units:] = (hidden_grad * act).astype(BF16)
        gate = gate_ref[...]
        flag_ref[...] = gate[:8]
        score = jnp.sum(hidden.astype(F32) * hidden_grad, axis=1, keepdims=True)
        score = score / jnp.where(gate > 0.0, gate, 1.0)
        first = score.astype(BF16).astype(F32)
        lane = lax.broadcasted_iota(jnp.int32, (total, LANES), 1)
        expert = expert_ref[0]
        score = jnp.where(lane == expert, first, jnp.where(lane == expert + groups, score - first, 0.0)).astype(BF16)
        forth = (gate[:, :1] * dot_nt(hidden, out_ref[...])).astype(BF16)
        back = dot_nt(pair_ref[...], in_ref[...]).astype(BF16)
        start = 0
        for piece in range(number):
            count = put[piece].shape[1]
            place = put[piece][...]
            for rows, at in ((forth, 0), (back, half), (score, 2 * half)):
                rows = rows[start : start + count, :]
                outs[piece][:, at : at + rows.shape[1]] = dot_nn(place, rows).astype(BF16)
            start += count

    shape = jax.ShapeDtypeStruct
    outs = [shape((total, hidden_units), BF16), shape((total, columns), BF16), shape((8, LANES), F32)]
    outs += [shape((place.shape[0], 2 * half + LANES), BF16) for place in places]
    got = run(kernel, outs, [expert, own, came, gate, weight_in, weight_out, *places], 1)
    return got[0], got[1], got[2], got[3:]


def ring_pairs(groups):
    chips = groups // 2
    levels = chips // 2
    order = [2 * z for z in range(levels)] + [2 * z + 1 for z in reversed(range(levels))]
    forward = []
    for place in range(chips):
        forward.append((2 * order[place], 2 * order[(place + 1) % chips]))
        forward.append((2 * order[(place + 1) % chips] + 1, 2 * order[place] + 1))
    backward = [(to, source) for source, to in forward]
    cores = [(index, index ^ 1) for index in range(groups)]
    return forward, backward, cores


def swap_pair(value):
    return lax.ppermute(value, "dp", [(0, 1), (1, 0)])


def swap_both(value):
    groups = lax.axis_size("expert")
    pairs = [(2 * e + r, 2 * (e ^ 1) + 1 - r) for e in range(groups) for r in range(2)]
    return lax.ppermute(value, ("expert", "dp"), pairs)


def by_replica(own, other, replica):
    return jnp.where(replica == 0, jnp.stack([own, other]), jnp.stack([other, own]))


def after(value, *anchors):
    anywhere = pl.BlockSpec(memory_space=pl.ANY)
    return pl.pallas_call(
        lambda *refs: None,
        out_shape=jax.ShapeDtypeStruct(value.shape, value.dtype),
        in_specs=[anywhere] * (1 + len(anchors)),
        out_specs=anywhere,
        input_output_aliases={0: 0},
        compiler_params=pltpu.CompilerParams(vmem_limit_bytes=1024 * 1024),
        cost_estimate=FREE,
    )(value, *anchors)


class Order:
    def __init__(self):
        self.last = None

    def __call__(self, value, *anchors):
        if self.last is not None:
            value = after(value, self.last, *anchors)
        self.last = value
        return value


def body_by_width(tokens, route_ids, gates, cotangent, w_gate_up, w_down):
    tok_dev, model_width = tokens.shape
    top_count = route_ids.shape[1]
    groups = lax.axis_size("expert")
    replica = lax.axis_index("dp")
    expert = lax.axis_index("expert").astype(jnp.int32).reshape(1)
    half = w_gate_up.shape[1]
    capacity = slot_capacity(tok_dev, top_count, groups)
    steps = groups // 4
    weight_in, weight_out = w_gate_up[0], w_down[0]
    forward, backward, cores = ring_pairs(groups)
    unit = 2 * tok_dev

    def swap_cores(value):
        return lax.ppermute(value, "expert", cores)

    def products(pieces):
        *kept, own, send, places = partial_products(
            pieces, weight_in, weight_out, expert, groups, tok_dev, capacity
        )
        return [kept, own, send, places, swap_pair(send)]

    def ring(block, step):
        return lax.ppermute(block if step < steps else block[:tok_dev], "expert", forward)

    order = Order()
    keep, send = prepare(tokens, route_ids.T, gates.T, cotangent, replica.astype(jnp.int32).reshape(1), groups)
    second = jnp.concatenate([order(swap_pair(send)), order(swap_both(send))], axis=0)
    first = jnp.concatenate([keep, order(swap_cores(keep))], axis=0)
    chunks = [products([first, second])]

    def wait_for(number):
        chunks[number][4] = order(chunks[number][4], chunks[-1][0][2])

    for step in range(1, steps + 1):
        if step == steps:
            wait_for(step - 2)
        first = order(ring(first, step), chunks[-1][0][2])
        if step == 1:
            wait_for(0)
        elif 3 <= step < steps:
            wait_for(step - 2)
        second = order(ring(second, step))
        first_other, second_other = swap_cores(first), order(swap_cores(second))
        chunks.append(products([first, first_other, second, second_other]))

    terms, grads = ([], []), []
    for number, ((x_rows, grad_rows, gate), own, _, places, came) in enumerate(chunks):
        if number == steps:
            came = order(came)
        elif number == steps - 1:
            came = order(came, flag, chunks[-1][0][2])
        elif number == steps - 2:
            came = after(came, flag, chunks[-1][0][2])
        elif number:
            came = after(came, flag)
        hidden, pair_grad, flag, out = expert_rows(own, came, gate, places, weight_in, weight_out, expert, groups)
        for stream in (1, 0):
            mine = out[stream * len(out) // 2 :][: len(out) // 2]
            terms[stream].append((mine[0], mine[1] if number else None))
        grads.append((x_rows, pair_grad, grad_rows, hidden))

    def pop_term(stream, arrived):
        mine, other = terms[stream].pop()
        if other is None:
            return mine.astype(F32)
        if arrived is not None:
            other = after(other, arrived)
        came_over.append(swap_cores(other))
        return mine.astype(F32) + came_over[-1].astype(F32)

    came_over = []
    totals, arrived = [pop_term(0, None), pop_term(1, None)], [[None, came_over[0]], [None, came_over[1]]]
    for step in reversed(range(steps)):
        for stream in (1, 0):
            came = lax.ppermute(totals[stream].astype(BF16), "expert", backward)
            if step == steps - 3 and stream == 0:
                came = after(came, grad_gate_up, grad_down)
            if step == steps - 2 and stream == 1:
                grads[0] = tuple(after(array, came) for array in grads[0])
                grad_gate_up, grad_down = outer_products(grads, 0, 1), outer_products(grads, 2, 3)
            base = pop_term(stream, arrived[stream].pop(0))
            arrived[stream].append(came)
            if came.shape[0] < unit:
                totals[stream] = jnp.concatenate([base[:tok_dev] + came.astype(F32), base[tok_dev:]], axis=0)
            else:
                totals[stream] = base + came.astype(F32)

    there = totals[1][:, : 2 * half].astype(BF16)
    kept = totals[0][:tok_dev], swap_cores(totals[0][tok_dev:].astype(BF16))
    scores = kept[0][:, 2 * half :] + kept[1][:, 2 * half :].astype(F32)
    scores = scores[:, :groups] + scores[:, groups : 2 * groups]
    named = route_ids[:, :, None] == jnp.arange(groups, dtype=jnp.int32)[None, None, :]
    grad_gates = jnp.sum(jnp.where(named, scores[:, None, :], 0.0), axis=2)
    other = swap_pair(there[:tok_dev]), after(swap_both(there[tok_dev:]), scores)
    mixed, grad_tokens = join_halves(kept, other, half, replica.astype(jnp.int32).reshape(1))
    return (mixed, grad_tokens, grad_gates, grad_gate_up, grad_down)


def join_halves(kept, other, half, replica):
    rows = kept[0].shape[0]

    def kernel(replica_ref, mine_ref, beside_ref, across_ref, diagonal_ref, *outs):
        low = replica_ref[0] == 0
        for number, out in enumerate(outs):
            at = slice(number * half, (number + 1) * half)
            here = mine_ref[:, at] + beside_ref[:, at].astype(F32)
            there = across_ref[:, at].astype(F32) + diagonal_ref[:, at].astype(F32)
            out[:, :half] = jnp.where(low, here, there).astype(BF16)
            out[:, half:] = jnp.where(low, there, here).astype(BF16)

    out = jax.ShapeDtypeStruct((rows, 2 * half), BF16)
    return run(kernel, [out, out], [replica, *kept, *other], 1)


def outer_products(chunks, left, right):
    left = jnp.concatenate([chunk[left] for chunk in chunks])
    right = jnp.concatenate([chunk[right] for chunk in chunks])
    return lax.dot_general(left, right, (((0,), (0,)), ((), ())), preferred_element_type=F32).astype(BF16)[None]


def slot_capacity(tok_dev, top_count, experts):
    assignments = tok_dev * top_count
    return min(tok_dev, max(2, assignments // experts + max(1, assignments // (3 * experts))))


def body(tokens, route_ids, gates, cotangent, w_gate_up, w_down):
    groups, replicas = lax.axis_size("expert"), lax.axis_size("dp")
    gathered = 2 * groups * tokens.shape[0] * replicas * w_gate_up.shape[1] * 2
    small = gathered <= 8 * 1024 * 1024 and 3 * groups <= 128 and groups % 4 == 0 and groups >= 16
    if replicas == 2 and w_gate_up.shape[0] == 1 and small:
        return body_by_width(tokens, route_ids, gates, cotangent, w_gate_up, w_down)
    return body_by_slots(tokens, route_ids, gates, cotangent, w_gate_up, w_down)


def solution(mesh):
    placed = (
        P(("expert", "dp"), None),
        P(("expert", "dp"), None),
        P(("expert", "dp"), None),
        P(("expert", "dp"), None),
        P("expert", "dp", None),
        P("expert", "dp", None),
    )
    return jax.shard_map(
        body,
        mesh=mesh,
        in_specs=placed,
        out_specs=(
            P(("expert", "dp"), None),
            P(("expert", "dp"), None),
            P(("expert", "dp"), None),
            P("expert", "dp", None),
            P("expert", "dp", None),
        ),
        check_vma=False,
    )
```

```python
import jax
import jax.numpy as jnp
from jax import lax
from jax.experimental import pallas as pl
from jax.experimental.pallas import tpu as pltpu
from jax.sharding import PartitionSpec as P


def expert_forward(x_rows, weight_in, weight_out, hidden_units):
    pre_act = jnp.dot(x_rows, weight_in, preferred_element_type=jnp.float32)
    gate_pre = pre_act[:, :hidden_units]
    up_pre = pre_act[:, hidden_units:]
    sigmoid_gate = jax.nn.sigmoid(gate_pre)
    activation = gate_pre * sigmoid_gate
    hidden = (activation * up_pre).astype(jnp.bfloat16)
    expert_out = lax.dot_general(
        hidden, weight_out, (((1,), (1,)), ((), ())), preferred_element_type=jnp.float32
    ).astype(jnp.bfloat16)
    return (gate_pre, up_pre, sigmoid_gate, activation, hidden, expert_out)


def expert_backward(saved, grad_rows, weight_in, weight_out):
    gate_pre, up_pre, sigmoid_gate, activation, hidden, expert_out = saved
    hidden_grad = jnp.dot(grad_rows, weight_out, preferred_element_type=jnp.float32)
    gate_grad = (
        hidden_grad * up_pre * (sigmoid_gate * (1.0 + gate_pre * (1.0 - sigmoid_gate)))
    ).astype(jnp.bfloat16)
    up_grad = (hidden_grad * activation).astype(jnp.bfloat16)
    pair_grad = jnp.concatenate([gate_grad, up_grad], axis=1)
    input_grad = lax.dot_general(
        pair_grad, weight_in, (((1,), (1,)), ((), ())), preferred_element_type=jnp.float32
    ).astype(jnp.bfloat16)
    return (pair_grad, input_grad)


def outer_blocks(left, right, pieces):
    span = left.shape[1] // pieces
    results = []
    for piece in range(pieces):
        product = lax.dot_general(
            left[:, piece * span : (piece + 1) * span],
            right,
            (((0,), (0,)), ((), ())),
            preferred_element_type=jnp.float32,
        )
        results.append(product.astype(jnp.bfloat16))
    return jnp.stack(results, axis=0)


def replica_total(received):
    return jnp.sum(received.astype(jnp.float32), axis=0).astype(jnp.bfloat16)


def body_by_slots(tokens, route_ids, gates, cotangent, w_gate_up, w_down):
    tok_dev, model_width = tokens.shape
    top_count = route_ids.shape[1]
    groups = lax.axis_size("expert")
    replicas = lax.axis_size("dp")
    local_experts = w_gate_up.shape[0]
    hidden_units = w_down.shape[2]
    experts = groups * local_experts
    assignments = tok_dev * top_count
    capacity = min(tok_dev, max(2, assignments // experts + max(1, assignments // (3 * experts))))
    flat_ids = route_ids.reshape(assignments)
    onehot = (flat_ids[:, None] == jnp.arange(experts, dtype=jnp.int32)[None, :]).astype(jnp.int32)
    earlier = jnp.sum(
        (jnp.cumsum(onehot, axis=0, dtype=jnp.int32) - onehot) * onehot, axis=1, dtype=jnp.int32
    )
    position = flat_ids * capacity + earlier
    source = (
        jnp.full((experts * capacity,), assignments, jnp.int32)
        .at[position]
        .set(jnp.arange(assignments, dtype=jnp.int32))
    )
    token_row = source // top_count
    tok_pad = jnp.concatenate([tokens, jnp.zeros((1, model_width), jnp.bfloat16)], axis=0)
    cot_pad = jnp.concatenate([cotangent, jnp.zeros((1, model_width), jnp.bfloat16)], axis=0)
    gate_pad = jnp.concatenate([gates.reshape(assignments), jnp.zeros((1,), jnp.float32)], axis=0)
    send_rows = tok_pad[token_row].reshape(experts, capacity, model_width)
    send_grads = (gate_pad[source][:, None] * cot_pad[token_row].astype(jnp.float32)).astype(
        jnp.bfloat16
    )
    send_grads = send_grads.reshape(experts, capacity, model_width)
    weights_in, weights_out = (
        lax.all_gather(w_gate_up, "dp", axis=1, tiled=True),
        lax.all_gather(w_down, "dp", axis=1, tiled=True),
    )
    rows_in, grads_in = (
        lax.all_to_all(send_rows, "expert", split_axis=0, concat_axis=1, tiled=True),
        lax.all_to_all(send_grads, "expert", split_axis=0, concat_axis=1, tiled=True),
    )
    local = 0
    forward_parts = expert_forward(
        rows_in[local], weights_in[local], weights_out[local], hidden_units
    )
    saved_all = [forward_parts]
    out_list = [forward_parts[5]]
    down_list = [outer_blocks(grads_in[local], forward_parts[4], replicas)]
    expert_outs = jnp.stack(out_list, axis=0)
    down_stack = jnp.stack(down_list, axis=1)
    outs_back = lax.all_to_all(expert_outs, "expert", split_axis=1, concat_axis=0, tiled=True)
    local = 0
    pair_grad, input_grad = expert_backward(
        saved_all[local], grads_in[local], weights_in[local], weights_out[local]
    )
    input_list = [input_grad]
    gate_up_list = [outer_blocks(rows_in[local], pair_grad, replicas)]
    input_grads = jnp.stack(input_list, axis=0)
    gate_up_stack = jnp.stack(gate_up_list, axis=1)
    grads_back = lax.all_to_all(input_grads, "expert", split_axis=1, concat_axis=0, tiled=True)
    gate_up_received, down_received = (
        lax.all_to_all(gate_up_stack, "dp", split_axis=0, concat_axis=0, tiled=True),
        lax.all_to_all(down_stack, "dp", split_axis=0, concat_axis=0, tiled=True),
    )
    grad_gate_up = replica_total(gate_up_received)
    grad_down = replica_total(down_received)
    out_rows = outs_back.reshape(experts * capacity, model_width)[position].reshape(
        tok_dev, top_count, model_width
    )
    mixed = jnp.sum(gates[:, :, None] * out_rows.astype(jnp.float32), axis=1).astype(jnp.bfloat16)
    grad_gates = jnp.einsum("td,tkd->tk", cotangent, out_rows, preferred_element_type=jnp.float32)
    back_rows = grads_back.reshape(experts * capacity, model_width)[position].reshape(
        tok_dev, top_count, model_width
    )
    grad_tokens = jnp.sum(back_rows.astype(jnp.float32), axis=1).astype(jnp.bfloat16)
    return (mixed, grad_tokens, grad_gates, grad_gate_up, grad_down)


F32, BF16 = jnp.float32, jnp.bfloat16
LANES = 128
FREE = pl.CostEstimate(flops=0, bytes_accessed=0, transcendentals=0)


def run(kernel, outs, args, scalars=0):
    spaces = [pltpu.SMEM] * scalars + [pltpu.VMEM] * (len(args) - scalars)
    return pl.pallas_call(
        kernel,
        out_shape=outs,
        in_specs=[pl.BlockSpec(memory_space=space) for space in spaces],
        out_specs=[pl.BlockSpec(memory_space=pltpu.VMEM) for _ in outs],
        compiler_params=pltpu.CompilerParams(vmem_limit_bytes=10 * 1024 * 1024),
        cost_estimate=FREE,
    )(*args)


def dot_nn(left, right):
    return jnp.dot(left, right, preferred_element_type=F32)


def dot_nt(left, right):
    return lax.dot_general(left, right, (((1,), (1,)), ((), ())), preferred_element_type=F32)


def own_column(expert, groups):
    lane = lax.broadcasted_iota(jnp.int32, (1, LANES), 1)
    hit = (lane == expert) | (lane == expert + groups) | (lane == expert + 2 * groups)
    return jnp.where(hit, 1.0, 0.0)


def prepare(tokens, route_ids, gates, cotangent, replica, groups):
    rows, width = tokens.shape
    half = width // 2

    def kernel(replica_ref, tok_ref, id_ref, gate_ref, cot_ref, keep_ref, send_ref):
        low = replica_ref[0] == 0
        line = lax.broadcasted_iota(jnp.int32, (LANES, rows), 0)
        term = lax.div(line, groups)
        named = line - term * groups
        dense = jnp.zeros((LANES, rows), F32)
        for k in range(id_ref.shape[0]):
            dense = dense + jnp.where(id_ref[k : k + 1, :] == named, gate_ref[k : k + 1, :], 0.0)
        first = dense.astype(BF16).astype(F32)
        second = (dense - first).astype(BF16).astype(F32)
        third = dense - first - second
        meta = jnp.where(term == 0, first, jnp.where(term == 1, second, jnp.where(term == 2, third, 0.0))).astype(BF16)
        down = lax.broadcasted_iota(jnp.int32, (rows, rows), 0)
        along = lax.broadcasted_iota(jnp.int32, (rows, rows), 1)
        meta = dot_nt(jnp.where(down == along, 1.0, 0.0).astype(BF16), meta).astype(BF16)
        for ref, start in ((tok_ref, 0), (cot_ref, half + LANES)):
            left, right = ref[:, :half], ref[:, half:]
            keep_ref[:, start : start + half] = jnp.where(low, left, right)
            send_ref[:, start : start + half] = jnp.where(low, right, left)
        keep_ref[:, half : half + LANES] = meta
        send_ref[:, half : half + LANES] = meta

    out = jax.ShapeDtypeStruct((rows, width + LANES), BF16)
    args = [tokens, route_ids, gates, cotangent]
    return pl.pallas_call(
        kernel,
        grid=(1,),
        out_shape=[out, out],
        in_specs=[pl.BlockSpec(memory_space=pltpu.SMEM)] + [pl.BlockSpec(arg.shape, lambda i: (0, 0)) for arg in args],
        out_specs=[pl.BlockSpec(out.shape, lambda i: (0, 0))] * 2,
        compiler_params=pltpu.CompilerParams(vmem_limit_bytes=60 * 1024 * 1024),
        cost_estimate=FREE,
    )(replica, *args)


def partial_products(pieces, weight_in, weight_out, expert, groups, tok_dev, capacity):
    counts = [piece.shape[0] // tok_dev * capacity for piece in pieces]
    total, number = sum(counts), len(pieces)
    half, columns = weight_in.shape
    hidden_units = weight_out.shape[1]

    def kernel(expert_ref, *refs):
        rows_refs, refs = refs[:number], refs[number:]
        in_ref, out_ref, x_ref, grad_ref, gate_ref, own_ref, send_ref = refs[:7]
        places = refs[7:]
        column = own_column(expert_ref[0], groups)
        column_rows = jnp.broadcast_to(column, (8, LANES)).astype(BF16)
        start = 0
        for piece in range(number):
            rows, count = rows_refs[piece].shape[0], counts[piece]
            meta = rows_refs[piece][:, half : half + LANES]
            gate_row = dot_nt(column_rows, meta)
            gate_col = jnp.sum(meta.astype(F32) * column, axis=1, keepdims=True)
            down = lax.broadcasted_iota(jnp.int32, (rows, rows), 0)
            along = lax.broadcasted_iota(jnp.int32, (rows, rows), 1)
            first_down, first_along = jnp.zeros_like(down), jnp.zeros_like(along)
            base_down, base_along = jnp.zeros_like(down), jnp.zeros_like(along)
            for device in range(1, rows // tok_dev):
                first_down += jnp.where(down >= device * tok_dev, tok_dev, 0)
                first_along += jnp.where(along >= device * tok_dev, tok_dev, 0)
                base_down += jnp.where(down >= device * tok_dev, capacity, 0)
                base_along += jnp.where(along >= device * tok_dev, capacity, 0)
            lower = jnp.where((along < down) & (along >= first_down), 1.0, 0.0).astype(BF16)
            upper = jnp.where((down < along) & (down >= first_along), 1.0, 0.0).astype(BF16)
            on_row = jnp.where(gate_row > 0.0, 1.0, 0.0)
            on_col = jnp.where(gate_col > 0.0, 1.0, 0.0)
            rank_row = dot_nn(on_row.astype(BF16), upper)
            rank_col = dot_nn(lower, jnp.broadcast_to(on_col, (rows, LANES)).astype(BF16))
            place_row = jnp.where(on_row > 0.0, rank_row + base_along[:8].astype(F32), -1.0)[:1, :]
            place_col = jnp.where(on_col > 0.0, rank_col[:, :1] + base_down[:, :1].astype(F32), -1.0)
            slot_down = lax.broadcasted_iota(jnp.int32, (count, rows), 0).astype(F32)
            slot_along = lax.broadcasted_iota(jnp.int32, (rows, count), 1).astype(F32)
            pick = jnp.where(place_row == slot_down, 1.0, 0.0).astype(BF16)
            places[piece][...] = jnp.where(place_col == slot_along, 1.0, 0.0).astype(BF16)
            picked = dot_nn(pick, rows_refs[piece][...])
            x_ref[start : start + count, :] = picked[:, :half].astype(BF16)
            gate = jnp.sum(picked[:, half : half + LANES] * column, axis=1, keepdims=True)
            gate_ref[start : start + count, :] = jnp.broadcast_to(gate, (count, LANES))
            grad_ref[start : start + count, :] = (gate * picked[:, half + LANES :]).astype(BF16)
            start += count
        for left, right, at in ((x_ref, in_ref, 0), (grad_ref, out_ref, columns)):
            part = dot_nn(left[...], right[...])
            own_ref[:, at : at + part.shape[1]] = part
            part = part.astype(BF16)
            send_ref[: total // 2, at : at + part.shape[1]] = part[total // 2 :]
            send_ref[total // 2 :, at : at + part.shape[1]] = part[: total // 2]

    shape = jax.ShapeDtypeStruct
    outs = [shape((total, half), BF16), shape((total, half), BF16), shape((total, LANES), F32)]
    outs += [shape((total, columns + hidden_units), F32), shape((total, columns + hidden_units), BF16)]
    outs += [shape((piece.shape[0], count), BF16) for piece, count in zip(pieces, counts)]
    got = run(kernel, outs, [expert, *pieces, weight_in, weight_out], 1)
    return (*got[:5], got[5:])


def expert_rows(own, came, gate, places, weight_in, weight_out, expert, groups):
    total = own.shape[0]
    half, columns = weight_in.shape
    hidden_units, number = columns // 2, len(places)

    def kernel(expert_ref, own_ref, came_ref, gate_ref, in_ref, out_ref, *refs):
        put, hidden_ref, pair_ref, flag_ref, outs = refs[:number], *refs[number : number + 3], refs[number + 3 :]
        gate_pre = own_ref[:, :hidden_units] + came_ref[:, :hidden_units].astype(F32)
        up_pre = own_ref[:, hidden_units:columns] + came_ref[:, hidden_units:columns].astype(F32)
        hidden_grad = own_ref[:, columns:] + came_ref[:, columns:].astype(F32)
        sig = jax.nn.sigmoid(gate_pre)
        act = gate_pre * sig
        hidden = (act * up_pre).astype(BF16)
        hidden_ref[...] = hidden
        pair_ref[:, :hidden_units] = (hidden_grad * up_pre * (sig * (1.0 + gate_pre * (1.0 - sig)))).astype(BF16)
        pair_ref[:, hidden_units:] = (hidden_grad * act).astype(BF16)
        gate = gate_ref[...]
        flag_ref[...] = gate[:8]
        score = jnp.sum(hidden.astype(F32) * hidden_grad, axis=1, keepdims=True)
        score = score / jnp.where(gate > 0.0, gate, 1.0)
        first = score.astype(BF16).astype(F32)
        lane = lax.broadcasted_iota(jnp.int32, (total, LANES), 1)
        expert = expert_ref[0]
        score = jnp.where(lane == expert, first, jnp.where(lane == expert + groups, score - first, 0.0)).astype(BF16)
        forth = (gate[:, :1] * dot_nt(hidden, out_ref[...])).astype(BF16)
        back = dot_nt(pair_ref[...], in_ref[...]).astype(BF16)
        start = 0
        for piece in range(number):
            count = put[piece].shape[1]
            place = put[piece][...]
            for rows, at in ((forth, 0), (back, half), (score, 2 * half)):
                rows = rows[start : start + count, :]
                outs[piece][:, at : at + rows.shape[1]] = dot_nn(place, rows).astype(BF16)
            start += count

    shape = jax.ShapeDtypeStruct
    outs = [shape((total, hidden_units), BF16), shape((total, columns), BF16), shape((8, LANES), F32)]
    outs += [shape((place.shape[0], 2 * half + LANES), BF16) for place in places]
    got = run(kernel, outs, [expert, own, came, gate, weight_in, weight_out, *places], 1)
    return got[0], got[1], got[2], got[3:]


def ring_pairs(groups):
    chips = groups // 2
    levels = chips // 2
    order = [2 * z for z in range(levels)] + [2 * z + 1 for z in reversed(range(levels))]
    forward = []
    for place in range(chips):
        forward.append((2 * order[place], 2 * order[(place + 1) % chips]))
        forward.append((2 * order[(place + 1) % chips] + 1, 2 * order[place] + 1))
    backward = [(to, source) for source, to in forward]
    cores = [(index, index ^ 1) for index in range(groups)]
    return forward, backward, cores


def swap_pair(value):
    return lax.ppermute(value, "dp", [(0, 1), (1, 0)])


def swap_both(value):
    groups = lax.axis_size("expert")
    pairs = [(2 * e + r, 2 * (e ^ 1) + 1 - r) for e in range(groups) for r in range(2)]
    return lax.ppermute(value, ("expert", "dp"), pairs)


def by_replica(own, other, replica):
    return jnp.where(replica == 0, jnp.stack([own, other]), jnp.stack([other, own]))


def after(value, *anchors):
    anywhere = pl.BlockSpec(memory_space=pl.ANY)
    return pl.pallas_call(
        lambda *refs: None,
        out_shape=jax.ShapeDtypeStruct(value.shape, value.dtype),
        in_specs=[anywhere] * (1 + len(anchors)),
        out_specs=anywhere,
        input_output_aliases={0: 0},
        compiler_params=pltpu.CompilerParams(vmem_limit_bytes=1024 * 1024),
        cost_estimate=FREE,
    )(value, *anchors)


class Order:
    def __init__(self):
        self.last = None

    def __call__(self, value, *anchors):
        if self.last is not None:
            value = after(value, self.last, *anchors)
        self.last = value
        return value


def body_by_width(tokens, route_ids, gates, cotangent, w_gate_up, w_down):
    tok_dev, model_width = tokens.shape
    top_count = route_ids.shape[1]
    groups = lax.axis_size("expert")
    replica = lax.axis_index("dp")
    expert = lax.axis_index("expert").astype(jnp.int32).reshape(1)
    half = w_gate_up.shape[1]
    capacity = slot_capacity(tok_dev, top_count, groups)
    steps = groups // 4
    weight_in, weight_out = w_gate_up[0], w_down[0]
    forward, backward, cores = ring_pairs(groups)
    unit = 2 * tok_dev

    def swap_cores(value):
        return lax.ppermute(value, "expert", cores)

    def products(pieces):
        *kept, own, send, places = partial_products(
            pieces, weight_in, weight_out, expert, groups, tok_dev, capacity
        )
        return [kept, own, send, places, swap_pair(send)]

    def ring(block, step):
        return lax.ppermute(block if step < steps else block[:tok_dev], "expert", forward)

    order = Order()
    keep, send = prepare(tokens, route_ids.T, gates.T, cotangent, replica.astype(jnp.int32).reshape(1), groups)
    second = jnp.concatenate([order(swap_pair(send)), order(swap_both(send))], axis=0)
    first = jnp.concatenate([keep, order(swap_cores(keep))], axis=0)
    chunks = [products([first, second])]

    def wait_for(number):
        chunks[number][4] = order(chunks[number][4], chunks[-1][0][2])

    first_next = order(ring(first, 1))
    for step in range(1, steps + 1):
        first = first_next
        second = order(ring(second, step), chunks[-1][0][2])
        if step < steps:
            first_next = order(ring(first, step + 1))
        if step != 2:
            wait_for(max(step - 2, 0))
        first_other, second_other = swap_cores(first), order(swap_cores(second))
        chunks.append(products([first, first_other, second, second_other]))

    terms, grads = ([], []), []
    for number, ((x_rows, grad_rows, gate), own, _, places, came) in enumerate(chunks):
        if number == steps:
            came = order(came)
        elif number == steps - 1:
            came = order(came, flag, chunks[-1][0][2])
        elif number == steps - 2:
            came = after(came, flag, chunks[-1][0][2])
        elif number:
            came = after(came, flag)
        hidden, pair_grad, flag, out = expert_rows(own, came, gate, places, weight_in, weight_out, expert, groups)
        for stream in (1, 0):
            mine = out[stream * len(out) // 2 :][: len(out) // 2]
            terms[stream].append((mine[0], mine[1] if number else None))
        grads.append((x_rows, pair_grad, grad_rows, hidden))

    def pop_term(stream, arrived):
        mine, other = terms[stream].pop()
        if other is None:
            return mine.astype(F32)
        if arrived is not None:
            other = after(other, arrived)
        came_over.append(swap_cores(other))
        return mine.astype(F32) + came_over[-1].astype(F32)

    came_over = []
    totals, arrived = [pop_term(0, None), pop_term(1, None)], [[None, came_over[0]], [None, came_over[1]]]
    for step in reversed(range(steps)):
        for stream in (1, 0):
            anchors = (grad_gate_up, grad_down) if step == steps - 3 and stream == 0 else ()
            came = order(lax.ppermute(totals[stream].astype(BF16), "expert", backward), *anchors)
            if step == steps - 2 and stream == 1:
                grads[0] = tuple(after(array, came) for array in grads[0])
                grad_gate_up, grad_down = outer_products(grads, 0, 1), outer_products(grads, 2, 3)
            base = pop_term(stream, arrived[stream].pop(0))
            arrived[stream].append(came)
            if came.shape[0] < unit:
                totals[stream] = jnp.concatenate([base[:tok_dev] + came.astype(F32), base[tok_dev:]], axis=0)
            else:
                totals[stream] = base + came.astype(F32)

    there = totals[1][:, : 2 * half].astype(BF16)
    kept = totals[0][:tok_dev], swap_cores(totals[0][tok_dev:].astype(BF16))
    scores = kept[0][:, 2 * half :] + kept[1][:, 2 * half :].astype(F32)
    scores = scores[:, :groups] + scores[:, groups : 2 * groups]
    named = route_ids[:, :, None] == jnp.arange(groups, dtype=jnp.int32)[None, None, :]
    grad_gates = jnp.sum(jnp.where(named, scores[:, None, :], 0.0), axis=2)
    other = swap_pair(there[:tok_dev]), after(swap_both(there[tok_dev:]), scores)
    mixed, grad_tokens = join_halves(kept, other, half, replica.astype(jnp.int32).reshape(1))
    return (mixed, grad_tokens, grad_gates, grad_gate_up, grad_down)


def join_halves(kept, other, half, replica):
    rows = kept[0].shape[0]

    def kernel(replica_ref, mine_ref, beside_ref, across_ref, diagonal_ref, *outs):
        low = replica_ref[0] == 0
        for number, out in enumerate(outs):
            at = slice(number * half, (number + 1) * half)
            here = mine_ref[:, at] + beside_ref[:, at].astype(F32)
            there = across_ref[:, at].astype(F32) + diagonal_ref[:, at].astype(F32)
            out[:, :half] = jnp.where(low, here, there).astype(BF16)
            out[:, half:] = jnp.where(low, there, here).astype(BF16)

    out = jax.ShapeDtypeStruct((rows, 2 * half), BF16)
    return run(kernel, [out, out], [replica, *kept, *other], 1)


def outer_products(chunks, left, right):
    left = jnp.concatenate([chunk[left] for chunk in chunks])
    right = jnp.concatenate([chunk[right] for chunk in chunks])
    return lax.dot_general(left, right, (((0,), (0,)), ((), ())), preferred_element_type=F32).astype(BF16)[None]


def slot_capacity(tok_dev, top_count, experts):
    assignments = tok_dev * top_count
    return min(tok_dev, max(2, assignments // experts + max(1, assignments // (3 * experts))))


def body(tokens, route_ids, gates, cotangent, w_gate_up, w_down):
    groups, replicas = lax.axis_size("expert"), lax.axis_size("dp")
    gathered = 2 * groups * tokens.shape[0] * replicas * w_gate_up.shape[1] * 2
    small = gathered <= 8 * 1024 * 1024 and 3 * groups <= 128 and groups % 4 == 0 and groups >= 16
    if replicas == 2 and w_gate_up.shape[0] == 1 and small:
        return body_by_width(tokens, route_ids, gates, cotangent, w_gate_up, w_down)
    return body_by_slots(tokens, route_ids, gates, cotangent, w_gate_up, w_down)


def solution(mesh):
    placed = (
        P(("expert", "dp"), None),
        P(("expert", "dp"), None),
        P(("expert", "dp"), None),
        P(("expert", "dp"), None),
        P("expert", "dp", None),
        P("expert", "dp", None),
    )
    return jax.shard_map(
        body,
        mesh=mesh,
        in_specs=placed,
        out_specs=(
            P(("expert", "dp"), None),
            P(("expert", "dp"), None),
            P(("expert", "dp"), None),
            P("expert", "dp", None),
            P("expert", "dp", None),
        ),
        check_vma=False,
    )
```

```python
import jax
import jax.numpy as jnp
from jax import lax
from jax.experimental import pallas as pl
from jax.experimental.pallas import tpu as pltpu
from jax.sharding import PartitionSpec as P


def expert_forward(x_rows, weight_in, weight_out, hidden_units):
    pre_act = jnp.dot(x_rows, weight_in, preferred_element_type=jnp.float32)
    gate_pre = pre_act[:, :hidden_units]
    up_pre = pre_act[:, hidden_units:]
    sigmoid_gate = jax.nn.sigmoid(gate_pre)
    activation = gate_pre * sigmoid_gate
    hidden = (activation * up_pre).astype(jnp.bfloat16)
    expert_out = lax.dot_general(
        hidden, weight_out, (((1,), (1,)), ((), ())), preferred_element_type=jnp.float32
    ).astype(jnp.bfloat16)
    return (gate_pre, up_pre, sigmoid_gate, activation, hidden, expert_out)


def expert_backward(saved, grad_rows, weight_in, weight_out):
    gate_pre, up_pre, sigmoid_gate, activation, hidden, expert_out = saved
    hidden_grad = jnp.dot(grad_rows, weight_out, preferred_element_type=jnp.float32)
    gate_grad = (
        hidden_grad * up_pre * (sigmoid_gate * (1.0 + gate_pre * (1.0 - sigmoid_gate)))
    ).astype(jnp.bfloat16)
    up_grad = (hidden_grad * activation).astype(jnp.bfloat16)
    pair_grad = jnp.concatenate([gate_grad, up_grad], axis=1)
    input_grad = lax.dot_general(
        pair_grad, weight_in, (((1,), (1,)), ((), ())), preferred_element_type=jnp.float32
    ).astype(jnp.bfloat16)
    return (pair_grad, input_grad)


def outer_blocks(left, right, pieces):
    span = left.shape[1] // pieces
    results = []
    for piece in range(pieces):
        product = lax.dot_general(
            left[:, piece * span : (piece + 1) * span],
            right,
            (((0,), (0,)), ((), ())),
            preferred_element_type=jnp.float32,
        )
        results.append(product.astype(jnp.bfloat16))
    return jnp.stack(results, axis=0)


def replica_total(received):
    return jnp.sum(received.astype(jnp.float32), axis=0).astype(jnp.bfloat16)


def body_by_slots(tokens, route_ids, gates, cotangent, w_gate_up, w_down):
    tok_dev, model_width = tokens.shape
    top_count = route_ids.shape[1]
    groups = lax.axis_size("expert")
    replicas = lax.axis_size("dp")
    local_experts = w_gate_up.shape[0]
    hidden_units = w_down.shape[2]
    experts = groups * local_experts
    assignments = tok_dev * top_count
    capacity = min(tok_dev, max(2, assignments // experts + max(1, assignments // (3 * experts))))
    flat_ids = route_ids.reshape(assignments)
    onehot = (flat_ids[:, None] == jnp.arange(experts, dtype=jnp.int32)[None, :]).astype(jnp.int32)
    earlier = jnp.sum(
        (jnp.cumsum(onehot, axis=0, dtype=jnp.int32) - onehot) * onehot, axis=1, dtype=jnp.int32
    )
    position = flat_ids * capacity + earlier
    source = (
        jnp.full((experts * capacity,), assignments, jnp.int32)
        .at[position]
        .set(jnp.arange(assignments, dtype=jnp.int32))
    )
    token_row = source // top_count
    tok_pad = jnp.concatenate([tokens, jnp.zeros((1, model_width), jnp.bfloat16)], axis=0)
    cot_pad = jnp.concatenate([cotangent, jnp.zeros((1, model_width), jnp.bfloat16)], axis=0)
    gate_pad = jnp.concatenate([gates.reshape(assignments), jnp.zeros((1,), jnp.float32)], axis=0)
    send_rows = tok_pad[token_row].reshape(experts, capacity, model_width)
    send_grads = (gate_pad[source][:, None] * cot_pad[token_row].astype(jnp.float32)).astype(
        jnp.bfloat16
    )
    send_grads = send_grads.reshape(experts, capacity, model_width)
    weights_in, weights_out = (
        lax.all_gather(w_gate_up, "dp", axis=1, tiled=True),
        lax.all_gather(w_down, "dp", axis=1, tiled=True),
    )
    rows_in, grads_in = (
        lax.all_to_all(send_rows, "expert", split_axis=0, concat_axis=1, tiled=True),
        lax.all_to_all(send_grads, "expert", split_axis=0, concat_axis=1, tiled=True),
    )
    local = 0
    forward_parts = expert_forward(
        rows_in[local], weights_in[local], weights_out[local], hidden_units
    )
    saved_all = [forward_parts]
    out_list = [forward_parts[5]]
    down_list = [outer_blocks(grads_in[local], forward_parts[4], replicas)]
    expert_outs = jnp.stack(out_list, axis=0)
    down_stack = jnp.stack(down_list, axis=1)
    outs_back = lax.all_to_all(expert_outs, "expert", split_axis=1, concat_axis=0, tiled=True)
    local = 0
    pair_grad, input_grad = expert_backward(
        saved_all[local], grads_in[local], weights_in[local], weights_out[local]
    )
    input_list = [input_grad]
    gate_up_list = [outer_blocks(rows_in[local], pair_grad, replicas)]
    input_grads = jnp.stack(input_list, axis=0)
    gate_up_stack = jnp.stack(gate_up_list, axis=1)
    grads_back = lax.all_to_all(input_grads, "expert", split_axis=1, concat_axis=0, tiled=True)
    gate_up_received, down_received = (
        lax.all_to_all(gate_up_stack, "dp", split_axis=0, concat_axis=0, tiled=True),
        lax.all_to_all(down_stack, "dp", split_axis=0, concat_axis=0, tiled=True),
    )
    grad_gate_up = replica_total(gate_up_received)
    grad_down = replica_total(down_received)
    out_rows = outs_back.reshape(experts * capacity, model_width)[position].reshape(
        tok_dev, top_count, model_width
    )
    mixed = jnp.sum(gates[:, :, None] * out_rows.astype(jnp.float32), axis=1).astype(jnp.bfloat16)
    grad_gates = jnp.einsum("td,tkd->tk", cotangent, out_rows, preferred_element_type=jnp.float32)
    back_rows = grads_back.reshape(experts * capacity, model_width)[position].reshape(
        tok_dev, top_count, model_width
    )
    grad_tokens = jnp.sum(back_rows.astype(jnp.float32), axis=1).astype(jnp.bfloat16)
    return (mixed, grad_tokens, grad_gates, grad_gate_up, grad_down)


F32, BF16 = jnp.float32, jnp.bfloat16
LANES = 128
FREE = pl.CostEstimate(flops=0, bytes_accessed=0, transcendentals=0)


def run(kernel, outs, args, scalars=0):
    spaces = [pltpu.SMEM] * scalars + [pltpu.VMEM] * (len(args) - scalars)
    return pl.pallas_call(
        kernel,
        out_shape=outs,
        in_specs=[pl.BlockSpec(memory_space=space) for space in spaces],
        out_specs=[pl.BlockSpec(memory_space=pltpu.VMEM) for _ in outs],
        compiler_params=pltpu.CompilerParams(vmem_limit_bytes=10 * 1024 * 1024),
        cost_estimate=FREE,
    )(*args)


def dot_nn(left, right):
    return jnp.dot(left, right, preferred_element_type=F32)


def dot_nt(left, right):
    return lax.dot_general(left, right, (((1,), (1,)), ((), ())), preferred_element_type=F32)


def own_column(expert, groups):
    lane = lax.broadcasted_iota(jnp.int32, (1, LANES), 1)
    hit = (lane == expert) | (lane == expert + groups) | (lane == expert + 2 * groups)
    return jnp.where(hit, 1.0, 0.0)


def prepare(tokens, route_ids, gates, cotangent, replica, groups):
    rows, width = tokens.shape
    half = width // 2

    def kernel(replica_ref, tok_ref, id_ref, gate_ref, cot_ref, keep_ref, send_ref):
        low = replica_ref[0] == 0
        line = lax.broadcasted_iota(jnp.int32, (LANES, rows), 0)
        term = lax.div(line, groups)
        named = line - term * groups
        dense = jnp.zeros((LANES, rows), F32)
        for k in range(id_ref.shape[0]):
            dense = dense + jnp.where(id_ref[k : k + 1, :] == named, gate_ref[k : k + 1, :], 0.0)
        first = dense.astype(BF16).astype(F32)
        second = (dense - first).astype(BF16).astype(F32)
        third = dense - first - second
        meta = jnp.where(term == 0, first, jnp.where(term == 1, second, jnp.where(term == 2, third, 0.0))).astype(BF16)
        down = lax.broadcasted_iota(jnp.int32, (rows, rows), 0)
        along = lax.broadcasted_iota(jnp.int32, (rows, rows), 1)
        meta = dot_nt(jnp.where(down == along, 1.0, 0.0).astype(BF16), meta).astype(BF16)
        for ref, start in ((tok_ref, 0), (cot_ref, half + LANES)):
            left, right = ref[:, :half], ref[:, half:]
            keep_ref[:, start : start + half] = jnp.where(low, left, right)
            send_ref[:, start : start + half] = jnp.where(low, right, left)
        keep_ref[:, half : half + LANES] = meta
        send_ref[:, half : half + LANES] = meta

    out = jax.ShapeDtypeStruct((rows, width + LANES), BF16)
    args = [tokens, route_ids, gates, cotangent]
    return pl.pallas_call(
        kernel,
        grid=(1,),
        out_shape=[out, out],
        in_specs=[pl.BlockSpec(memory_space=pltpu.SMEM)] + [pl.BlockSpec(arg.shape, lambda i: (0, 0)) for arg in args],
        out_specs=[pl.BlockSpec(out.shape, lambda i: (0, 0))] * 2,
        compiler_params=pltpu.CompilerParams(vmem_limit_bytes=60 * 1024 * 1024),
        cost_estimate=FREE,
    )(replica, *args)


def partial_products(pieces, weight_in, weight_out, expert, groups, tok_dev, capacity):
    counts = [piece.shape[0] // tok_dev * capacity for piece in pieces]
    total, number = sum(counts), len(pieces)
    half, columns = weight_in.shape
    hidden_units = weight_out.shape[1]

    def kernel(expert_ref, *refs):
        rows_refs, refs = refs[:number], refs[number:]
        in_ref, out_ref, x_ref, grad_ref, gate_ref, own_ref, send_ref = refs[:7]
        places = refs[7:]
        column = own_column(expert_ref[0], groups)
        column_rows = jnp.broadcast_to(column, (8, LANES)).astype(BF16)
        start = 0
        for piece in range(number):
            rows, count = rows_refs[piece].shape[0], counts[piece]
            meta = rows_refs[piece][:, half : half + LANES]
            gate_row = dot_nt(column_rows, meta)
            gate_col = jnp.sum(meta.astype(F32) * column, axis=1, keepdims=True)
            down = lax.broadcasted_iota(jnp.int32, (rows, rows), 0)
            along = lax.broadcasted_iota(jnp.int32, (rows, rows), 1)
            first_down, first_along = jnp.zeros_like(down), jnp.zeros_like(along)
            base_down, base_along = jnp.zeros_like(down), jnp.zeros_like(along)
            for device in range(1, rows // tok_dev):
                first_down += jnp.where(down >= device * tok_dev, tok_dev, 0)
                first_along += jnp.where(along >= device * tok_dev, tok_dev, 0)
                base_down += jnp.where(down >= device * tok_dev, capacity, 0)
                base_along += jnp.where(along >= device * tok_dev, capacity, 0)
            lower = jnp.where((along < down) & (along >= first_down), 1.0, 0.0).astype(BF16)
            upper = jnp.where((down < along) & (down >= first_along), 1.0, 0.0).astype(BF16)
            on_row = jnp.where(gate_row > 0.0, 1.0, 0.0)
            on_col = jnp.where(gate_col > 0.0, 1.0, 0.0)
            rank_row = dot_nn(on_row.astype(BF16), upper)
            rank_col = dot_nn(lower, jnp.broadcast_to(on_col, (rows, LANES)).astype(BF16))
            place_row = jnp.where(on_row > 0.0, rank_row + base_along[:8].astype(F32), -1.0)[:1, :]
            place_col = jnp.where(on_col > 0.0, rank_col[:, :1] + base_down[:, :1].astype(F32), -1.0)
            slot_down = lax.broadcasted_iota(jnp.int32, (count, rows), 0).astype(F32)
            slot_along = lax.broadcasted_iota(jnp.int32, (rows, count), 1).astype(F32)
            pick = jnp.where(place_row == slot_down, 1.0, 0.0).astype(BF16)
            places[piece][...] = jnp.where(place_col == slot_along, 1.0, 0.0).astype(BF16)
            picked = dot_nn(pick, rows_refs[piece][...])
            x_ref[start : start + count, :] = picked[:, :half].astype(BF16)
            gate = jnp.sum(picked[:, half : half + LANES] * column, axis=1, keepdims=True)
            gate_ref[start : start + count, :] = jnp.broadcast_to(gate, (count, LANES))
            grad_ref[start : start + count, :] = (gate * picked[:, half + LANES :]).astype(BF16)
            start += count
        for left, right, at in ((x_ref, in_ref, 0), (grad_ref, out_ref, columns)):
            part = dot_nn(left[...], right[...])
            own_ref[:, at : at + part.shape[1]] = part
            part = part.astype(BF16)
            send_ref[: total // 2, at : at + part.shape[1]] = part[total // 2 :]
            send_ref[total // 2 :, at : at + part.shape[1]] = part[: total // 2]

    shape = jax.ShapeDtypeStruct
    outs = [shape((total, half), BF16), shape((total, half), BF16), shape((total, LANES), F32)]
    outs += [shape((total, columns + hidden_units), F32), shape((total, columns + hidden_units), BF16)]
    outs += [shape((piece.shape[0], count), BF16) for piece, count in zip(pieces, counts)]
    got = run(kernel, outs, [expert, *pieces, weight_in, weight_out], 1)
    return (*got[:5], got[5:])


def expert_rows(own, came, gate, places, weight_in, weight_out, expert, groups):
    total = own.shape[0]
    half, columns = weight_in.shape
    hidden_units, number = columns // 2, len(places)

    def kernel(expert_ref, own_ref, came_ref, gate_ref, in_ref, out_ref, *refs):
        put, hidden_ref, pair_ref, flag_ref, outs = refs[:number], *refs[number : number + 3], refs[number + 3 :]
        gate_pre = own_ref[:, :hidden_units] + came_ref[:, :hidden_units].astype(F32)
        up_pre = own_ref[:, hidden_units:columns] + came_ref[:, hidden_units:columns].astype(F32)
        hidden_grad = own_ref[:, columns:] + came_ref[:, columns:].astype(F32)
        sig = jax.nn.sigmoid(gate_pre)
        act = gate_pre * sig
        hidden = (act * up_pre).astype(BF16)
        hidden_ref[...] = hidden
        pair_ref[:, :hidden_units] = (hidden_grad * up_pre * (sig * (1.0 + gate_pre * (1.0 - sig)))).astype(BF16)
        pair_ref[:, hidden_units:] = (hidden_grad * act).astype(BF16)
        gate = gate_ref[...]
        flag_ref[...] = gate[:8]
        score = jnp.sum(hidden.astype(F32) * hidden_grad, axis=1, keepdims=True)
        score = score / jnp.where(gate > 0.0, gate, 1.0)
        first = score.astype(BF16).astype(F32)
        lane = lax.broadcasted_iota(jnp.int32, (total, LANES), 1)
        expert = expert_ref[0]
        score = jnp.where(lane == expert, first, jnp.where(lane == expert + groups, score - first, 0.0)).astype(BF16)
        forth = (gate[:, :1] * dot_nt(hidden, out_ref[...])).astype(BF16)
        back = dot_nt(pair_ref[...], in_ref[...]).astype(BF16)
        start = 0
        for piece in range(number):
            count = put[piece].shape[1]
            place = put[piece][...]
            for rows, at in ((forth, 0), (back, half), (score, 2 * half)):
                rows = rows[start : start + count, :]
                outs[piece][:, at : at + rows.shape[1]] = dot_nn(place, rows).astype(BF16)
            start += count

    shape = jax.ShapeDtypeStruct
    outs = [shape((total, hidden_units), BF16), shape((total, columns), BF16), shape((8, LANES), F32)]
    outs += [shape((place.shape[0], 2 * half + LANES), BF16) for place in places]
    got = run(kernel, outs, [expert, own, came, gate, weight_in, weight_out, *places], 1)
    return got[0], got[1], got[2], got[3:]


def ring_pairs(groups):
    chips = groups // 2
    levels = chips // 2
    order = [2 * z for z in range(levels)] + [2 * z + 1 for z in reversed(range(levels))]
    forward = []
    for place in range(chips):
        forward.append((2 * order[place], 2 * order[(place + 1) % chips]))
        forward.append((2 * order[(place + 1) % chips] + 1, 2 * order[place] + 1))
    backward = [(to, source) for source, to in forward]
    cores = [(index, index ^ 1) for index in range(groups)]
    return forward, backward, cores


def swap_pair(value):
    return lax.ppermute(value, "dp", [(0, 1), (1, 0)])


def swap_both(value):
    groups = lax.axis_size("expert")
    pairs = [(2 * e + r, 2 * (e ^ 1) + 1 - r) for e in range(groups) for r in range(2)]
    return lax.ppermute(value, ("expert", "dp"), pairs)


def by_replica(own, other, replica):
    return jnp.where(replica == 0, jnp.stack([own, other]), jnp.stack([other, own]))


def after(value, *anchors):
    anywhere = pl.BlockSpec(memory_space=pl.ANY)
    return pl.pallas_call(
        lambda *refs: None,
        out_shape=jax.ShapeDtypeStruct(value.shape, value.dtype),
        in_specs=[anywhere] * (1 + len(anchors)),
        out_specs=anywhere,
        input_output_aliases={0: 0},
        compiler_params=pltpu.CompilerParams(vmem_limit_bytes=1024 * 1024),
        cost_estimate=FREE,
    )(value, *anchors)


class Order:
    def __init__(self):
        self.last = None

    def __call__(self, value, *anchors):
        if self.last is not None:
            value = after(value, self.last, *anchors)
        self.last = value
        return value


def body_by_width(tokens, route_ids, gates, cotangent, w_gate_up, w_down):
    tok_dev, model_width = tokens.shape
    top_count = route_ids.shape[1]
    groups = lax.axis_size("expert")
    replica = lax.axis_index("dp")
    expert = lax.axis_index("expert").astype(jnp.int32).reshape(1)
    half = w_gate_up.shape[1]
    capacity = slot_capacity(tok_dev, top_count, groups)
    steps = groups // 4
    weight_in, weight_out = w_gate_up[0], w_down[0]
    forward, backward, cores = ring_pairs(groups)
    unit = 2 * tok_dev

    def swap_cores(value):
        return lax.ppermute(value, "expert", cores)

    def products(pieces):
        *kept, own, send, places = partial_products(
            pieces, weight_in, weight_out, expert, groups, tok_dev, capacity
        )
        return [kept, own, send, places, swap_pair(send)]

    def ring(block, step):
        return lax.ppermute(block if step < steps else block[:tok_dev], "expert", forward)

    order = Order()
    keep, send = prepare(tokens, route_ids.T, gates.T, cotangent, replica.astype(jnp.int32).reshape(1), groups)
    second = jnp.concatenate([order(swap_pair(send)), order(swap_both(send))], axis=0)
    first = jnp.concatenate([keep, order(swap_cores(keep))], axis=0)
    chunks = [products([first, second])]

    def wait_for(number):
        chunks[number][4] = order(chunks[number][4], chunks[-1][0][2])

    for step in range(1, steps + 1):
        if step == steps:
            wait_for(step - 2)
        first = order(ring(first, step), chunks[-1][0][2])
        if step == 1:
            wait_for(0)
        elif 3 <= step < steps:
            wait_for(step - 2)
        second = order(ring(second, step))
        first_other, second_other = swap_cores(first), order(swap_cores(second))
        chunks.append(products([first, first_other, second, second_other]))

    terms, grads, swapped = ([], []), [], []
    for number, ((x_rows, grad_rows, gate), own, _, places, came) in enumerate(chunks):
        if number == steps:
            came = order(came)
            for place, (stream, at, other) in enumerate(swapped[:4]):
                swapped[place] = (stream, at, order(other))
        elif number == steps - 1:
            came = order(came, flag, chunks[-1][0][2])
        elif number == steps - 2:
            came = after(came, flag, chunks[-1][0][2])
        elif number:
            came = after(came, flag)
        hidden, pair_grad, flag, out = expert_rows(own, came, gate, places, weight_in, weight_out, expert, groups)
        for stream in (1, 0):
            mine = out[stream * len(out) // 2 :][: len(out) // 2]
            terms[stream].append([mine[0]])
            if number:
                swapped.append((stream, number, swap_cores(mine[1])))
        grads.append((x_rows, pair_grad, grad_rows, hidden))

    for stream, number, other in swapped:
        terms[stream][number].append(other)

    def pop_term(stream):
        return sum(term.astype(F32) for term in terms[stream].pop())

    totals = [pop_term(0), pop_term(1)]
    for step in reversed(range(steps)):
        for stream in (1, 0):
            came = lax.ppermute(totals[stream].astype(BF16), "expert", backward)
            if step == steps - 3 and stream == 1:
                came = after(came, grad_gate_up, grad_down)
            if step == steps - 2 and stream == 1:
                grads[0] = tuple(after(array, came) for array in grads[0])
                grad_gate_up, grad_down = outer_products(grads, 0, 1), outer_products(grads, 2, 3)
            base = pop_term(stream)
            if came.shape[0] < unit:
                totals[stream] = jnp.concatenate([base[:tok_dev] + came.astype(F32), base[tok_dev:]], axis=0)
            else:
                totals[stream] = base + came.astype(F32)

    there = totals[1][:, : 2 * half].astype(BF16)
    kept = totals[0][:tok_dev], swap_cores(totals[0][tok_dev:].astype(BF16))
    scores = kept[0][:, 2 * half :] + kept[1][:, 2 * half :].astype(F32)
    scores = scores[:, :groups] + scores[:, groups : 2 * groups]
    named = route_ids[:, :, None] == jnp.arange(groups, dtype=jnp.int32)[None, None, :]
    grad_gates = jnp.sum(jnp.where(named, scores[:, None, :], 0.0), axis=2)
    other = swap_pair(there[:tok_dev]), after(swap_both(there[tok_dev:]), scores)
    mixed, grad_tokens = join_halves(kept, other, half, replica.astype(jnp.int32).reshape(1))
    return (mixed, grad_tokens, grad_gates, grad_gate_up, grad_down)


def join_halves(kept, other, half, replica):
    rows = kept[0].shape[0]

    def kernel(replica_ref, mine_ref, beside_ref, across_ref, diagonal_ref, *outs):
        low = replica_ref[0] == 0
        for number, out in enumerate(outs):
            at = slice(number * half, (number + 1) * half)
            here = mine_ref[:, at] + beside_ref[:, at].astype(F32)
            there = across_ref[:, at].astype(F32) + diagonal_ref[:, at].astype(F32)
            out[:, :half] = jnp.where(low, here, there).astype(BF16)
            out[:, half:] = jnp.where(low, there, here).astype(BF16)

    out = jax.ShapeDtypeStruct((rows, 2 * half), BF16)
    return run(kernel, [out, out], [replica, *kept, *other], 1)


def outer_products(chunks, left, right):
    left = jnp.concatenate([chunk[left] for chunk in chunks])
    right = jnp.concatenate([chunk[right] for chunk in chunks])
    return lax.dot_general(left, right, (((0,), (0,)), ((), ())), preferred_element_type=F32).astype(BF16)[None]


def slot_capacity(tok_dev, top_count, experts):
    assignments = tok_dev * top_count
    return min(tok_dev, max(2, assignments // experts + max(1, assignments // (3 * experts))))


def body(tokens, route_ids, gates, cotangent, w_gate_up, w_down):
    groups, replicas = lax.axis_size("expert"), lax.axis_size("dp")
    gathered = 2 * groups * tokens.shape[0] * replicas * w_gate_up.shape[1] * 2
    small = gathered <= 8 * 1024 * 1024 and 3 * groups <= 128 and groups % 4 == 0 and groups >= 16
    if replicas == 2 and w_gate_up.shape[0] == 1 and small:
        return body_by_width(tokens, route_ids, gates, cotangent, w_gate_up, w_down)
    return body_by_slots(tokens, route_ids, gates, cotangent, w_gate_up, w_down)


def solution(mesh):
    placed = (
        P(("expert", "dp"), None),
        P(("expert", "dp"), None),
        P(("expert", "dp"), None),
        P(("expert", "dp"), None),
        P("expert", "dp", None),
        P("expert", "dp", None),
    )
    return jax.shard_map(
        body,
        mesh=mesh,
        in_specs=placed,
        out_specs=(
            P(("expert", "dp"), None),
            P(("expert", "dp"), None),
            P(("expert", "dp"), None),
            P("expert", "dp", None),
            P("expert", "dp", None),
        ),
        check_vma=False,
    )
```

```python
import jax
import jax.numpy as jnp
from jax import lax
from jax.experimental import pallas as pl
from jax.experimental.pallas import tpu as pltpu
from jax.sharding import PartitionSpec as P


def expert_forward(x_rows, weight_in, weight_out, hidden_units):
    pre_act = jnp.dot(x_rows, weight_in, preferred_element_type=jnp.float32)
    gate_pre = pre_act[:, :hidden_units]
    up_pre = pre_act[:, hidden_units:]
    sigmoid_gate = jax.nn.sigmoid(gate_pre)
    activation = gate_pre * sigmoid_gate
    hidden = (activation * up_pre).astype(jnp.bfloat16)
    expert_out = lax.dot_general(
        hidden, weight_out, (((1,), (1,)), ((), ())), preferred_element_type=jnp.float32
    ).astype(jnp.bfloat16)
    return (gate_pre, up_pre, sigmoid_gate, activation, hidden, expert_out)


def expert_backward(saved, grad_rows, weight_in, weight_out):
    gate_pre, up_pre, sigmoid_gate, activation, hidden, expert_out = saved
    hidden_grad = jnp.dot(grad_rows, weight_out, preferred_element_type=jnp.float32)
    gate_grad = (
        hidden_grad * up_pre * (sigmoid_gate * (1.0 + gate_pre * (1.0 - sigmoid_gate)))
    ).astype(jnp.bfloat16)
    up_grad = (hidden_grad * activation).astype(jnp.bfloat16)
    pair_grad = jnp.concatenate([gate_grad, up_grad], axis=1)
    input_grad = lax.dot_general(
        pair_grad, weight_in, (((1,), (1,)), ((), ())), preferred_element_type=jnp.float32
    ).astype(jnp.bfloat16)
    return (pair_grad, input_grad)


def outer_blocks(left, right, pieces):
    span = left.shape[1] // pieces
    results = []
    for piece in range(pieces):
        product = lax.dot_general(
            left[:, piece * span : (piece + 1) * span],
            right,
            (((0,), (0,)), ((), ())),
            preferred_element_type=jnp.float32,
        )
        results.append(product.astype(jnp.bfloat16))
    return jnp.stack(results, axis=0)


def replica_total(received):
    return jnp.sum(received.astype(jnp.float32), axis=0).astype(jnp.bfloat16)


def body_by_slots(tokens, route_ids, gates, cotangent, w_gate_up, w_down):
    tok_dev, model_width = tokens.shape
    top_count = route_ids.shape[1]
    groups = lax.axis_size("expert")
    replicas = lax.axis_size("dp")
    local_experts = w_gate_up.shape[0]
    hidden_units = w_down.shape[2]
    experts = groups * local_experts
    assignments = tok_dev * top_count
    capacity = min(tok_dev, max(2, assignments // experts + max(1, assignments // (3 * experts))))
    flat_ids = route_ids.reshape(assignments)
    onehot = (flat_ids[:, None] == jnp.arange(experts, dtype=jnp.int32)[None, :]).astype(jnp.int32)
    earlier = jnp.sum(
        (jnp.cumsum(onehot, axis=0, dtype=jnp.int32) - onehot) * onehot, axis=1, dtype=jnp.int32
    )
    position = flat_ids * capacity + earlier
    source = (
        jnp.full((experts * capacity,), assignments, jnp.int32)
        .at[position]
        .set(jnp.arange(assignments, dtype=jnp.int32))
    )
    token_row = source // top_count
    tok_pad = jnp.concatenate([tokens, jnp.zeros((1, model_width), jnp.bfloat16)], axis=0)
    cot_pad = jnp.concatenate([cotangent, jnp.zeros((1, model_width), jnp.bfloat16)], axis=0)
    gate_pad = jnp.concatenate([gates.reshape(assignments), jnp.zeros((1,), jnp.float32)], axis=0)
    send_rows = tok_pad[token_row].reshape(experts, capacity, model_width)
    send_grads = (gate_pad[source][:, None] * cot_pad[token_row].astype(jnp.float32)).astype(
        jnp.bfloat16
    )
    send_grads = send_grads.reshape(experts, capacity, model_width)
    weights_in, weights_out = (
        lax.all_gather(w_gate_up, "dp", axis=1, tiled=True),
        lax.all_gather(w_down, "dp", axis=1, tiled=True),
    )
    rows_in, grads_in = (
        lax.all_to_all(send_rows, "expert", split_axis=0, concat_axis=1, tiled=True),
        lax.all_to_all(send_grads, "expert", split_axis=0, concat_axis=1, tiled=True),
    )
    local = 0
    forward_parts = expert_forward(
        rows_in[local], weights_in[local], weights_out[local], hidden_units
    )
    saved_all = [forward_parts]
    out_list = [forward_parts[5]]
    down_list = [outer_blocks(grads_in[local], forward_parts[4], replicas)]
    expert_outs = jnp.stack(out_list, axis=0)
    down_stack = jnp.stack(down_list, axis=1)
    outs_back = lax.all_to_all(expert_outs, "expert", split_axis=1, concat_axis=0, tiled=True)
    local = 0
    pair_grad, input_grad = expert_backward(
        saved_all[local], grads_in[local], weights_in[local], weights_out[local]
    )
    input_list = [input_grad]
    gate_up_list = [outer_blocks(rows_in[local], pair_grad, replicas)]
    input_grads = jnp.stack(input_list, axis=0)
    gate_up_stack = jnp.stack(gate_up_list, axis=1)
    grads_back = lax.all_to_all(input_grads, "expert", split_axis=1, concat_axis=0, tiled=True)
    gate_up_received, down_received = (
        lax.all_to_all(gate_up_stack, "dp", split_axis=0, concat_axis=0, tiled=True),
        lax.all_to_all(down_stack, "dp", split_axis=0, concat_axis=0, tiled=True),
    )
    grad_gate_up = replica_total(gate_up_received)
    grad_down = replica_total(down_received)
    out_rows = outs_back.reshape(experts * capacity, model_width)[position].reshape(
        tok_dev, top_count, model_width
    )
    mixed = jnp.sum(gates[:, :, None] * out_rows.astype(jnp.float32), axis=1).astype(jnp.bfloat16)
    grad_gates = jnp.einsum("td,tkd->tk", cotangent, out_rows, preferred_element_type=jnp.float32)
    back_rows = grads_back.reshape(experts * capacity, model_width)[position].reshape(
        tok_dev, top_count, model_width
    )
    grad_tokens = jnp.sum(back_rows.astype(jnp.float32), axis=1).astype(jnp.bfloat16)
    return (mixed, grad_tokens, grad_gates, grad_gate_up, grad_down)


F32, BF16 = jnp.float32, jnp.bfloat16
LANES = 128
FREE = pl.CostEstimate(flops=0, bytes_accessed=0, transcendentals=0)


def run(kernel, outs, args, scalars=0):
    spaces = [pltpu.SMEM] * scalars + [pltpu.VMEM] * (len(args) - scalars)
    return pl.pallas_call(
        kernel,
        out_shape=outs,
        in_specs=[pl.BlockSpec(memory_space=space) for space in spaces],
        out_specs=[pl.BlockSpec(memory_space=pltpu.VMEM) for _ in outs],
        compiler_params=pltpu.CompilerParams(vmem_limit_bytes=10 * 1024 * 1024),
        cost_estimate=FREE,
    )(*args)


def dot_nn(left, right):
    return jnp.dot(left, right, preferred_element_type=F32)


def dot_nt(left, right):
    return lax.dot_general(left, right, (((1,), (1,)), ((), ())), preferred_element_type=F32)


def own_column(expert, groups):
    lane = lax.broadcasted_iota(jnp.int32, (1, LANES), 1)
    hit = (lane == expert) | (lane == expert + groups) | (lane == expert + 2 * groups)
    return jnp.where(hit, 1.0, 0.0)


def prepare(tokens, route_ids, gates, cotangent, replica, groups):
    rows, width = tokens.shape
    half = width // 2

    def kernel(replica_ref, tok_ref, id_ref, gate_ref, cot_ref, keep_ref, send_ref):
        low = replica_ref[0] == 0
        line = lax.broadcasted_iota(jnp.int32, (LANES, rows), 0)
        term = lax.div(line, groups)
        named = line - term * groups
        dense = jnp.zeros((LANES, rows), F32)
        for k in range(id_ref.shape[0]):
            dense = dense + jnp.where(id_ref[k : k + 1, :] == named, gate_ref[k : k + 1, :], 0.0)
        first = dense.astype(BF16).astype(F32)
        second = (dense - first).astype(BF16).astype(F32)
        third = dense - first - second
        meta = jnp.where(term == 0, first, jnp.where(term == 1, second, jnp.where(term == 2, third, 0.0))).astype(BF16)
        down = lax.broadcasted_iota(jnp.int32, (rows, rows), 0)
        along = lax.broadcasted_iota(jnp.int32, (rows, rows), 1)
        meta = dot_nt(jnp.where(down == along, 1.0, 0.0).astype(BF16), meta).astype(BF16)
        for ref, start in ((tok_ref, 0), (cot_ref, half + LANES)):
            left, right = ref[:, :half], ref[:, half:]
            keep_ref[:, start : start + half] = jnp.where(low, left, right)
            send_ref[:, start : start + half] = jnp.where(low, right, left)
        keep_ref[:, half : half + LANES] = meta
        send_ref[:, half : half + LANES] = meta

    out = jax.ShapeDtypeStruct((rows, width + LANES), BF16)
    args = [tokens, route_ids, gates, cotangent]
    return pl.pallas_call(
        kernel,
        grid=(1,),
        out_shape=[out, out],
        in_specs=[pl.BlockSpec(memory_space=pltpu.SMEM)] + [pl.BlockSpec(arg.shape, lambda i: (0, 0)) for arg in args],
        out_specs=[pl.BlockSpec(out.shape, lambda i: (0, 0))] * 2,
        compiler_params=pltpu.CompilerParams(vmem_limit_bytes=60 * 1024 * 1024),
        cost_estimate=FREE,
    )(replica, *args)


def partial_products(pieces, weight_in, weight_out, expert, groups, tok_dev, capacity):
    counts = [piece.shape[0] // tok_dev * capacity for piece in pieces]
    total, number = sum(counts), len(pieces)
    half, columns = weight_in.shape
    hidden_units = weight_out.shape[1]

    def kernel(expert_ref, *refs):
        rows_refs, refs = refs[:number], refs[number:]
        in_ref, out_ref, x_ref, grad_ref, gate_ref, own_ref, send_ref = refs[:7]
        places = refs[7:]
        column = own_column(expert_ref[0], groups)
        column_rows = jnp.broadcast_to(column, (8, LANES)).astype(BF16)
        start = 0
        for piece in range(number):
            rows, count = rows_refs[piece].shape[0], counts[piece]
            meta = rows_refs[piece][:, half : half + LANES]
            gate_row = dot_nt(column_rows, meta)
            gate_col = jnp.sum(meta.astype(F32) * column, axis=1, keepdims=True)
            down = lax.broadcasted_iota(jnp.int32, (rows, rows), 0)
            along = lax.broadcasted_iota(jnp.int32, (rows, rows), 1)
            first_down, first_along = jnp.zeros_like(down), jnp.zeros_like(along)
            base_down, base_along = jnp.zeros_like(down), jnp.zeros_like(along)
            for device in range(1, rows // tok_dev):
                first_down += jnp.where(down >= device * tok_dev, tok_dev, 0)
                first_along += jnp.where(along >= device * tok_dev, tok_dev, 0)
                base_down += jnp.where(down >= device * tok_dev, capacity, 0)
                base_along += jnp.where(along >= device * tok_dev, capacity, 0)
            lower = jnp.where((along < down) & (along >= first_down), 1.0, 0.0).astype(BF16)
            upper = jnp.where((down < along) & (down >= first_along), 1.0, 0.0).astype(BF16)
            on_row = jnp.where(gate_row > 0.0, 1.0, 0.0)
            on_col = jnp.where(gate_col > 0.0, 1.0, 0.0)
            rank_row = dot_nn(on_row.astype(BF16), upper)
            rank_col = dot_nn(lower, jnp.broadcast_to(on_col, (rows, LANES)).astype(BF16))
            place_row = jnp.where(on_row > 0.0, rank_row + base_along[:8].astype(F32), -1.0)[:1, :]
            place_col = jnp.where(on_col > 0.0, rank_col[:, :1] + base_down[:, :1].astype(F32), -1.0)
            slot_down = lax.broadcasted_iota(jnp.int32, (count, rows), 0).astype(F32)
            slot_along = lax.broadcasted_iota(jnp.int32, (rows, count), 1).astype(F32)
            pick = jnp.where(place_row == slot_down, 1.0, 0.0).astype(BF16)
            places[piece][...] = jnp.where(place_col == slot_along, 1.0, 0.0).astype(BF16)
            picked = dot_nn(pick, rows_refs[piece][...])
            x_ref[start : start + count, :] = picked[:, :half].astype(BF16)
            gate = jnp.sum(picked[:, half : half + LANES] * column, axis=1, keepdims=True)
            gate_ref[start : start + count, :] = jnp.broadcast_to(gate, (count, LANES))
            grad_ref[start : start + count, :] = (gate * picked[:, half + LANES :]).astype(BF16)
            start += count
        for left, right, at in ((x_ref, in_ref, 0), (grad_ref, out_ref, columns)):
            part = dot_nn(left[...], right[...])
            own_ref[:, at : at + part.shape[1]] = part
            part = part.astype(BF16)
            send_ref[: total // 2, at : at + part.shape[1]] = part[total // 2 :]
            send_ref[total // 2 :, at : at + part.shape[1]] = part[: total // 2]

    shape = jax.ShapeDtypeStruct
    outs = [shape((total, half), BF16), shape((total, half), BF16), shape((total, LANES), F32)]
    outs += [shape((total, columns + hidden_units), F32), shape((total, columns + hidden_units), BF16)]
    outs += [shape((piece.shape[0], count), BF16) for piece, count in zip(pieces, counts)]
    got = run(kernel, outs, [expert, *pieces, weight_in, weight_out], 1)
    return (*got[:5], got[5:])


def expert_rows(own, came, gate, places, weight_in, weight_out, expert, groups):
    total = own.shape[0]
    half, columns = weight_in.shape
    hidden_units, number = columns // 2, len(places)
    rows = places[0].shape[0]
    targets, heights = ([(0, 0), (2, 0), (1, 0), (2, rows)], [rows, rows, 2 * rows])
    if number == 2:
        targets, heights = [(0, 0), (1, 0)], [rows, rows]

    def kernel(expert_ref, own_ref, came_ref, gate_ref, in_ref, out_ref, *refs):
        put, hidden_ref, pair_ref, flag_ref, outs = refs[:number], *refs[number : number + 3], refs[number + 3 :]
        gate_pre = own_ref[:, :hidden_units] + came_ref[:, :hidden_units].astype(F32)
        up_pre = own_ref[:, hidden_units:columns] + came_ref[:, hidden_units:columns].astype(F32)
        hidden_grad = own_ref[:, columns:] + came_ref[:, columns:].astype(F32)
        sig = jax.nn.sigmoid(gate_pre)
        act = gate_pre * sig
        hidden = (act * up_pre).astype(BF16)
        hidden_ref[...] = hidden
        pair_ref[:, :hidden_units] = (hidden_grad * up_pre * (sig * (1.0 + gate_pre * (1.0 - sig)))).astype(BF16)
        pair_ref[:, hidden_units:] = (hidden_grad * act).astype(BF16)
        gate = gate_ref[...]
        flag_ref[...] = gate[:8]
        score = jnp.sum(hidden.astype(F32) * hidden_grad, axis=1, keepdims=True)
        score = score / jnp.where(gate > 0.0, gate, 1.0)
        first = score.astype(BF16).astype(F32)
        lane = lax.broadcasted_iota(jnp.int32, (total, LANES), 1)
        expert = expert_ref[0]
        score = jnp.where(lane == expert, first, jnp.where(lane == expert + groups, score - first, 0.0)).astype(BF16)
        forth = (gate[:, :1] * dot_nt(hidden, out_ref[...])).astype(BF16)
        back = dot_nt(pair_ref[...], in_ref[...]).astype(BF16)
        start = 0
        for piece in range(number):
            count = put[piece].shape[1]
            place = put[piece][...]
            to, down = targets[piece]
            for rows, at in ((forth, 0), (back, half), (score, 2 * half)):
                rows = dot_nn(place, rows[start : start + count, :]).astype(BF16)
                outs[to][down : down + rows.shape[0], at : at + rows.shape[1]] = rows
            start += count

    shape = jax.ShapeDtypeStruct
    outs = [shape((total, hidden_units), BF16), shape((total, columns), BF16), shape((8, LANES), F32)]
    outs += [shape((height, 2 * half + LANES), BF16) for height in heights]
    got = run(kernel, outs, [expert, own, came, gate, weight_in, weight_out, *places], 1)
    return got[0], got[1], got[2], got[3:]


def ring_pairs(groups):
    chips = groups // 2
    levels = chips // 2
    order = [2 * z for z in range(levels)] + [2 * z + 1 for z in reversed(range(levels))]
    forward = []
    for place in range(chips):
        forward.append((2 * order[place], 2 * order[(place + 1) % chips]))
        forward.append((2 * order[(place + 1) % chips] + 1, 2 * order[place] + 1))
    backward = [(to, source) for source, to in forward]
    cores = [(index, index ^ 1) for index in range(groups)]
    return forward, backward, cores


def swap_pair(value):
    return lax.ppermute(value, "dp", [(0, 1), (1, 0)])


def swap_both(value):
    groups = lax.axis_size("expert")
    pairs = [(2 * e + r, 2 * (e ^ 1) + 1 - r) for e in range(groups) for r in range(2)]
    return lax.ppermute(value, ("expert", "dp"), pairs)


def by_replica(own, other, replica):
    return jnp.where(replica == 0, jnp.stack([own, other]), jnp.stack([other, own]))


def after(value, *anchors):
    anywhere = pl.BlockSpec(memory_space=pl.ANY)
    return pl.pallas_call(
        lambda *refs: None,
        out_shape=jax.ShapeDtypeStruct(value.shape, value.dtype),
        in_specs=[anywhere] * (1 + len(anchors)),
        out_specs=anywhere,
        input_output_aliases={0: 0},
        compiler_params=pltpu.CompilerParams(vmem_limit_bytes=1024 * 1024),
        cost_estimate=FREE,
    )(value, *anchors)


class Order:
    def __init__(self):
        self.last = None

    def __call__(self, value, *anchors):
        if self.last is not None:
            value = after(value, self.last, *anchors)
        self.last = value
        return value


def body_by_width(tokens, route_ids, gates, cotangent, w_gate_up, w_down):
    tok_dev, model_width = tokens.shape
    top_count = route_ids.shape[1]
    groups = lax.axis_size("expert")
    replica = lax.axis_index("dp")
    expert = lax.axis_index("expert").astype(jnp.int32).reshape(1)
    half = w_gate_up.shape[1]
    capacity = slot_capacity(tok_dev, top_count, groups)
    steps = groups // 4
    weight_in, weight_out = w_gate_up[0], w_down[0]
    forward, backward, cores = ring_pairs(groups)
    unit = 2 * tok_dev

    def swap_cores(value):
        return lax.ppermute(value, "expert", cores)

    def products(pieces):
        *kept, own, send, places = partial_products(
            pieces, weight_in, weight_out, expert, groups, tok_dev, capacity
        )
        return [kept, own, send, places, swap_pair(send)]

    def ring(block, step):
        return lax.ppermute(block if step < steps else block[:tok_dev], "expert", forward)

    order = Order()
    keep, send = prepare(tokens, route_ids.T, gates.T, cotangent, replica.astype(jnp.int32).reshape(1), groups)
    second = jnp.concatenate([order(swap_pair(send)), order(swap_both(send))], axis=0)
    first = jnp.concatenate([keep, order(swap_cores(keep))], axis=0)
    chunks = [products([first, second])]

    def wait_for(number):
        chunks[number][4] = order(chunks[number][4], chunks[-1][0][2])

    for step in range(1, steps + 1):
        if step == steps:
            wait_for(step - 2)
        first = order(ring(first, step), chunks[-1][0][2])
        if step == 1:
            wait_for(0)
        elif 3 <= step < steps:
            wait_for(step - 2)
        second = order(ring(second, step))
        first_other, second_other = swap_cores(first), order(swap_cores(second))
        chunks.append(products([first, first_other, second, second_other]))

    terms, grads, swapped = ([], []), [], []
    for number, ((x_rows, grad_rows, gate), own, _, places, came) in enumerate(chunks):
        if number == steps:
            came = order(came)
        elif number == steps - 1:
            came = order(came, flag, chunks[-1][0][2])
        elif number == steps - 2:
            came = after(came, flag, chunks[-1][0][2])
        elif number:
            came = after(came, flag)
        hidden, pair_grad, flag, out = expert_rows(own, came, gate, places, weight_in, weight_out, expert, groups)
        for stream in range(2):
            terms[stream].append([out[stream]])
        if number:
            swapped.append(swap_cores(out[2]))
        grads.append((x_rows, pair_grad, grad_rows, hidden))

    for number, other in enumerate(swapped, 1):
        half_way = other.shape[0] // 2
        terms[0][number].append(other[:half_way])
        terms[1][number].append(after(other[half_way:], flag))

    def pop_term(stream):
        return sum(term.astype(F32) for term in terms[stream].pop())

    totals = [pop_term(0), pop_term(1)]
    for step in reversed(range(steps)):
        for stream in (1, 0):
            came = lax.ppermute(totals[stream].astype(BF16), "expert", backward)
            if step == steps - 3 and stream == 1:
                came = after(came, grad_gate_up, grad_down)
            if step == steps - 2 and stream == 1:
                grads[0] = tuple(after(array, came) for array in grads[0])
                grad_gate_up, grad_down = outer_products(grads, 0, 1), outer_products(grads, 2, 3)
            base = pop_term(stream)
            if came.shape[0] < unit:
                totals[stream] = jnp.concatenate([base[:tok_dev] + came.astype(F32), base[tok_dev:]], axis=0)
            else:
                totals[stream] = base + came.astype(F32)

    there = totals[1][:, : 2 * half].astype(BF16)
    kept = totals[0][:tok_dev], swap_cores(totals[0][tok_dev:].astype(BF16))
    scores = kept[0][:, 2 * half :] + kept[1][:, 2 * half :].astype(F32)
    scores = scores[:, :groups] + scores[:, groups : 2 * groups]
    named = route_ids[:, :, None] == jnp.arange(groups, dtype=jnp.int32)[None, None, :]
    grad_gates = jnp.sum(jnp.where(named, scores[:, None, :], 0.0), axis=2)
    other = swap_pair(there[:tok_dev]), after(swap_both(there[tok_dev:]), scores)
    mixed, grad_tokens = join_halves(kept, other, half, replica.astype(jnp.int32).reshape(1))
    return (mixed, grad_tokens, grad_gates, grad_gate_up, grad_down)


def join_halves(kept, other, half, replica):
    rows = kept[0].shape[0]

    def kernel(replica_ref, mine_ref, beside_ref, across_ref, diagonal_ref, *outs):
        low = replica_ref[0] == 0
        for number, out in enumerate(outs):
            at = slice(number * half, (number + 1) * half)
            here = mine_ref[:, at] + beside_ref[:, at].astype(F32)
            there = across_ref[:, at].astype(F32) + diagonal_ref[:, at].astype(F32)
            out[:, :half] = jnp.where(low, here, there).astype(BF16)
            out[:, half:] = jnp.where(low, there, here).astype(BF16)

    out = jax.ShapeDtypeStruct((rows, 2 * half), BF16)
    return run(kernel, [out, out], [replica, *kept, *other], 1)


def outer_products(chunks, left, right):
    left = jnp.concatenate([chunk[left] for chunk in chunks])
    right = jnp.concatenate([chunk[right] for chunk in chunks])
    return lax.dot_general(left, right, (((0,), (0,)), ((), ())), preferred_element_type=F32).astype(BF16)[None]


def slot_capacity(tok_dev, top_count, experts):
    assignments = tok_dev * top_count
    return min(tok_dev, max(2, assignments // experts + max(1, assignments // (3 * experts))))


def body(tokens, route_ids, gates, cotangent, w_gate_up, w_down):
    groups, replicas = lax.axis_size("expert"), lax.axis_size("dp")
    gathered = 2 * groups * tokens.shape[0] * replicas * w_gate_up.shape[1] * 2
    small = gathered <= 8 * 1024 * 1024 and 3 * groups <= 128 and groups % 4 == 0 and groups >= 16
    if replicas == 2 and w_gate_up.shape[0] == 1 and small:
        return body_by_width(tokens, route_ids, gates, cotangent, w_gate_up, w_down)
    return body_by_slots(tokens, route_ids, gates, cotangent, w_gate_up, w_down)


def solution(mesh):
    placed = (
        P(("expert", "dp"), None),
        P(("expert", "dp"), None),
        P(("expert", "dp"), None),
        P(("expert", "dp"), None),
        P("expert", "dp", None),
        P("expert", "dp", None),
    )
    return jax.shard_map(
        body,
        mesh=mesh,
        in_specs=placed,
        out_specs=(
            P(("expert", "dp"), None),
            P(("expert", "dp"), None),
            P(("expert", "dp"), None),
            P("expert", "dp", None),
            P("expert", "dp", None),
        ),
        check_vma=False,
    )
```

```python
import jax
import jax.numpy as jnp
from jax import lax
from jax.experimental import pallas as pl
from jax.experimental.pallas import tpu as pltpu
from jax.sharding import PartitionSpec as P


def expert_forward(x_rows, weight_in, weight_out, hidden_units):
    pre_act = jnp.dot(x_rows, weight_in, preferred_element_type=jnp.float32)
    gate_pre = pre_act[:, :hidden_units]
    up_pre = pre_act[:, hidden_units:]
    sigmoid_gate = jax.nn.sigmoid(gate_pre)
    activation = gate_pre * sigmoid_gate
    hidden = (activation * up_pre).astype(jnp.bfloat16)
    expert_out = lax.dot_general(
        hidden, weight_out, (((1,), (1,)), ((), ())), preferred_element_type=jnp.float32
    ).astype(jnp.bfloat16)
    return (gate_pre, up_pre, sigmoid_gate, activation, hidden, expert_out)


def expert_backward(saved, grad_rows, weight_in, weight_out):
    gate_pre, up_pre, sigmoid_gate, activation, hidden, expert_out = saved
    hidden_grad = jnp.dot(grad_rows, weight_out, preferred_element_type=jnp.float32)
    gate_grad = (
        hidden_grad * up_pre * (sigmoid_gate * (1.0 + gate_pre * (1.0 - sigmoid_gate)))
    ).astype(jnp.bfloat16)
    up_grad = (hidden_grad * activation).astype(jnp.bfloat16)
    pair_grad = jnp.concatenate([gate_grad, up_grad], axis=1)
    input_grad = lax.dot_general(
        pair_grad, weight_in, (((1,), (1,)), ((), ())), preferred_element_type=jnp.float32
    ).astype(jnp.bfloat16)
    return (pair_grad, input_grad)


def outer_blocks(left, right, pieces):
    span = left.shape[1] // pieces
    results = []
    for piece in range(pieces):
        product = lax.dot_general(
            left[:, piece * span : (piece + 1) * span],
            right,
            (((0,), (0,)), ((), ())),
            preferred_element_type=jnp.float32,
        )
        results.append(product.astype(jnp.bfloat16))
    return jnp.stack(results, axis=0)


def replica_total(received):
    return jnp.sum(received.astype(jnp.float32), axis=0).astype(jnp.bfloat16)


def body_by_slots(tokens, route_ids, gates, cotangent, w_gate_up, w_down):
    tok_dev, model_width = tokens.shape
    top_count = route_ids.shape[1]
    groups = lax.axis_size("expert")
    replicas = lax.axis_size("dp")
    local_experts = w_gate_up.shape[0]
    hidden_units = w_down.shape[2]
    experts = groups * local_experts
    assignments = tok_dev * top_count
    capacity = min(tok_dev, max(2, assignments // experts + max(1, assignments // (3 * experts))))
    flat_ids = route_ids.reshape(assignments)
    onehot = (flat_ids[:, None] == jnp.arange(experts, dtype=jnp.int32)[None, :]).astype(jnp.int32)
    earlier = jnp.sum(
        (jnp.cumsum(onehot, axis=0, dtype=jnp.int32) - onehot) * onehot, axis=1, dtype=jnp.int32
    )
    position = flat_ids * capacity + earlier
    source = (
        jnp.full((experts * capacity,), assignments, jnp.int32)
        .at[position]
        .set(jnp.arange(assignments, dtype=jnp.int32))
    )
    token_row = source // top_count
    tok_pad = jnp.concatenate([tokens, jnp.zeros((1, model_width), jnp.bfloat16)], axis=0)
    cot_pad = jnp.concatenate([cotangent, jnp.zeros((1, model_width), jnp.bfloat16)], axis=0)
    gate_pad = jnp.concatenate([gates.reshape(assignments), jnp.zeros((1,), jnp.float32)], axis=0)
    send_rows = tok_pad[token_row].reshape(experts, capacity, model_width)
    send_grads = (gate_pad[source][:, None] * cot_pad[token_row].astype(jnp.float32)).astype(
        jnp.bfloat16
    )
    send_grads = send_grads.reshape(experts, capacity, model_width)
    weights_in, weights_out = (
        lax.all_gather(w_gate_up, "dp", axis=1, tiled=True),
        lax.all_gather(w_down, "dp", axis=1, tiled=True),
    )
    rows_in, grads_in = (
        lax.all_to_all(send_rows, "expert", split_axis=0, concat_axis=1, tiled=True),
        lax.all_to_all(send_grads, "expert", split_axis=0, concat_axis=1, tiled=True),
    )
    local = 0
    forward_parts = expert_forward(
        rows_in[local], weights_in[local], weights_out[local], hidden_units
    )
    saved_all = [forward_parts]
    out_list = [forward_parts[5]]
    down_list = [outer_blocks(grads_in[local], forward_parts[4], replicas)]
    expert_outs = jnp.stack(out_list, axis=0)
    down_stack = jnp.stack(down_list, axis=1)
    outs_back = lax.all_to_all(expert_outs, "expert", split_axis=1, concat_axis=0, tiled=True)
    local = 0
    pair_grad, input_grad = expert_backward(
        saved_all[local], grads_in[local], weights_in[local], weights_out[local]
    )
    input_list = [input_grad]
    gate_up_list = [outer_blocks(rows_in[local], pair_grad, replicas)]
    input_grads = jnp.stack(input_list, axis=0)
    gate_up_stack = jnp.stack(gate_up_list, axis=1)
    grads_back = lax.all_to_all(input_grads, "expert", split_axis=1, concat_axis=0, tiled=True)
    gate_up_received, down_received = (
        lax.all_to_all(gate_up_stack, "dp", split_axis=0, concat_axis=0, tiled=True),
        lax.all_to_all(down_stack, "dp", split_axis=0, concat_axis=0, tiled=True),
    )
    grad_gate_up = replica_total(gate_up_received)
    grad_down = replica_total(down_received)
    out_rows = outs_back.reshape(experts * capacity, model_width)[position].reshape(
        tok_dev, top_count, model_width
    )
    mixed = jnp.sum(gates[:, :, None] * out_rows.astype(jnp.float32), axis=1).astype(jnp.bfloat16)
    grad_gates = jnp.einsum("td,tkd->tk", cotangent, out_rows, preferred_element_type=jnp.float32)
    back_rows = grads_back.reshape(experts * capacity, model_width)[position].reshape(
        tok_dev, top_count, model_width
    )
    grad_tokens = jnp.sum(back_rows.astype(jnp.float32), axis=1).astype(jnp.bfloat16)
    return (mixed, grad_tokens, grad_gates, grad_gate_up, grad_down)


F32, BF16 = jnp.float32, jnp.bfloat16
LANES = 128
FREE = pl.CostEstimate(flops=0, bytes_accessed=0, transcendentals=0)


def run(kernel, outs, args, scalars=0):
    spaces = [pltpu.SMEM] * scalars + [pltpu.VMEM] * (len(args) - scalars)
    return pl.pallas_call(
        kernel,
        out_shape=outs,
        in_specs=[pl.BlockSpec(memory_space=space) for space in spaces],
        out_specs=[pl.BlockSpec(memory_space=pltpu.VMEM) for _ in outs],
        compiler_params=pltpu.CompilerParams(vmem_limit_bytes=10 * 1024 * 1024),
        cost_estimate=FREE,
    )(*args)


def dot_nn(left, right):
    return jnp.dot(left, right, preferred_element_type=F32)


def dot_nt(left, right):
    return lax.dot_general(left, right, (((1,), (1,)), ((), ())), preferred_element_type=F32)


def own_column(expert, groups):
    lane = lax.broadcasted_iota(jnp.int32, (1, LANES), 1)
    hit = (lane == expert) | (lane == expert + groups) | (lane == expert + 2 * groups)
    return jnp.where(hit, 1.0, 0.0)


def prepare(tokens, route_ids, gates, cotangent, replica, groups):
    rows, width = tokens.shape
    half = width // 2

    def kernel(replica_ref, tok_ref, id_ref, gate_ref, cot_ref, keep_ref, send_ref):
        low = replica_ref[0] == 0
        line = lax.broadcasted_iota(jnp.int32, (LANES, rows), 0)
        term = lax.div(line, groups)
        named = line - term * groups
        dense = jnp.zeros((LANES, rows), F32)
        for k in range(id_ref.shape[0]):
            dense = dense + jnp.where(id_ref[k : k + 1, :] == named, gate_ref[k : k + 1, :], 0.0)
        first = dense.astype(BF16).astype(F32)
        second = (dense - first).astype(BF16).astype(F32)
        third = dense - first - second
        meta = jnp.where(term == 0, first, jnp.where(term == 1, second, jnp.where(term == 2, third, 0.0))).astype(BF16)
        down = lax.broadcasted_iota(jnp.int32, (rows, rows), 0)
        along = lax.broadcasted_iota(jnp.int32, (rows, rows), 1)
        meta = dot_nt(jnp.where(down == along, 1.0, 0.0).astype(BF16), meta).astype(BF16)
        for ref, start in ((tok_ref, 0), (cot_ref, half + LANES)):
            left, right = ref[:, :half], ref[:, half:]
            keep_ref[:, start : start + half] = jnp.where(low, left, right)
            send_ref[:, start : start + half] = jnp.where(low, right, left)
        keep_ref[:, half : half + LANES] = meta
        send_ref[:, half : half + LANES] = meta

    out = jax.ShapeDtypeStruct((rows, width + LANES), BF16)
    args = [tokens, route_ids, gates, cotangent]
    return pl.pallas_call(
        kernel,
        grid=(1,),
        out_shape=[out, out],
        in_specs=[pl.BlockSpec(memory_space=pltpu.SMEM)] + [pl.BlockSpec(arg.shape, lambda i: (0, 0)) for arg in args],
        out_specs=[pl.BlockSpec(out.shape, lambda i: (0, 0))] * 2,
        compiler_params=pltpu.CompilerParams(vmem_limit_bytes=60 * 1024 * 1024),
        cost_estimate=FREE,
    )(replica, *args)


def partial_products(pieces, weight_in, weight_out, expert, groups, tok_dev, capacity):
    counts = [piece.shape[0] // tok_dev * capacity for piece in pieces]
    total, number = sum(counts), len(pieces)
    half, columns = weight_in.shape
    hidden_units = weight_out.shape[1]

    def kernel(expert_ref, *refs):
        rows_refs, refs = refs[:number], refs[number:]
        in_ref, out_ref, x_ref, grad_ref, gate_ref, own_ref, send_ref = refs[:7]
        places = refs[7:]
        column = own_column(expert_ref[0], groups)
        column_rows = jnp.broadcast_to(column, (8, LANES)).astype(BF16)
        start = 0
        for piece in range(number):
            rows, count = rows_refs[piece].shape[0], counts[piece]
            meta = rows_refs[piece][:, half : half + LANES]
            gate_row = dot_nt(column_rows, meta)
            gate_col = jnp.sum(meta.astype(F32) * column, axis=1, keepdims=True)
            down = lax.broadcasted_iota(jnp.int32, (rows, rows), 0)
            along = lax.broadcasted_iota(jnp.int32, (rows, rows), 1)
            first_down, first_along = jnp.zeros_like(down), jnp.zeros_like(along)
            base_down, base_along = jnp.zeros_like(down), jnp.zeros_like(along)
            for device in range(1, rows // tok_dev):
                first_down += jnp.where(down >= device * tok_dev, tok_dev, 0)
                first_along += jnp.where(along >= device * tok_dev, tok_dev, 0)
                base_down += jnp.where(down >= device * tok_dev, capacity, 0)
                base_along += jnp.where(along >= device * tok_dev, capacity, 0)
            lower = jnp.where((along < down) & (along >= first_down), 1.0, 0.0).astype(BF16)
            upper = jnp.where((down < along) & (down >= first_along), 1.0, 0.0).astype(BF16)
            on_row = jnp.where(gate_row > 0.0, 1.0, 0.0)
            on_col = jnp.where(gate_col > 0.0, 1.0, 0.0)
            rank_row = dot_nn(on_row.astype(BF16), upper)
            rank_col = dot_nn(lower, jnp.broadcast_to(on_col, (rows, LANES)).astype(BF16))
            place_row = jnp.where(on_row > 0.0, rank_row + base_along[:8].astype(F32), -1.0)[:1, :]
            place_col = jnp.where(on_col > 0.0, rank_col[:, :1] + base_down[:, :1].astype(F32), -1.0)
            slot_down = lax.broadcasted_iota(jnp.int32, (count, rows), 0).astype(F32)
            slot_along = lax.broadcasted_iota(jnp.int32, (rows, count), 1).astype(F32)
            pick = jnp.where(place_row == slot_down, 1.0, 0.0).astype(BF16)
            places[piece][...] = jnp.where(place_col == slot_along, 1.0, 0.0).astype(BF16)
            picked = dot_nn(pick, rows_refs[piece][...])
            x_ref[start : start + count, :] = picked[:, :half].astype(BF16)
            gate = jnp.sum(picked[:, half : half + LANES] * column, axis=1, keepdims=True)
            gate_ref[start : start + count, :] = jnp.broadcast_to(gate, (count, LANES))
            grad_ref[start : start + count, :] = (gate * picked[:, half + LANES :]).astype(BF16)
            start += count
        for left, right, at in ((x_ref, in_ref, 0), (grad_ref, out_ref, columns)):
            part = dot_nn(left[...], right[...])
            own_ref[:, at : at + part.shape[1]] = part
            part = part.astype(BF16)
            send_ref[: total // 2, at : at + part.shape[1]] = part[total // 2 :]
            send_ref[total // 2 :, at : at + part.shape[1]] = part[: total // 2]

    shape = jax.ShapeDtypeStruct
    outs = [shape((total, half), BF16), shape((total, half), BF16), shape((total, LANES), F32)]
    outs += [shape((total, columns + hidden_units), F32), shape((total, columns + hidden_units), BF16)]
    outs += [shape((piece.shape[0], count), BF16) for piece, count in zip(pieces, counts)]
    got = run(kernel, outs, [expert, *pieces, weight_in, weight_out], 1)
    return (*got[:5], got[5:])


def expert_rows(own, came, gate, places, weight_in, weight_out, expert, groups):
    total = own.shape[0]
    half, columns = weight_in.shape
    hidden_units, number = columns // 2, len(places)
    rows = places[0].shape[0]
    targets, heights = ([(0, 0), (2, 0), (1, 0), (2, rows)], [rows, rows, 2 * rows])
    if number == 2:
        targets, heights = [(0, 0), (1, 0)], [rows, rows]

    def kernel(expert_ref, own_ref, came_ref, gate_ref, in_ref, out_ref, *refs):
        put, hidden_ref, pair_ref, flag_ref, outs = refs[:number], *refs[number : number + 3], refs[number + 3 :]
        gate_pre = own_ref[:, :hidden_units] + came_ref[:, :hidden_units].astype(F32)
        up_pre = own_ref[:, hidden_units:columns] + came_ref[:, hidden_units:columns].astype(F32)
        hidden_grad = own_ref[:, columns:] + came_ref[:, columns:].astype(F32)
        sig = jax.nn.sigmoid(gate_pre)
        act = gate_pre * sig
        hidden = (act * up_pre).astype(BF16)
        hidden_ref[...] = hidden
        pair_ref[:, :hidden_units] = (hidden_grad * up_pre * (sig * (1.0 + gate_pre * (1.0 - sig)))).astype(BF16)
        pair_ref[:, hidden_units:] = (hidden_grad * act).astype(BF16)
        gate = gate_ref[...]
        flag_ref[...] = gate[:8]
        score = jnp.sum(hidden.astype(F32) * hidden_grad, axis=1, keepdims=True)
        score = score / jnp.where(gate > 0.0, gate, 1.0)
        first = score.astype(BF16).astype(F32)
        lane = lax.broadcasted_iota(jnp.int32, (total, LANES), 1)
        expert = expert_ref[0]
        score = jnp.where(lane == expert, first, jnp.where(lane == expert + groups, score - first, 0.0)).astype(BF16)
        forth = (gate[:, :1] * dot_nt(hidden, out_ref[...])).astype(BF16)
        back = dot_nt(pair_ref[...], in_ref[...]).astype(BF16)
        start = 0
        for piece in range(number):
            count = put[piece].shape[1]
            place = put[piece][...]
            to, down = targets[piece]
            for rows, at in ((forth, 0), (back, half), (score, 2 * half)):
                rows = dot_nn(place, rows[start : start + count, :]).astype(BF16)
                outs[to][down : down + rows.shape[0], at : at + rows.shape[1]] = rows
            start += count

    shape = jax.ShapeDtypeStruct
    outs = [shape((total, hidden_units), BF16), shape((total, columns), BF16), shape((8, LANES), F32)]
    outs += [shape((height, 2 * half + LANES), BF16) for height in heights]
    got = run(kernel, outs, [expert, own, came, gate, weight_in, weight_out, *places], 1)
    return got[0], got[1], got[2], got[3:]


def ring_pairs(groups):
    chips = groups // 2
    levels = chips // 2
    order = [2 * z for z in range(levels)] + [2 * z + 1 for z in reversed(range(levels))]
    forward = []
    for place in range(chips):
        forward.append((2 * order[place], 2 * order[(place + 1) % chips]))
        forward.append((2 * order[(place + 1) % chips] + 1, 2 * order[place] + 1))
    backward = [(to, source) for source, to in forward]
    cores = [(index, index ^ 1) for index in range(groups)]
    return forward, backward, cores


def swap_pair(value):
    return lax.ppermute(value, "dp", [(0, 1), (1, 0)])


def swap_both(value):
    groups = lax.axis_size("expert")
    pairs = [(2 * e + r, 2 * (e ^ 1) + 1 - r) for e in range(groups) for r in range(2)]
    return lax.ppermute(value, ("expert", "dp"), pairs)


def by_replica(own, other, replica):
    return jnp.where(replica == 0, jnp.stack([own, other]), jnp.stack([other, own]))


def after(value, *anchors):
    anywhere = pl.BlockSpec(memory_space=pl.ANY)
    return pl.pallas_call(
        lambda *refs: None,
        out_shape=jax.ShapeDtypeStruct(value.shape, value.dtype),
        in_specs=[anywhere] * (1 + len(anchors)),
        out_specs=anywhere,
        input_output_aliases={0: 0},
        compiler_params=pltpu.CompilerParams(vmem_limit_bytes=1024 * 1024),
        cost_estimate=FREE,
    )(value, *anchors)


class Order:
    def __init__(self):
        self.last = None

    def __call__(self, value, *anchors):
        if self.last is not None:
            value = after(value, self.last, *anchors)
        self.last = value
        return value


def body_by_width(tokens, route_ids, gates, cotangent, w_gate_up, w_down):
    tok_dev, model_width = tokens.shape
    top_count = route_ids.shape[1]
    groups = lax.axis_size("expert")
    replica = lax.axis_index("dp")
    expert = lax.axis_index("expert").astype(jnp.int32).reshape(1)
    half = w_gate_up.shape[1]
    capacity = slot_capacity(tok_dev, top_count, groups)
    steps = groups // 4
    weight_in, weight_out = w_gate_up[0], w_down[0]
    forward, backward, cores = ring_pairs(groups)
    unit = 2 * tok_dev

    def swap_cores(value):
        return lax.ppermute(value, "expert", cores)

    def products(pieces):
        *kept, own, send, places = partial_products(
            pieces, weight_in, weight_out, expert, groups, tok_dev, capacity
        )
        return [kept, own, send, places, swap_pair(send)]

    def ring(block, step):
        return lax.ppermute(block if step < steps else block[:tok_dev], "expert", forward)

    order = Order()
    keep, send = prepare(tokens, route_ids.T, gates.T, cotangent, replica.astype(jnp.int32).reshape(1), groups)
    second = jnp.concatenate([order(swap_pair(send)), order(swap_both(send))], axis=0)
    first = jnp.concatenate([keep, order(swap_cores(keep))], axis=0)
    chunks = [products([first, second])]

    def wait_for(number):
        chunks[number][4] = order(chunks[number][4], chunks[-1][0][2])

    for step in range(1, steps + 1):
        if step == 2 or step == steps:
            wait_for(step - 2)
        first = order(ring(first, step), chunks[-1][0][2])
        if 3 <= step < steps:
            wait_for(step - 2)
        second = order(ring(second, step))
        first_other, second_other = swap_cores(first), order(swap_cores(second))
        chunks.append(products([first, first_other, second, second_other]))

    terms, grads, swapped = ([], []), [], []
    for number, ((x_rows, grad_rows, gate), own, _, places, came) in enumerate(chunks):
        if number == steps:
            came = order(came)
        elif number == steps - 1:
            came = order(came, flag, chunks[-1][0][2])
        elif number == steps - 2:
            came = after(came, flag, chunks[-1][0][2])
        elif number:
            came = after(came, flag)
        hidden, pair_grad, flag, out = expert_rows(own, came, gate, places, weight_in, weight_out, expert, groups)
        for stream in range(2):
            terms[stream].append([out[stream]])
        if number:
            swapped.append(swap_cores(out[2]))
        grads.append((x_rows, pair_grad, grad_rows, hidden))

    for number, other in enumerate(swapped, 1):
        half_way = other.shape[0] // 2
        terms[0][number].append(other[:half_way])
        terms[1][number].append(after(other[half_way:], flag))

    def pop_term(stream):
        return sum(term.astype(F32) for term in terms[stream].pop())

    totals = [pop_term(0), pop_term(1)]
    for step in reversed(range(steps)):
        for stream in (1, 0):
            came = lax.ppermute(totals[stream].astype(BF16), "expert", backward)
            if step == steps - 3 and stream == 1:
                came = after(came, grad_gate_up, grad_down)
            if step == steps - 2 and stream == 1:
                grads[0] = tuple(after(array, came) for array in grads[0])
                grad_gate_up, grad_down = outer_products(grads, 0, 1), outer_products(grads, 2, 3)
            base = pop_term(stream)
            if came.shape[0] < unit:
                totals[stream] = jnp.concatenate([base[:tok_dev] + came.astype(F32), base[tok_dev:]], axis=0)
            else:
                totals[stream] = base + came.astype(F32)

    there = totals[1][:, : 2 * half].astype(BF16)
    kept = totals[0][:tok_dev], swap_cores(totals[0][tok_dev:].astype(BF16))
    scores = kept[0][:, 2 * half :] + kept[1][:, 2 * half :].astype(F32)
    scores = scores[:, :groups] + scores[:, groups : 2 * groups]
    named = route_ids[:, :, None] == jnp.arange(groups, dtype=jnp.int32)[None, None, :]
    grad_gates = jnp.sum(jnp.where(named, scores[:, None, :], 0.0), axis=2)
    other = swap_pair(there[:tok_dev]), after(swap_both(there[tok_dev:]), scores)
    mixed, grad_tokens = join_halves(kept, other, half, replica.astype(jnp.int32).reshape(1))
    return (mixed, grad_tokens, grad_gates, grad_gate_up, grad_down)


def join_halves(kept, other, half, replica):
    rows = kept[0].shape[0]

    def kernel(replica_ref, mine_ref, beside_ref, across_ref, diagonal_ref, *outs):
        low = replica_ref[0] == 0
        for number, out in enumerate(outs):
            at = slice(number * half, (number + 1) * half)
            here = mine_ref[:, at] + beside_ref[:, at].astype(F32)
            there = across_ref[:, at].astype(F32) + diagonal_ref[:, at].astype(F32)
            out[:, :half] = jnp.where(low, here, there).astype(BF16)
            out[:, half:] = jnp.where(low, there, here).astype(BF16)

    out = jax.ShapeDtypeStruct((rows, 2 * half), BF16)
    return run(kernel, [out, out], [replica, *kept, *other], 1)


def outer_products(chunks, left, right):
    left = jnp.concatenate([chunk[left] for chunk in chunks])
    right = jnp.concatenate([chunk[right] for chunk in chunks])
    return lax.dot_general(left, right, (((0,), (0,)), ((), ())), preferred_element_type=F32).astype(BF16)[None]


def slot_capacity(tok_dev, top_count, experts):
    assignments = tok_dev * top_count
    return min(tok_dev, max(2, assignments // experts + max(1, assignments // (3 * experts))))


def body(tokens, route_ids, gates, cotangent, w_gate_up, w_down):
    groups, replicas = lax.axis_size("expert"), lax.axis_size("dp")
    gathered = 2 * groups * tokens.shape[0] * replicas * w_gate_up.shape[1] * 2
    small = gathered <= 8 * 1024 * 1024 and 3 * groups <= 128 and groups % 4 == 0 and groups >= 16
    if replicas == 2 and w_gate_up.shape[0] == 1 and small:
        return body_by_width(tokens, route_ids, gates, cotangent, w_gate_up, w_down)
    return body_by_slots(tokens, route_ids, gates, cotangent, w_gate_up, w_down)


def solution(mesh):
    placed = (
        P(("expert", "dp"), None),
        P(("expert", "dp"), None),
        P(("expert", "dp"), None),
        P(("expert", "dp"), None),
        P("expert", "dp", None),
        P("expert", "dp", None),
    )
    return jax.shard_map(
        body,
        mesh=mesh,
        in_specs=placed,
        out_specs=(
            P(("expert", "dp"), None),
            P(("expert", "dp"), None),
            P(("expert", "dp"), None),
            P("expert", "dp", None),
            P("expert", "dp", None),
        ),
        check_vma=False,
    )
```

```python
import jax
import jax.numpy as jnp
from jax import lax
from jax.experimental import pallas as pl
from jax.experimental.pallas import tpu as pltpu
from jax.sharding import PartitionSpec as P


def expert_forward(x_rows, weight_in, weight_out, hidden_units):
    pre_act = jnp.dot(x_rows, weight_in, preferred_element_type=jnp.float32)
    gate_pre = pre_act[:, :hidden_units]
    up_pre = pre_act[:, hidden_units:]
    sigmoid_gate = jax.nn.sigmoid(gate_pre)
    activation = gate_pre * sigmoid_gate
    hidden = (activation * up_pre).astype(jnp.bfloat16)
    expert_out = lax.dot_general(
        hidden, weight_out, (((1,), (1,)), ((), ())), preferred_element_type=jnp.float32
    ).astype(jnp.bfloat16)
    return (gate_pre, up_pre, sigmoid_gate, activation, hidden, expert_out)


def expert_backward(saved, grad_rows, weight_in, weight_out):
    gate_pre, up_pre, sigmoid_gate, activation, hidden, expert_out = saved
    hidden_grad = jnp.dot(grad_rows, weight_out, preferred_element_type=jnp.float32)
    gate_grad = (
        hidden_grad * up_pre * (sigmoid_gate * (1.0 + gate_pre * (1.0 - sigmoid_gate)))
    ).astype(jnp.bfloat16)
    up_grad = (hidden_grad * activation).astype(jnp.bfloat16)
    pair_grad = jnp.concatenate([gate_grad, up_grad], axis=1)
    input_grad = lax.dot_general(
        pair_grad, weight_in, (((1,), (1,)), ((), ())), preferred_element_type=jnp.float32
    ).astype(jnp.bfloat16)
    return (pair_grad, input_grad)


def outer_blocks(left, right, pieces):
    span = left.shape[1] // pieces
    results = []
    for piece in range(pieces):
        product = lax.dot_general(
            left[:, piece * span : (piece + 1) * span],
            right,
            (((0,), (0,)), ((), ())),
            preferred_element_type=jnp.float32,
        )
        results.append(product.astype(jnp.bfloat16))
    return jnp.stack(results, axis=0)


def replica_total(received):
    return jnp.sum(received.astype(jnp.float32), axis=0).astype(jnp.bfloat16)


def body_by_slots(tokens, route_ids, gates, cotangent, w_gate_up, w_down):
    tok_dev, model_width = tokens.shape
    top_count = route_ids.shape[1]
    groups = lax.axis_size("expert")
    replicas = lax.axis_size("dp")
    local_experts = w_gate_up.shape[0]
    hidden_units = w_down.shape[2]
    experts = groups * local_experts
    assignments = tok_dev * top_count
    capacity = min(tok_dev, max(2, assignments // experts + max(1, assignments // (3 * experts))))
    flat_ids = route_ids.reshape(assignments)
    onehot = (flat_ids[:, None] == jnp.arange(experts, dtype=jnp.int32)[None, :]).astype(jnp.int32)
    earlier = jnp.sum(
        (jnp.cumsum(onehot, axis=0, dtype=jnp.int32) - onehot) * onehot, axis=1, dtype=jnp.int32
    )
    position = flat_ids * capacity + earlier
    source = (
        jnp.full((experts * capacity,), assignments, jnp.int32)
        .at[position]
        .set(jnp.arange(assignments, dtype=jnp.int32))
    )
    token_row = source // top_count
    tok_pad = jnp.concatenate([tokens, jnp.zeros((1, model_width), jnp.bfloat16)], axis=0)
    cot_pad = jnp.concatenate([cotangent, jnp.zeros((1, model_width), jnp.bfloat16)], axis=0)
    gate_pad = jnp.concatenate([gates.reshape(assignments), jnp.zeros((1,), jnp.float32)], axis=0)
    send_rows = tok_pad[token_row].reshape(experts, capacity, model_width)
    send_grads = (gate_pad[source][:, None] * cot_pad[token_row].astype(jnp.float32)).astype(
        jnp.bfloat16
    )
    send_grads = send_grads.reshape(experts, capacity, model_width)
    weights_in, weights_out = (
        lax.all_gather(w_gate_up, "dp", axis=1, tiled=True),
        lax.all_gather(w_down, "dp", axis=1, tiled=True),
    )
    rows_in, grads_in = (
        lax.all_to_all(send_rows, "expert", split_axis=0, concat_axis=1, tiled=True),
        lax.all_to_all(send_grads, "expert", split_axis=0, concat_axis=1, tiled=True),
    )
    local = 0
    forward_parts = expert_forward(
        rows_in[local], weights_in[local], weights_out[local], hidden_units
    )
    saved_all = [forward_parts]
    out_list = [forward_parts[5]]
    down_list = [outer_blocks(grads_in[local], forward_parts[4], replicas)]
    expert_outs = jnp.stack(out_list, axis=0)
    down_stack = jnp.stack(down_list, axis=1)
    outs_back = lax.all_to_all(expert_outs, "expert", split_axis=1, concat_axis=0, tiled=True)
    local = 0
    pair_grad, input_grad = expert_backward(
        saved_all[local], grads_in[local], weights_in[local], weights_out[local]
    )
    input_list = [input_grad]
    gate_up_list = [outer_blocks(rows_in[local], pair_grad, replicas)]
    input_grads = jnp.stack(input_list, axis=0)
    gate_up_stack = jnp.stack(gate_up_list, axis=1)
    grads_back = lax.all_to_all(input_grads, "expert", split_axis=1, concat_axis=0, tiled=True)
    gate_up_received, down_received = (
        lax.all_to_all(gate_up_stack, "dp", split_axis=0, concat_axis=0, tiled=True),
        lax.all_to_all(down_stack, "dp", split_axis=0, concat_axis=0, tiled=True),
    )
    grad_gate_up = replica_total(gate_up_received)
    grad_down = replica_total(down_received)
    out_rows = outs_back.reshape(experts * capacity, model_width)[position].reshape(
        tok_dev, top_count, model_width
    )
    mixed = jnp.sum(gates[:, :, None] * out_rows.astype(jnp.float32), axis=1).astype(jnp.bfloat16)
    grad_gates = jnp.einsum("td,tkd->tk", cotangent, out_rows, preferred_element_type=jnp.float32)
    back_rows = grads_back.reshape(experts * capacity, model_width)[position].reshape(
        tok_dev, top_count, model_width
    )
    grad_tokens = jnp.sum(back_rows.astype(jnp.float32), axis=1).astype(jnp.bfloat16)
    return (mixed, grad_tokens, grad_gates, grad_gate_up, grad_down)


F32, BF16 = jnp.float32, jnp.bfloat16
LANES = 128
FREE = pl.CostEstimate(flops=0, bytes_accessed=0, transcendentals=0)


def run(kernel, outs, args, scalars=0):
    spaces = [pltpu.SMEM] * scalars + [pltpu.VMEM] * (len(args) - scalars)
    return pl.pallas_call(
        kernel,
        out_shape=outs,
        in_specs=[pl.BlockSpec(memory_space=space) for space in spaces],
        out_specs=[pl.BlockSpec(memory_space=pltpu.VMEM) for _ in outs],
        compiler_params=pltpu.CompilerParams(vmem_limit_bytes=10 * 1024 * 1024),
        cost_estimate=FREE,
    )(*args)


def dot_nn(left, right):
    return jnp.dot(left, right, preferred_element_type=F32)


def dot_nt(left, right):
    return lax.dot_general(left, right, (((1,), (1,)), ((), ())), preferred_element_type=F32)


def own_column(expert, groups):
    lane = lax.broadcasted_iota(jnp.int32, (1, LANES), 1)
    hit = (lane == expert) | (lane == expert + groups) | (lane == expert + 2 * groups)
    return jnp.where(hit, 1.0, 0.0)


def prepare(tokens, route_ids, gates, cotangent, replica, groups):
    rows, width = tokens.shape
    half = width // 2

    def kernel(replica_ref, tok_ref, id_ref, gate_ref, cot_ref, keep_ref, send_ref):
        low = replica_ref[0] == 0
        line = lax.broadcasted_iota(jnp.int32, (LANES, rows), 0)
        term = lax.div(line, groups)
        named = line - term * groups
        dense = jnp.zeros((LANES, rows), F32)
        for k in range(id_ref.shape[0]):
            dense = dense + jnp.where(id_ref[k : k + 1, :] == named, gate_ref[k : k + 1, :], 0.0)
        first = dense.astype(BF16).astype(F32)
        second = (dense - first).astype(BF16).astype(F32)
        third = dense - first - second
        meta = jnp.where(term == 0, first, jnp.where(term == 1, second, jnp.where(term == 2, third, 0.0))).astype(BF16)
        down = lax.broadcasted_iota(jnp.int32, (rows, rows), 0)
        along = lax.broadcasted_iota(jnp.int32, (rows, rows), 1)
        meta = dot_nt(jnp.where(down == along, 1.0, 0.0).astype(BF16), meta).astype(BF16)
        for ref, start in ((tok_ref, 0), (cot_ref, half + LANES)):
            left, right = ref[:, :half], ref[:, half:]
            keep_ref[:, start : start + half] = jnp.where(low, left, right)
            send_ref[:, start : start + half] = jnp.where(low, right, left)
        keep_ref[:, half : half + LANES] = meta
        send_ref[:, half : half + LANES] = meta

    out = jax.ShapeDtypeStruct((rows, width + LANES), BF16)
    args = [tokens, route_ids, gates, cotangent]
    return pl.pallas_call(
        kernel,
        grid=(1,),
        out_shape=[out, out],
        in_specs=[pl.BlockSpec(memory_space=pltpu.SMEM)] + [pl.BlockSpec(arg.shape, lambda i: (0, 0)) for arg in args],
        out_specs=[pl.BlockSpec(out.shape, lambda i: (0, 0))] * 2,
        compiler_params=pltpu.CompilerParams(vmem_limit_bytes=60 * 1024 * 1024),
        cost_estimate=FREE,
    )(replica, *args)


def partial_products(pieces, weight_in, weight_out, expert, groups, tok_dev, capacity):
    counts = [piece.shape[0] // tok_dev * capacity for piece in pieces]
    total, number = sum(counts), len(pieces)
    half, columns = weight_in.shape
    hidden_units = weight_out.shape[1]

    def kernel(expert_ref, *refs):
        rows_refs, refs = refs[:number], refs[number:]
        in_ref, out_ref, x_ref, grad_ref, gate_ref, own_ref, send_ref = refs[:7]
        places = refs[7:]
        column = own_column(expert_ref[0], groups)
        column_rows = jnp.broadcast_to(column, (8, LANES)).astype(BF16)
        start = 0
        for piece in range(number):
            rows, count = rows_refs[piece].shape[0], counts[piece]
            meta = rows_refs[piece][:, half : half + LANES]
            gate_row = dot_nt(column_rows, meta)
            gate_col = jnp.sum(meta.astype(F32) * column, axis=1, keepdims=True)
            down = lax.broadcasted_iota(jnp.int32, (rows, rows), 0)
            along = lax.broadcasted_iota(jnp.int32, (rows, rows), 1)
            first_down, first_along = jnp.zeros_like(down), jnp.zeros_like(along)
            base_down, base_along = jnp.zeros_like(down), jnp.zeros_like(along)
            for device in range(1, rows // tok_dev):
                first_down += jnp.where(down >= device * tok_dev, tok_dev, 0)
                first_along += jnp.where(along >= device * tok_dev, tok_dev, 0)
                base_down += jnp.where(down >= device * tok_dev, capacity, 0)
                base_along += jnp.where(along >= device * tok_dev, capacity, 0)
            lower = jnp.where((along < down) & (along >= first_down), 1.0, 0.0).astype(BF16)
            upper = jnp.where((down < along) & (down >= first_along), 1.0, 0.0).astype(BF16)
            on_row = jnp.where(gate_row > 0.0, 1.0, 0.0)
            on_col = jnp.where(gate_col > 0.0, 1.0, 0.0)
            rank_row = dot_nn(on_row.astype(BF16), upper)
            rank_col = dot_nn(lower, jnp.broadcast_to(on_col, (rows, LANES)).astype(BF16))
            place_row = jnp.where(on_row > 0.0, rank_row + base_along[:8].astype(F32), -1.0)[:1, :]
            place_col = jnp.where(on_col > 0.0, rank_col[:, :1] + base_down[:, :1].astype(F32), -1.0)
            slot_down = lax.broadcasted_iota(jnp.int32, (count, rows), 0).astype(F32)
            slot_along = lax.broadcasted_iota(jnp.int32, (rows, count), 1).astype(F32)
            pick = jnp.where(place_row == slot_down, 1.0, 0.0).astype(BF16)
            places[piece][...] = jnp.where(place_col == slot_along, 1.0, 0.0).astype(BF16)
            picked = dot_nn(pick, rows_refs[piece][...])
            x_ref[start : start + count, :] = picked[:, :half].astype(BF16)
            gate = jnp.sum(picked[:, half : half + LANES] * column, axis=1, keepdims=True)
            gate_ref[start : start + count, :] = jnp.broadcast_to(gate, (count, LANES))
            grad_ref[start : start + count, :] = (gate * picked[:, half + LANES :]).astype(BF16)
            start += count
        for left, right, at in ((x_ref, in_ref, 0), (grad_ref, out_ref, columns)):
            part = dot_nn(left[...], right[...])
            own_ref[:, at : at + part.shape[1]] = part
            part = part.astype(BF16)
            send_ref[: total // 2, at : at + part.shape[1]] = part[total // 2 :]
            send_ref[total // 2 :, at : at + part.shape[1]] = part[: total // 2]

    shape = jax.ShapeDtypeStruct
    outs = [shape((total, half), BF16), shape((total, half), BF16), shape((total, LANES), F32)]
    outs += [shape((total, columns + hidden_units), F32), shape((total, columns + hidden_units), BF16)]
    outs += [shape((piece.shape[0], count), BF16) for piece, count in zip(pieces, counts)]
    got = run(kernel, outs, [expert, *pieces, weight_in, weight_out], 1)
    return (*got[:5], got[5:])


def expert_rows(own, came, gate, places, weight_in, weight_out, expert, groups):
    total = own.shape[0]
    half, columns = weight_in.shape
    hidden_units, number = columns // 2, len(places)
    rows = places[0].shape[0]
    targets, heights = ([(0, 0), (2, 0), (1, 0), (2, rows)], [rows, rows, 2 * rows])
    if number == 2:
        targets, heights = [(0, 0), (1, 0)], [rows, rows]

    def kernel(expert_ref, own_ref, came_ref, gate_ref, in_ref, out_ref, *refs):
        put, hidden_ref, pair_ref, flag_ref, outs = refs[:number], *refs[number : number + 3], refs[number + 3 :]
        gate_pre = own_ref[:, :hidden_units] + came_ref[:, :hidden_units].astype(F32)
        up_pre = own_ref[:, hidden_units:columns] + came_ref[:, hidden_units:columns].astype(F32)
        hidden_grad = own_ref[:, columns:] + came_ref[:, columns:].astype(F32)
        sig = jax.nn.sigmoid(gate_pre)
        act = gate_pre * sig
        hidden = (act * up_pre).astype(BF16)
        hidden_ref[...] = hidden
        pair_ref[:, :hidden_units] = (hidden_grad * up_pre * (sig * (1.0 + gate_pre * (1.0 - sig)))).astype(BF16)
        pair_ref[:, hidden_units:] = (hidden_grad * act).astype(BF16)
        gate = gate_ref[...]
        flag_ref[...] = gate[:8]
        score = jnp.sum(hidden.astype(F32) * hidden_grad, axis=1, keepdims=True)
        score = score / jnp.where(gate > 0.0, gate, 1.0)
        first = score.astype(BF16).astype(F32)
        lane = lax.broadcasted_iota(jnp.int32, (total, LANES), 1)
        expert = expert_ref[0]
        score = jnp.where(lane == expert, first, jnp.where(lane == expert + groups, score - first, 0.0)).astype(BF16)
        forth = (gate[:, :1] * dot_nt(hidden, out_ref[...])).astype(BF16)
        back = dot_nt(pair_ref[...], in_ref[...]).astype(BF16)
        start = 0
        for piece in range(number):
            count = put[piece].shape[1]
            place = put[piece][...]
            to, down = targets[piece]
            for rows, at in ((forth, 0), (back, half), (score, 2 * half)):
                rows = dot_nn(place, rows[start : start + count, :]).astype(BF16)
                outs[to][down : down + rows.shape[0], at : at + rows.shape[1]] = rows
            start += count

    shape = jax.ShapeDtypeStruct
    outs = [shape((total, hidden_units), BF16), shape((total, columns), BF16), shape((8, LANES), F32)]
    outs += [shape((height, 2 * half + LANES), BF16) for height in heights]
    got = run(kernel, outs, [expert, own, came, gate, weight_in, weight_out, *places], 1)
    return got[0], got[1], got[2], got[3:]


def ring_pairs(groups):
    chips = groups // 2
    levels = chips // 2
    order = [2 * z for z in range(levels)] + [2 * z + 1 for z in reversed(range(levels))]
    forward = []
    for place in range(chips):
        forward.append((2 * order[place], 2 * order[(place + 1) % chips]))
        forward.append((2 * order[(place + 1) % chips] + 1, 2 * order[place] + 1))
    backward = [(to, source) for source, to in forward]
    cores = [(index, index ^ 1) for index in range(groups)]
    return forward, backward, cores


def swap_pair(value):
    return lax.ppermute(value, "dp", [(0, 1), (1, 0)])


def swap_both(value):
    groups = lax.axis_size("expert")
    pairs = [(2 * e + r, 2 * (e ^ 1) + 1 - r) for e in range(groups) for r in range(2)]
    return lax.ppermute(value, ("expert", "dp"), pairs)


def by_replica(own, other, replica):
    return jnp.where(replica == 0, jnp.stack([own, other]), jnp.stack([other, own]))


def after(value, *anchors):
    anywhere = pl.BlockSpec(memory_space=pl.ANY)
    return pl.pallas_call(
        lambda *refs: None,
        out_shape=jax.ShapeDtypeStruct(value.shape, value.dtype),
        in_specs=[anywhere] * (1 + len(anchors)),
        out_specs=anywhere,
        input_output_aliases={0: 0},
        compiler_params=pltpu.CompilerParams(vmem_limit_bytes=1024 * 1024),
        cost_estimate=FREE,
    )(value, *anchors)


class Order:
    def __init__(self):
        self.last = None

    def __call__(self, value, *anchors):
        if self.last is not None:
            value = after(value, self.last, *anchors)
        self.last = value
        return value


def body_by_width(tokens, route_ids, gates, cotangent, w_gate_up, w_down):
    tok_dev, model_width = tokens.shape
    top_count = route_ids.shape[1]
    groups = lax.axis_size("expert")
    replica = lax.axis_index("dp")
    expert = lax.axis_index("expert").astype(jnp.int32).reshape(1)
    half = w_gate_up.shape[1]
    capacity = slot_capacity(tok_dev, top_count, groups)
    steps = groups // 4
    weight_in, weight_out = w_gate_up[0], w_down[0]
    forward, backward, cores = ring_pairs(groups)
    unit = 2 * tok_dev

    def swap_cores(value):
        return lax.ppermute(value, "expert", cores)

    def products(pieces):
        *kept, own, send, places = partial_products(
            pieces, weight_in, weight_out, expert, groups, tok_dev, capacity
        )
        return [kept, own, send, places, swap_pair(send)]

    def ring(block, step):
        return lax.ppermute(block if step < steps else block[:tok_dev], "expert", forward)

    order = Order()
    keep, send = prepare(tokens, route_ids.T, gates.T, cotangent, replica.astype(jnp.int32).reshape(1), groups)
    beside = order(swap_cores(keep))
    first = jnp.concatenate([keep, beside], axis=0)
    second = jnp.concatenate([order(swap_pair(send)), order(swap_both(send))], axis=0)
    chunks = [products([first, second])]

    def wait_for(number):
        chunks[number][4] = order(chunks[number][4], chunks[-1][0][2])

    for step in range(1, steps + 1):
        if step == 2 or step == steps:
            wait_for(step - 2)
        first = order(ring(first, step), chunks[-1][0][2])
        if 3 <= step < steps:
            wait_for(step - 2)
        second = order(ring(second, step))
        first_other, second_other = swap_cores(first), order(swap_cores(second))
        chunks.append(products([first, first_other, second, second_other]))

    terms, grads, swapped = ([], []), [], []
    for number, ((x_rows, grad_rows, gate), own, _, places, came) in enumerate(chunks):
        if number == steps:
            came = order(came)
        elif number == steps - 1:
            came = order(came, flag, chunks[-1][0][2])
        elif number == steps - 2:
            came = after(came, flag, chunks[-1][0][2])
        elif number:
            came = after(came, flag)
        hidden, pair_grad, flag, out = expert_rows(own, came, gate, places, weight_in, weight_out, expert, groups)
        for stream in range(2):
            terms[stream].append([out[stream]])
        if number:
            swapped.append(swap_cores(out[2]))
        grads.append((x_rows, pair_grad, grad_rows, hidden))

    for number, other in enumerate(swapped, 1):
        half_way = other.shape[0] // 2
        terms[0][number].append(other[:half_way])
        terms[1][number].append(after(other[half_way:], flag))

    def pop_term(stream):
        return sum(term.astype(F32) for term in terms[stream].pop())

    totals = [pop_term(0), pop_term(1)]
    for step in reversed(range(steps)):
        for stream in (1, 0):
            came = lax.ppermute(totals[stream].astype(BF16), "expert", backward)
            if step == steps - 3 and stream == 1:
                came = after(came, grad_gate_up, grad_down)
            if step == steps - 2 and stream == 1:
                grads[0] = tuple(after(array, came) for array in grads[0])
                grad_gate_up, grad_down = outer_products(grads, 0, 1), outer_products(grads, 2, 3)
            base = pop_term(stream)
            if came.shape[0] < unit:
                totals[stream] = jnp.concatenate([base[:tok_dev] + came.astype(F32), base[tok_dev:]], axis=0)
            else:
                totals[stream] = base + came.astype(F32)

    there = totals[1][:, : 2 * half].astype(BF16)
    kept = totals[0][:tok_dev], swap_cores(totals[0][tok_dev:].astype(BF16))
    scores = kept[0][:, 2 * half :] + kept[1][:, 2 * half :].astype(F32)
    scores = scores[:, :groups] + scores[:, groups : 2 * groups]
    named = route_ids[:, :, None] == jnp.arange(groups, dtype=jnp.int32)[None, None, :]
    grad_gates = jnp.sum(jnp.where(named, scores[:, None, :], 0.0), axis=2)
    other = swap_pair(there[:tok_dev]), after(swap_both(there[tok_dev:]), scores)
    mixed, grad_tokens = join_halves(kept, other, half, replica.astype(jnp.int32).reshape(1))
    return (mixed, grad_tokens, grad_gates, grad_gate_up, grad_down)


def join_halves(kept, other, half, replica):
    rows = kept[0].shape[0]

    def kernel(replica_ref, mine_ref, beside_ref, across_ref, diagonal_ref, *outs):
        low = replica_ref[0] == 0
        for number, out in enumerate(outs):
            at = slice(number * half, (number + 1) * half)
            here = mine_ref[:, at] + beside_ref[:, at].astype(F32)
            there = across_ref[:, at].astype(F32) + diagonal_ref[:, at].astype(F32)
            out[:, :half] = jnp.where(low, here, there).astype(BF16)
            out[:, half:] = jnp.where(low, there, here).astype(BF16)

    out = jax.ShapeDtypeStruct((rows, 2 * half), BF16)
    return run(kernel, [out, out], [replica, *kept, *other], 1)


def outer_products(chunks, left, right):
    left = jnp.concatenate([chunk[left] for chunk in chunks])
    right = jnp.concatenate([chunk[right] for chunk in chunks])
    return lax.dot_general(left, right, (((0,), (0,)), ((), ())), preferred_element_type=F32).astype(BF16)[None]


def slot_capacity(tok_dev, top_count, experts):
    assignments = tok_dev * top_count
    return min(tok_dev, max(2, assignments // experts + max(1, assignments // (3 * experts))))


def body(tokens, route_ids, gates, cotangent, w_gate_up, w_down):
    groups, replicas = lax.axis_size("expert"), lax.axis_size("dp")
    gathered = 2 * groups * tokens.shape[0] * replicas * w_gate_up.shape[1] * 2
    small = gathered <= 8 * 1024 * 1024 and 3 * groups <= 128 and groups % 4 == 0 and groups >= 16
    if replicas == 2 and w_gate_up.shape[0] == 1 and small:
        return body_by_width(tokens, route_ids, gates, cotangent, w_gate_up, w_down)
    return body_by_slots(tokens, route_ids, gates, cotangent, w_gate_up, w_down)


def solution(mesh):
    placed = (
        P(("expert", "dp"), None),
        P(("expert", "dp"), None),
        P(("expert", "dp"), None),
        P(("expert", "dp"), None),
        P("expert", "dp", None),
        P("expert", "dp", None),
    )
    return jax.shard_map(
        body,
        mesh=mesh,
        in_specs=placed,
        out_specs=(
            P(("expert", "dp"), None),
            P(("expert", "dp"), None),
            P(("expert", "dp"), None),
            P("expert", "dp", None),
            P("expert", "dp", None),
        ),
        check_vma=False,
    )
```

```python
import jax
import jax.numpy as jnp
from jax import lax
from jax.experimental import pallas as pl
from jax.experimental.pallas import tpu as pltpu
from jax.sharding import PartitionSpec as P


def expert_forward(x_rows, weight_in, weight_out, hidden_units):
    pre_act = jnp.dot(x_rows, weight_in, preferred_element_type=jnp.float32)
    gate_pre = pre_act[:, :hidden_units]
    up_pre = pre_act[:, hidden_units:]
    sigmoid_gate = jax.nn.sigmoid(gate_pre)
    activation = gate_pre * sigmoid_gate
    hidden = (activation * up_pre).astype(jnp.bfloat16)
    expert_out = lax.dot_general(
        hidden, weight_out, (((1,), (1,)), ((), ())), preferred_element_type=jnp.float32
    ).astype(jnp.bfloat16)
    return (gate_pre, up_pre, sigmoid_gate, activation, hidden, expert_out)


def expert_backward(saved, grad_rows, weight_in, weight_out):
    gate_pre, up_pre, sigmoid_gate, activation, hidden, expert_out = saved
    hidden_grad = jnp.dot(grad_rows, weight_out, preferred_element_type=jnp.float32)
    gate_grad = (
        hidden_grad * up_pre * (sigmoid_gate * (1.0 + gate_pre * (1.0 - sigmoid_gate)))
    ).astype(jnp.bfloat16)
    up_grad = (hidden_grad * activation).astype(jnp.bfloat16)
    pair_grad = jnp.concatenate([gate_grad, up_grad], axis=1)
    input_grad = lax.dot_general(
        pair_grad, weight_in, (((1,), (1,)), ((), ())), preferred_element_type=jnp.float32
    ).astype(jnp.bfloat16)
    return (pair_grad, input_grad)


def outer_blocks(left, right, pieces):
    span = left.shape[1] // pieces
    results = []
    for piece in range(pieces):
        product = lax.dot_general(
            left[:, piece * span : (piece + 1) * span],
            right,
            (((0,), (0,)), ((), ())),
            preferred_element_type=jnp.float32,
        )
        results.append(product.astype(jnp.bfloat16))
    return jnp.stack(results, axis=0)


def replica_total(received):
    return jnp.sum(received.astype(jnp.float32), axis=0).astype(jnp.bfloat16)


def body_by_slots(tokens, route_ids, gates, cotangent, w_gate_up, w_down):
    tok_dev, model_width = tokens.shape
    top_count = route_ids.shape[1]
    groups = lax.axis_size("expert")
    replicas = lax.axis_size("dp")
    local_experts = w_gate_up.shape[0]
    hidden_units = w_down.shape[2]
    experts = groups * local_experts
    assignments = tok_dev * top_count
    capacity = min(tok_dev, max(2, assignments // experts + max(1, assignments // (3 * experts))))
    flat_ids = route_ids.reshape(assignments)
    onehot = (flat_ids[:, None] == jnp.arange(experts, dtype=jnp.int32)[None, :]).astype(jnp.int32)
    earlier = jnp.sum(
        (jnp.cumsum(onehot, axis=0, dtype=jnp.int32) - onehot) * onehot, axis=1, dtype=jnp.int32
    )
    position = flat_ids * capacity + earlier
    source = (
        jnp.full((experts * capacity,), assignments, jnp.int32)
        .at[position]
        .set(jnp.arange(assignments, dtype=jnp.int32))
    )
    token_row = source // top_count
    tok_pad = jnp.concatenate([tokens, jnp.zeros((1, model_width), jnp.bfloat16)], axis=0)
    cot_pad = jnp.concatenate([cotangent, jnp.zeros((1, model_width), jnp.bfloat16)], axis=0)
    gate_pad = jnp.concatenate([gates.reshape(assignments), jnp.zeros((1,), jnp.float32)], axis=0)
    send_rows = tok_pad[token_row].reshape(experts, capacity, model_width)
    send_grads = (gate_pad[source][:, None] * cot_pad[token_row].astype(jnp.float32)).astype(
        jnp.bfloat16
    )
    send_grads = send_grads.reshape(experts, capacity, model_width)
    weights_in, weights_out = (
        lax.all_gather(w_gate_up, "dp", axis=1, tiled=True),
        lax.all_gather(w_down, "dp", axis=1, tiled=True),
    )
    rows_in, grads_in = (
        lax.all_to_all(send_rows, "expert", split_axis=0, concat_axis=1, tiled=True),
        lax.all_to_all(send_grads, "expert", split_axis=0, concat_axis=1, tiled=True),
    )
    local = 0
    forward_parts = expert_forward(
        rows_in[local], weights_in[local], weights_out[local], hidden_units
    )
    saved_all = [forward_parts]
    out_list = [forward_parts[5]]
    down_list = [outer_blocks(grads_in[local], forward_parts[4], replicas)]
    expert_outs = jnp.stack(out_list, axis=0)
    down_stack = jnp.stack(down_list, axis=1)
    outs_back = lax.all_to_all(expert_outs, "expert", split_axis=1, concat_axis=0, tiled=True)
    local = 0
    pair_grad, input_grad = expert_backward(
        saved_all[local], grads_in[local], weights_in[local], weights_out[local]
    )
    input_list = [input_grad]
    gate_up_list = [outer_blocks(rows_in[local], pair_grad, replicas)]
    input_grads = jnp.stack(input_list, axis=0)
    gate_up_stack = jnp.stack(gate_up_list, axis=1)
    grads_back = lax.all_to_all(input_grads, "expert", split_axis=1, concat_axis=0, tiled=True)
    gate_up_received, down_received = (
        lax.all_to_all(gate_up_stack, "dp", split_axis=0, concat_axis=0, tiled=True),
        lax.all_to_all(down_stack, "dp", split_axis=0, concat_axis=0, tiled=True),
    )
    grad_gate_up = replica_total(gate_up_received)
    grad_down = replica_total(down_received)
    out_rows = outs_back.reshape(experts * capacity, model_width)[position].reshape(
        tok_dev, top_count, model_width
    )
    mixed = jnp.sum(gates[:, :, None] * out_rows.astype(jnp.float32), axis=1).astype(jnp.bfloat16)
    grad_gates = jnp.einsum("td,tkd->tk", cotangent, out_rows, preferred_element_type=jnp.float32)
    back_rows = grads_back.reshape(experts * capacity, model_width)[position].reshape(
        tok_dev, top_count, model_width
    )
    grad_tokens = jnp.sum(back_rows.astype(jnp.float32), axis=1).astype(jnp.bfloat16)
    return (mixed, grad_tokens, grad_gates, grad_gate_up, grad_down)


F32, BF16 = jnp.float32, jnp.bfloat16
LANES = 128
FREE = pl.CostEstimate(flops=0, bytes_accessed=0, transcendentals=0)


def run(kernel, outs, args, scalars=0):
    spaces = [pltpu.SMEM] * scalars + [pltpu.VMEM] * (len(args) - scalars)
    return pl.pallas_call(
        kernel,
        out_shape=outs,
        in_specs=[pl.BlockSpec(memory_space=space) for space in spaces],
        out_specs=[pl.BlockSpec(memory_space=pltpu.VMEM) for _ in outs],
        compiler_params=pltpu.CompilerParams(vmem_limit_bytes=10 * 1024 * 1024),
        cost_estimate=FREE,
    )(*args)


def dot_nn(left, right):
    return jnp.dot(left, right, preferred_element_type=F32)


def dot_nt(left, right):
    return lax.dot_general(left, right, (((1,), (1,)), ((), ())), preferred_element_type=F32)


def own_column(expert, groups):
    lane = lax.broadcasted_iota(jnp.int32, (1, LANES), 1)
    hit = (lane == expert) | (lane == expert + groups) | (lane == expert + 2 * groups)
    return jnp.where(hit, 1.0, 0.0)


def prepare(tokens, route_ids, gates, cotangent, replica, groups):
    rows, width = tokens.shape
    half = width // 2

    def kernel(replica_ref, tok_ref, id_ref, gate_ref, cot_ref, keep_ref, send_ref):
        low = replica_ref[0] == 0
        line = lax.broadcasted_iota(jnp.int32, (LANES, rows), 0)
        term = lax.div(line, groups)
        named = line - term * groups
        dense = jnp.zeros((LANES, rows), F32)
        for k in range(id_ref.shape[0]):
            dense = dense + jnp.where(id_ref[k : k + 1, :] == named, gate_ref[k : k + 1, :], 0.0)
        first = dense.astype(BF16).astype(F32)
        second = (dense - first).astype(BF16).astype(F32)
        third = dense - first - second
        meta = jnp.where(term == 0, first, jnp.where(term == 1, second, jnp.where(term == 2, third, 0.0))).astype(BF16)
        down = lax.broadcasted_iota(jnp.int32, (rows, rows), 0)
        along = lax.broadcasted_iota(jnp.int32, (rows, rows), 1)
        meta = dot_nt(jnp.where(down == along, 1.0, 0.0).astype(BF16), meta).astype(BF16)
        for ref, start in ((tok_ref, 0), (cot_ref, half + LANES)):
            left, right = ref[:, :half], ref[:, half:]
            keep_ref[:, start : start + half] = jnp.where(low, left, right)
            send_ref[:, start : start + half] = jnp.where(low, right, left)
        keep_ref[:, half : half + LANES] = meta
        send_ref[:, half : half + LANES] = meta

    out = jax.ShapeDtypeStruct((rows, width + LANES), BF16)
    args = [tokens, route_ids, gates, cotangent]
    return pl.pallas_call(
        kernel,
        grid=(1,),
        out_shape=[out, out],
        in_specs=[pl.BlockSpec(memory_space=pltpu.SMEM)] + [pl.BlockSpec(arg.shape, lambda i: (0, 0)) for arg in args],
        out_specs=[pl.BlockSpec(out.shape, lambda i: (0, 0))] * 2,
        compiler_params=pltpu.CompilerParams(vmem_limit_bytes=60 * 1024 * 1024),
        cost_estimate=FREE,
    )(replica, *args)


def partial_products(pieces, weight_in, weight_out, expert, groups, tok_dev, capacity):
    counts = [piece.shape[0] // tok_dev * capacity for piece in pieces]
    total, number = sum(counts), len(pieces)
    half, columns = weight_in.shape
    hidden_units = weight_out.shape[1]

    def kernel(expert_ref, *refs):
        rows_refs, refs = refs[:number], refs[number:]
        in_ref, out_ref, x_ref, grad_ref, gate_ref, own_ref, send_ref = refs[:7]
        places = refs[7:]
        column = own_column(expert_ref[0], groups)
        column_rows = jnp.broadcast_to(column, (8, LANES)).astype(BF16)
        start = 0
        for piece in range(number):
            rows, count = rows_refs[piece].shape[0], counts[piece]
            meta = rows_refs[piece][:, half : half + LANES]
            gate_row = dot_nt(column_rows, meta)
            gate_col = jnp.sum(meta.astype(F32) * column, axis=1, keepdims=True)
            down = lax.broadcasted_iota(jnp.int32, (rows, rows), 0)
            along = lax.broadcasted_iota(jnp.int32, (rows, rows), 1)
            first_down, first_along = jnp.zeros_like(down), jnp.zeros_like(along)
            base_down, base_along = jnp.zeros_like(down), jnp.zeros_like(along)
            for device in range(1, rows // tok_dev):
                first_down += jnp.where(down >= device * tok_dev, tok_dev, 0)
                first_along += jnp.where(along >= device * tok_dev, tok_dev, 0)
                base_down += jnp.where(down >= device * tok_dev, capacity, 0)
                base_along += jnp.where(along >= device * tok_dev, capacity, 0)
            lower = jnp.where((along < down) & (along >= first_down), 1.0, 0.0).astype(BF16)
            upper = jnp.where((down < along) & (down >= first_along), 1.0, 0.0).astype(BF16)
            on_row = jnp.where(gate_row > 0.0, 1.0, 0.0)
            on_col = jnp.where(gate_col > 0.0, 1.0, 0.0)
            rank_row = dot_nn(on_row.astype(BF16), upper)
            rank_col = dot_nn(lower, jnp.broadcast_to(on_col, (rows, LANES)).astype(BF16))
            place_row = jnp.where(on_row > 0.0, rank_row + base_along[:8].astype(F32), -1.0)[:1, :]
            place_col = jnp.where(on_col > 0.0, rank_col[:, :1] + base_down[:, :1].astype(F32), -1.0)
            slot_down = lax.broadcasted_iota(jnp.int32, (count, rows), 0).astype(F32)
            slot_along = lax.broadcasted_iota(jnp.int32, (rows, count), 1).astype(F32)
            pick = jnp.where(place_row == slot_down, 1.0, 0.0).astype(BF16)
            places[piece][...] = jnp.where(place_col == slot_along, 1.0, 0.0).astype(BF16)
            picked = dot_nn(pick, rows_refs[piece][...])
            x_ref[start : start + count, :] = picked[:, :half].astype(BF16)
            gate = jnp.sum(picked[:, half : half + LANES] * column, axis=1, keepdims=True)
            gate_ref[start : start + count, :] = jnp.broadcast_to(gate, (count, LANES))
            grad_ref[start : start + count, :] = (gate * picked[:, half + LANES :]).astype(BF16)
            start += count
        for left, right, at in ((x_ref, in_ref, 0), (grad_ref, out_ref, columns)):
            part = dot_nn(left[...], right[...])
            own_ref[:, at : at + part.shape[1]] = part
            part = part.astype(BF16)
            send_ref[: total // 2, at : at + part.shape[1]] = part[total // 2 :]
            send_ref[total // 2 :, at : at + part.shape[1]] = part[: total // 2]

    shape = jax.ShapeDtypeStruct
    outs = [shape((total, half), BF16), shape((total, half), BF16), shape((total, LANES), F32)]
    outs += [shape((total, columns + hidden_units), F32), shape((total, columns + hidden_units), BF16)]
    outs += [shape((piece.shape[0], count), BF16) for piece, count in zip(pieces, counts)]
    got = run(kernel, outs, [expert, *pieces, weight_in, weight_out], 1)
    return (*got[:5], got[5:])


def expert_rows(own, came, gate, places, weight_in, weight_out, expert, groups):
    total = own.shape[0]
    half, columns = weight_in.shape
    hidden_units, number = columns // 2, len(places)
    rows = places[0].shape[0]
    targets, heights = ([(0, 0), (2, 0), (1, 0), (2, rows)], [rows, rows, 2 * rows])
    if number == 2:
        targets, heights = [(0, 0), (1, 0)], [rows, rows]

    def kernel(expert_ref, own_ref, came_ref, gate_ref, in_ref, out_ref, *refs):
        put, hidden_ref, pair_ref, flag_ref, outs = refs[:number], *refs[number : number + 3], refs[number + 3 :]
        gate_pre = own_ref[:, :hidden_units] + came_ref[:, :hidden_units].astype(F32)
        up_pre = own_ref[:, hidden_units:columns] + came_ref[:, hidden_units:columns].astype(F32)
        hidden_grad = own_ref[:, columns:] + came_ref[:, columns:].astype(F32)
        sig = jax.nn.sigmoid(gate_pre)
        act = gate_pre * sig
        hidden = (act * up_pre).astype(BF16)
        hidden_ref[...] = hidden
        pair_ref[:, :hidden_units] = (hidden_grad * up_pre * (sig * (1.0 + gate_pre * (1.0 - sig)))).astype(BF16)
        pair_ref[:, hidden_units:] = (hidden_grad * act).astype(BF16)
        gate = gate_ref[...]
        flag_ref[...] = gate[:8]
        score = jnp.sum(hidden.astype(F32) * hidden_grad, axis=1, keepdims=True)
        score = score / jnp.where(gate > 0.0, gate, 1.0)
        first = score.astype(BF16).astype(F32)
        lane = lax.broadcasted_iota(jnp.int32, (total, LANES), 1)
        expert = expert_ref[0]
        score = jnp.where(lane == expert, first, jnp.where(lane == expert + groups, score - first, 0.0)).astype(BF16)
        forth = (gate[:, :1] * dot_nt(hidden, out_ref[...])).astype(BF16)
        back = dot_nt(pair_ref[...], in_ref[...]).astype(BF16)
        start = 0
        for piece in range(number):
            count = put[piece].shape[1]
            place = put[piece][...]
            to, down = targets[piece]
            for rows, at in ((forth, 0), (back, half), (score, 2 * half)):
                rows = dot_nn(place, rows[start : start + count, :]).astype(BF16)
                outs[to][down : down + rows.shape[0], at : at + rows.shape[1]] = rows
            start += count

    shape = jax.ShapeDtypeStruct
    outs = [shape((total, hidden_units), BF16), shape((total, columns), BF16), shape((8, LANES), F32)]
    outs += [shape((height, 2 * half + LANES), BF16) for height in heights]
    got = run(kernel, outs, [expert, own, came, gate, weight_in, weight_out, *places], 1)
    return got[0], got[1], got[2], got[3:]


def ring_pairs(groups):
    chips = groups // 2
    levels = chips // 2
    order = [2 * z for z in range(levels)] + [2 * z + 1 for z in reversed(range(levels))]
    forward = []
    for place in range(chips):
        forward.append((2 * order[place], 2 * order[(place + 1) % chips]))
        forward.append((2 * order[(place + 1) % chips] + 1, 2 * order[place] + 1))
    backward = [(to, source) for source, to in forward]
    cores = [(index, index ^ 1) for index in range(groups)]
    return forward, backward, cores


def swap_pair(value):
    return lax.ppermute(value, "dp", [(0, 1), (1, 0)])


def swap_both(value):
    groups = lax.axis_size("expert")
    pairs = [(2 * e + r, 2 * (e ^ 1) + 1 - r) for e in range(groups) for r in range(2)]
    return lax.ppermute(value, ("expert", "dp"), pairs)


def by_replica(own, other, replica):
    return jnp.where(replica == 0, jnp.stack([own, other]), jnp.stack([other, own]))


def after(value, *anchors):
    anywhere = pl.BlockSpec(memory_space=pl.ANY)
    return pl.pallas_call(
        lambda *refs: None,
        out_shape=jax.ShapeDtypeStruct(value.shape, value.dtype),
        in_specs=[anywhere] * (1 + len(anchors)),
        out_specs=anywhere,
        input_output_aliases={0: 0},
        compiler_params=pltpu.CompilerParams(vmem_limit_bytes=1024 * 1024),
        cost_estimate=FREE,
    )(value, *anchors)


class Order:
    def __init__(self):
        self.last = None

    def __call__(self, value, *anchors):
        if self.last is not None:
            value = after(value, self.last, *anchors)
        self.last = value
        return value


def body_by_width(tokens, route_ids, gates, cotangent, w_gate_up, w_down):
    tok_dev, model_width = tokens.shape
    top_count = route_ids.shape[1]
    groups = lax.axis_size("expert")
    replica = lax.axis_index("dp")
    expert = lax.axis_index("expert").astype(jnp.int32).reshape(1)
    half = w_gate_up.shape[1]
    capacity = slot_capacity(tok_dev, top_count, groups)
    steps = groups // 4
    weight_in, weight_out = w_gate_up[0], w_down[0]
    forward, backward, cores = ring_pairs(groups)
    unit = 2 * tok_dev

    def swap_cores(value):
        return lax.ppermute(value, "expert", cores)

    def products(pieces):
        *kept, own, send, places = partial_products(
            pieces, weight_in, weight_out, expert, groups, tok_dev, capacity
        )
        return [kept, own, send, places, swap_pair(send)]

    def ring(block, step):
        return lax.ppermute(block if step < steps else block[:tok_dev], "expert", forward)

    order = Order()
    keep, send = prepare(tokens, route_ids.T, gates.T, cotangent, replica.astype(jnp.int32).reshape(1), groups)
    beside = order(swap_cores(keep))
    first = jnp.concatenate([keep, beside], axis=0)
    second = jnp.concatenate([order(swap_pair(send)), order(swap_both(send))], axis=0)
    chunks = [products([first, second])]

    def wait_for(number):
        chunks[number][4] = order(chunks[number][4], chunks[-1][0][2])

    first_next = order(ring(first, 1))
    for step in range(1, steps + 1):
        first = first_next
        if step == 2 or step == steps:
            wait_for(step - 2)
        if step > 2:
            first = order(ring(first, step), chunks[-1][0][2])
        if 3 <= step < steps:
            wait_for(step - 2)
        second = order(ring(second, step), chunks[-1][0][2])
        first_next = order(ring(first, 2)) if step == 1 else first
        first_other, second_other = swap_cores(first), order(swap_cores(second))
        chunks.append(products([first, first_other, second, second_other]))

    terms, grads, swapped = ([], []), [], []
    for number, ((x_rows, grad_rows, gate), own, _, places, came) in enumerate(chunks):
        if number == steps:
            came = order(came)
        elif number == steps - 1:
            came = order(came, flag, chunks[-1][0][2])
        elif number == steps - 2:
            came = after(came, flag, chunks[-1][0][2])
        elif number:
            came = after(came, flag)
        hidden, pair_grad, flag, out = expert_rows(own, came, gate, places, weight_in, weight_out, expert, groups)
        for stream in range(2):
            terms[stream].append([out[stream]])
        if number:
            swapped.append(swap_cores(out[2]))
        grads.append((x_rows, pair_grad, grad_rows, hidden))

    for number, other in enumerate(swapped, 1):
        half_way = other.shape[0] // 2
        terms[0][number].append(other[:half_way])
        terms[1][number].append(after(other[half_way:], flag))

    def pop_term(stream):
        return sum(term.astype(F32) for term in terms[stream].pop())

    totals = [pop_term(0), pop_term(1)]
    for step in reversed(range(steps)):
        for stream in (1, 0):
            came = lax.ppermute(totals[stream].astype(BF16), "expert", backward)
            if step == steps - 3 and stream == 1:
                came = after(came, grad_gate_up, grad_down)
            if step == steps - 2 and stream == 1:
                grads[0] = tuple(after(array, came) for array in grads[0])
                grad_gate_up, grad_down = outer_products(grads, 0, 1), outer_products(grads, 2, 3)
            base = pop_term(stream)
            if came.shape[0] < unit:
                totals[stream] = jnp.concatenate([base[:tok_dev] + came.astype(F32), base[tok_dev:]], axis=0)
            else:
                totals[stream] = base + came.astype(F32)

    there = totals[1][:, : 2 * half].astype(BF16)
    kept = totals[0][:tok_dev], swap_cores(totals[0][tok_dev:].astype(BF16))
    scores = kept[0][:, 2 * half :] + kept[1][:, 2 * half :].astype(F32)
    scores = scores[:, :groups] + scores[:, groups : 2 * groups]
    named = route_ids[:, :, None] == jnp.arange(groups, dtype=jnp.int32)[None, None, :]
    grad_gates = jnp.sum(jnp.where(named, scores[:, None, :], 0.0), axis=2)
    other = swap_pair(there[:tok_dev]), after(swap_both(there[tok_dev:]), scores)
    mixed, grad_tokens = join_halves(kept, other, half, replica.astype(jnp.int32).reshape(1))
    return (mixed, grad_tokens, grad_gates, grad_gate_up, grad_down)


def join_halves(kept, other, half, replica):
    rows = kept[0].shape[0]

    def kernel(replica_ref, mine_ref, beside_ref, across_ref, diagonal_ref, *outs):
        low = replica_ref[0] == 0
        for number, out in enumerate(outs):
            at = slice(number * half, (number + 1) * half)
            here = mine_ref[:, at] + beside_ref[:, at].astype(F32)
            there = across_ref[:, at].astype(F32) + diagonal_ref[:, at].astype(F32)
            out[:, :half] = jnp.where(low, here, there).astype(BF16)
            out[:, half:] = jnp.where(low, there, here).astype(BF16)

    out = jax.ShapeDtypeStruct((rows, 2 * half), BF16)
    return run(kernel, [out, out], [replica, *kept, *other], 1)


def outer_products(chunks, left, right):
    left = jnp.concatenate([chunk[left] for chunk in chunks])
    right = jnp.concatenate([chunk[right] for chunk in chunks])
    return lax.dot_general(left, right, (((0,), (0,)), ((), ())), preferred_element_type=F32).astype(BF16)[None]


def slot_capacity(tok_dev, top_count, experts):
    assignments = tok_dev * top_count
    return min(tok_dev, max(2, assignments // experts + max(1, assignments // (3 * experts))))


def body(tokens, route_ids, gates, cotangent, w_gate_up, w_down):
    groups, replicas = lax.axis_size("expert"), lax.axis_size("dp")
    gathered = 2 * groups * tokens.shape[0] * replicas * w_gate_up.shape[1] * 2
    small = gathered <= 8 * 1024 * 1024 and 3 * groups <= 128 and groups % 4 == 0 and groups >= 16
    if replicas == 2 and w_gate_up.shape[0] == 1 and small:
        return body_by_width(tokens, route_ids, gates, cotangent, w_gate_up, w_down)
    return body_by_slots(tokens, route_ids, gates, cotangent, w_gate_up, w_down)


def solution(mesh):
    placed = (
        P(("expert", "dp"), None),
        P(("expert", "dp"), None),
        P(("expert", "dp"), None),
        P(("expert", "dp"), None),
        P("expert", "dp", None),
        P("expert", "dp", None),
    )
    return jax.shard_map(
        body,
        mesh=mesh,
        in_specs=placed,
        out_specs=(
            P(("expert", "dp"), None),
            P(("expert", "dp"), None),
            P(("expert", "dp"), None),
            P("expert", "dp", None),
            P("expert", "dp", None),
        ),
        check_vma=False,
    )
```

```python
import jax
import jax.numpy as jnp
from jax import lax
from jax.experimental import pallas as pl
from jax.experimental.pallas import tpu as pltpu
from jax.sharding import PartitionSpec as P


def expert_forward(x_rows, weight_in, weight_out, hidden_units):
    pre_act = jnp.dot(x_rows, weight_in, preferred_element_type=jnp.float32)
    gate_pre = pre_act[:, :hidden_units]
    up_pre = pre_act[:, hidden_units:]
    sigmoid_gate = jax.nn.sigmoid(gate_pre)
    activation = gate_pre * sigmoid_gate
    hidden = (activation * up_pre).astype(jnp.bfloat16)
    expert_out = lax.dot_general(
        hidden, weight_out, (((1,), (1,)), ((), ())), preferred_element_type=jnp.float32
    ).astype(jnp.bfloat16)
    return (gate_pre, up_pre, sigmoid_gate, activation, hidden, expert_out)


def expert_backward(saved, grad_rows, weight_in, weight_out):
    gate_pre, up_pre, sigmoid_gate, activation, hidden, expert_out = saved
    hidden_grad = jnp.dot(grad_rows, weight_out, preferred_element_type=jnp.float32)
    gate_grad = (
        hidden_grad * up_pre * (sigmoid_gate * (1.0 + gate_pre * (1.0 - sigmoid_gate)))
    ).astype(jnp.bfloat16)
    up_grad = (hidden_grad * activation).astype(jnp.bfloat16)
    pair_grad = jnp.concatenate([gate_grad, up_grad], axis=1)
    input_grad = lax.dot_general(
        pair_grad, weight_in, (((1,), (1,)), ((), ())), preferred_element_type=jnp.float32
    ).astype(jnp.bfloat16)
    return (pair_grad, input_grad)


def outer_blocks(left, right, pieces):
    span = left.shape[1] // pieces
    results = []
    for piece in range(pieces):
        product = lax.dot_general(
            left[:, piece * span : (piece + 1) * span],
            right,
            (((0,), (0,)), ((), ())),
            preferred_element_type=jnp.float32,
        )
        results.append(product.astype(jnp.bfloat16))
    return jnp.stack(results, axis=0)


def replica_total(received):
    return jnp.sum(received.astype(jnp.float32), axis=0).astype(jnp.bfloat16)


def body_by_slots(tokens, route_ids, gates, cotangent, w_gate_up, w_down):
    tok_dev, model_width = tokens.shape
    top_count = route_ids.shape[1]
    groups = lax.axis_size("expert")
    replicas = lax.axis_size("dp")
    local_experts = w_gate_up.shape[0]
    hidden_units = w_down.shape[2]
    experts = groups * local_experts
    assignments = tok_dev * top_count
    capacity = min(tok_dev, max(2, assignments // experts + max(1, assignments // (3 * experts))))
    flat_ids = route_ids.reshape(assignments)
    onehot = (flat_ids[:, None] == jnp.arange(experts, dtype=jnp.int32)[None, :]).astype(jnp.int32)
    earlier = jnp.sum(
        (jnp.cumsum(onehot, axis=0, dtype=jnp.int32) - onehot) * onehot, axis=1, dtype=jnp.int32
    )
    position = flat_ids * capacity + earlier
    source = (
        jnp.full((experts * capacity,), assignments, jnp.int32)
        .at[position]
        .set(jnp.arange(assignments, dtype=jnp.int32))
    )
    token_row = source // top_count
    tok_pad = jnp.concatenate([tokens, jnp.zeros((1, model_width), jnp.bfloat16)], axis=0)
    cot_pad = jnp.concatenate([cotangent, jnp.zeros((1, model_width), jnp.bfloat16)], axis=0)
    gate_pad = jnp.concatenate([gates.reshape(assignments), jnp.zeros((1,), jnp.float32)], axis=0)
    send_rows = tok_pad[token_row].reshape(experts, capacity, model_width)
    send_grads = (gate_pad[source][:, None] * cot_pad[token_row].astype(jnp.float32)).astype(
        jnp.bfloat16
    )
    send_grads = send_grads.reshape(experts, capacity, model_width)
    weights_in, weights_out = (
        lax.all_gather(w_gate_up, "dp", axis=1, tiled=True),
        lax.all_gather(w_down, "dp", axis=1, tiled=True),
    )
    rows_in, grads_in = (
        lax.all_to_all(send_rows, "expert", split_axis=0, concat_axis=1, tiled=True),
        lax.all_to_all(send_grads, "expert", split_axis=0, concat_axis=1, tiled=True),
    )
    local = 0
    forward_parts = expert_forward(
        rows_in[local], weights_in[local], weights_out[local], hidden_units
    )
    saved_all = [forward_parts]
    out_list = [forward_parts[5]]
    down_list = [outer_blocks(grads_in[local], forward_parts[4], replicas)]
    expert_outs = jnp.stack(out_list, axis=0)
    down_stack = jnp.stack(down_list, axis=1)
    outs_back = lax.all_to_all(expert_outs, "expert", split_axis=1, concat_axis=0, tiled=True)
    local = 0
    pair_grad, input_grad = expert_backward(
        saved_all[local], grads_in[local], weights_in[local], weights_out[local]
    )
    input_list = [input_grad]
    gate_up_list = [outer_blocks(rows_in[local], pair_grad, replicas)]
    input_grads = jnp.stack(input_list, axis=0)
    gate_up_stack = jnp.stack(gate_up_list, axis=1)
    grads_back = lax.all_to_all(input_grads, "expert", split_axis=1, concat_axis=0, tiled=True)
    gate_up_received, down_received = (
        lax.all_to_all(gate_up_stack, "dp", split_axis=0, concat_axis=0, tiled=True),
        lax.all_to_all(down_stack, "dp", split_axis=0, concat_axis=0, tiled=True),
    )
    grad_gate_up = replica_total(gate_up_received)
    grad_down = replica_total(down_received)
    out_rows = outs_back.reshape(experts * capacity, model_width)[position].reshape(
        tok_dev, top_count, model_width
    )
    mixed = jnp.sum(gates[:, :, None] * out_rows.astype(jnp.float32), axis=1).astype(jnp.bfloat16)
    grad_gates = jnp.einsum("td,tkd->tk", cotangent, out_rows, preferred_element_type=jnp.float32)
    back_rows = grads_back.reshape(experts * capacity, model_width)[position].reshape(
        tok_dev, top_count, model_width
    )
    grad_tokens = jnp.sum(back_rows.astype(jnp.float32), axis=1).astype(jnp.bfloat16)
    return (mixed, grad_tokens, grad_gates, grad_gate_up, grad_down)


F32, BF16 = jnp.float32, jnp.bfloat16
LANES = 128
FREE = pl.CostEstimate(flops=0, bytes_accessed=0, transcendentals=0)


def run(kernel, outs, args, scalars=0):
    spaces = [pltpu.SMEM] * scalars + [pltpu.VMEM] * (len(args) - scalars)
    return pl.pallas_call(
        kernel,
        out_shape=outs,
        in_specs=[pl.BlockSpec(memory_space=space) for space in spaces],
        out_specs=[pl.BlockSpec(memory_space=pltpu.VMEM) for _ in outs],
        compiler_params=pltpu.CompilerParams(vmem_limit_bytes=10 * 1024 * 1024),
        cost_estimate=FREE,
    )(*args)


def dot_nn(left, right):
    return jnp.dot(left, right, preferred_element_type=F32)


def dot_nt(left, right):
    return lax.dot_general(left, right, (((1,), (1,)), ((), ())), preferred_element_type=F32)


def own_column(expert, groups):
    lane = lax.broadcasted_iota(jnp.int32, (1, LANES), 1)
    hit = (lane == expert) | (lane == expert + groups) | (lane == expert + 2 * groups)
    return jnp.where(hit, 1.0, 0.0)


def prepare(tokens, route_ids, gates, cotangent, replica, groups):
    rows, width = tokens.shape
    half = width // 2

    def kernel(replica_ref, tok_ref, id_ref, gate_ref, cot_ref, keep_ref, send_ref):
        low = replica_ref[0] == 0
        line = lax.broadcasted_iota(jnp.int32, (LANES, rows), 0)
        term = lax.div(line, groups)
        named = line - term * groups
        dense = jnp.zeros((LANES, rows), F32)
        for k in range(id_ref.shape[0]):
            dense = dense + jnp.where(id_ref[k : k + 1, :] == named, gate_ref[k : k + 1, :], 0.0)
        first = dense.astype(BF16).astype(F32)
        second = (dense - first).astype(BF16).astype(F32)
        third = dense - first - second
        meta = jnp.where(term == 0, first, jnp.where(term == 1, second, jnp.where(term == 2, third, 0.0))).astype(BF16)
        down = lax.broadcasted_iota(jnp.int32, (rows, rows), 0)
        along = lax.broadcasted_iota(jnp.int32, (rows, rows), 1)
        meta = dot_nt(jnp.where(down == along, 1.0, 0.0).astype(BF16), meta).astype(BF16)
        for ref, start in ((tok_ref, 0), (cot_ref, half + LANES)):
            left, right = ref[:, :half], ref[:, half:]
            keep_ref[:, start : start + half] = jnp.where(low, left, right)
            send_ref[:, start : start + half] = jnp.where(low, right, left)
        keep_ref[:, half : half + LANES] = meta
        send_ref[:, half : half + LANES] = meta

    out = jax.ShapeDtypeStruct((rows, width + LANES), BF16)
    args = [tokens, route_ids, gates, cotangent]
    return pl.pallas_call(
        kernel,
        grid=(1,),
        out_shape=[out, out],
        in_specs=[pl.BlockSpec(memory_space=pltpu.SMEM)] + [pl.BlockSpec(arg.shape, lambda i: (0, 0)) for arg in args],
        out_specs=[pl.BlockSpec(out.shape, lambda i: (0, 0))] * 2,
        compiler_params=pltpu.CompilerParams(vmem_limit_bytes=60 * 1024 * 1024),
        cost_estimate=FREE,
    )(replica, *args)


def partial_products(pieces, weight_in, weight_out, expert, groups, tok_dev, capacity):
    counts = [piece.shape[0] // tok_dev * capacity for piece in pieces]
    total, number = sum(counts), len(pieces)
    half, columns = weight_in.shape
    hidden_units = weight_out.shape[1]

    def kernel(expert_ref, *refs):
        rows_refs, refs = refs[:number], refs[number:]
        in_ref, out_ref, x_ref, grad_ref, gate_ref, own_ref, send_ref = refs[:7]
        places = refs[7:]
        column = own_column(expert_ref[0], groups)
        column_rows = jnp.broadcast_to(column, (8, LANES)).astype(BF16)
        start = 0
        for piece in range(number):
            rows, count = rows_refs[piece].shape[0], counts[piece]
            meta = rows_refs[piece][:, half : half + LANES]
            gate_row = dot_nt(column_rows, meta)
            gate_col = jnp.sum(meta.astype(F32) * column, axis=1, keepdims=True)
            down = lax.broadcasted_iota(jnp.int32, (rows, rows), 0)
            along = lax.broadcasted_iota(jnp.int32, (rows, rows), 1)
            first_down, first_along = jnp.zeros_like(down), jnp.zeros_like(along)
            base_down, base_along = jnp.zeros_like(down), jnp.zeros_like(along)
            for device in range(1, rows // tok_dev):
                first_down += jnp.where(down >= device * tok_dev, tok_dev, 0)
                first_along += jnp.where(along >= device * tok_dev, tok_dev, 0)
                base_down += jnp.where(down >= device * tok_dev, capacity, 0)
                base_along += jnp.where(along >= device * tok_dev, capacity, 0)
            lower = jnp.where((along < down) & (along >= first_down), 1.0, 0.0).astype(BF16)
            upper = jnp.where((down < along) & (down >= first_along), 1.0, 0.0).astype(BF16)
            on_row = jnp.where(gate_row > 0.0, 1.0, 0.0)
            on_col = jnp.where(gate_col > 0.0, 1.0, 0.0)
            rank_row = dot_nn(on_row.astype(BF16), upper)
            rank_col = dot_nn(lower, jnp.broadcast_to(on_col, (rows, LANES)).astype(BF16))
            place_row = jnp.where(on_row > 0.0, rank_row + base_along[:8].astype(F32), -1.0)[:1, :]
            place_col = jnp.where(on_col > 0.0, rank_col[:, :1] + base_down[:, :1].astype(F32), -1.0)
            slot_down = lax.broadcasted_iota(jnp.int32, (count, rows), 0).astype(F32)
            slot_along = lax.broadcasted_iota(jnp.int32, (rows, count), 1).astype(F32)
            pick = jnp.where(place_row == slot_down, 1.0, 0.0).astype(BF16)
            places[piece][...] = jnp.where(place_col == slot_along, 1.0, 0.0).astype(BF16)
            picked = dot_nn(pick, rows_refs[piece][...])
            x_ref[start : start + count, :] = picked[:, :half].astype(BF16)
            gate = jnp.sum(picked[:, half : half + LANES] * column, axis=1, keepdims=True)
            gate_ref[start : start + count, :] = jnp.broadcast_to(gate, (count, LANES))
            grad_ref[start : start + count, :] = (gate * picked[:, half + LANES :]).astype(BF16)
            start += count
        for left, right, at in ((x_ref, in_ref, 0), (grad_ref, out_ref, columns)):
            part = dot_nn(left[...], right[...])
            own_ref[:, at : at + part.shape[1]] = part
            part = part.astype(BF16)
            send_ref[: total // 2, at : at + part.shape[1]] = part[total // 2 :]
            send_ref[total // 2 :, at : at + part.shape[1]] = part[: total // 2]

    shape = jax.ShapeDtypeStruct
    outs = [shape((total, half), BF16), shape((total, half), BF16), shape((total, LANES), F32)]
    outs += [shape((total, columns + hidden_units), F32), shape((total, columns + hidden_units), BF16)]
    outs += [shape((piece.shape[0], count), BF16) for piece, count in zip(pieces, counts)]
    got = run(kernel, outs, [expert, *pieces, weight_in, weight_out], 1)
    return (*got[:5], got[5:])


def expert_rows(own, came, gate, places, weight_in, weight_out, expert, groups):
    total = own.shape[0]
    half, columns = weight_in.shape
    hidden_units, number = columns // 2, len(places)
    rows = places[0].shape[0]
    targets, heights = ([(0, 0), (2, 0), (1, 0), (2, rows)], [rows, rows, 2 * rows])
    if number == 2:
        targets, heights = [(0, 0), (1, 0)], [rows, rows]

    def kernel(expert_ref, own_ref, came_ref, gate_ref, in_ref, out_ref, *refs):
        put, hidden_ref, pair_ref, flag_ref, outs = refs[:number], *refs[number : number + 3], refs[number + 3 :]
        gate_pre = own_ref[:, :hidden_units] + came_ref[:, :hidden_units].astype(F32)
        up_pre = own_ref[:, hidden_units:columns] + came_ref[:, hidden_units:columns].astype(F32)
        hidden_grad = own_ref[:, columns:] + came_ref[:, columns:].astype(F32)
        sig = jax.nn.sigmoid(gate_pre)
        act = gate_pre * sig
        hidden = (act * up_pre).astype(BF16)
        hidden_ref[...] = hidden
        pair_ref[:, :hidden_units] = (hidden_grad * up_pre * (sig * (1.0 + gate_pre * (1.0 - sig)))).astype(BF16)
        pair_ref[:, hidden_units:] = (hidden_grad * act).astype(BF16)
        gate = gate_ref[...]
        flag_ref[...] = gate[:8]
        score = jnp.sum(hidden.astype(F32) * hidden_grad, axis=1, keepdims=True)
        score = score / jnp.where(gate > 0.0, gate, 1.0)
        first = score.astype(BF16).astype(F32)
        lane = lax.broadcasted_iota(jnp.int32, (total, LANES), 1)
        expert = expert_ref[0]
        score = jnp.where(lane == expert, first, jnp.where(lane == expert + groups, score - first, 0.0)).astype(BF16)
        forth = (gate[:, :1] * dot_nt(hidden, out_ref[...])).astype(BF16)
        back = dot_nt(pair_ref[...], in_ref[...]).astype(BF16)
        start = 0
        for piece in range(number):
            count = put[piece].shape[1]
            place = put[piece][...]
            to, down = targets[piece]
            for rows, at in ((forth, 0), (back, half), (score, 2 * half)):
                rows = dot_nn(place, rows[start : start + count, :]).astype(BF16)
                outs[to][down : down + rows.shape[0], at : at + rows.shape[1]] = rows
            start += count

    shape = jax.ShapeDtypeStruct
    outs = [shape((total, hidden_units), BF16), shape((total, columns), BF16), shape((8, LANES), F32)]
    outs += [shape((height, 2 * half + LANES), BF16) for height in heights]
    got = run(kernel, outs, [expert, own, came, gate, weight_in, weight_out, *places], 1)
    return got[0], got[1], got[2], got[3:]


def ring_pairs(groups):
    chips = groups // 2
    levels = chips // 2
    order = [2 * z for z in range(levels)] + [2 * z + 1 for z in reversed(range(levels))]
    forward = []
    for place in range(chips):
        forward.append((2 * order[place], 2 * order[(place + 1) % chips]))
        forward.append((2 * order[(place + 1) % chips] + 1, 2 * order[place] + 1))
    backward = [(to, source) for source, to in forward]
    cores = [(index, index ^ 1) for index in range(groups)]
    return forward, backward, cores


def swap_pair(value):
    return lax.ppermute(value, "dp", [(0, 1), (1, 0)])


def swap_both(value):
    groups = lax.axis_size("expert")
    pairs = [(2 * e + r, 2 * (e ^ 1) + 1 - r) for e in range(groups) for r in range(2)]
    return lax.ppermute(value, ("expert", "dp"), pairs)


def by_replica(own, other, replica):
    return jnp.where(replica == 0, jnp.stack([own, other]), jnp.stack([other, own]))


def after(value, *anchors):
    anywhere = pl.BlockSpec(memory_space=pl.ANY)
    return pl.pallas_call(
        lambda *refs: None,
        out_shape=jax.ShapeDtypeStruct(value.shape, value.dtype),
        in_specs=[anywhere] * (1 + len(anchors)),
        out_specs=anywhere,
        input_output_aliases={0: 0},
        compiler_params=pltpu.CompilerParams(vmem_limit_bytes=1024 * 1024),
        cost_estimate=FREE,
    )(value, *anchors)


class Order:
    def __init__(self):
        self.last = None

    def __call__(self, value, *anchors):
        if self.last is not None:
            value = after(value, self.last, *anchors)
        self.last = value
        return value


def body_by_width(tokens, route_ids, gates, cotangent, w_gate_up, w_down):
    tok_dev, model_width = tokens.shape
    top_count = route_ids.shape[1]
    groups = lax.axis_size("expert")
    replica = lax.axis_index("dp")
    expert = lax.axis_index("expert").astype(jnp.int32).reshape(1)
    half = w_gate_up.shape[1]
    capacity = slot_capacity(tok_dev, top_count, groups)
    steps = groups // 4
    weight_in, weight_out = w_gate_up[0], w_down[0]
    forward, backward, cores = ring_pairs(groups)
    unit = 2 * tok_dev

    def swap_cores(value):
        return lax.ppermute(value, "expert", cores)

    def products(pieces):
        *kept, own, send, places = partial_products(
            pieces, weight_in, weight_out, expert, groups, tok_dev, capacity
        )
        return [kept, own, send, places, swap_pair(send)]

    def ring(block, step):
        return lax.ppermute(block if step < steps else block[:tok_dev], "expert", forward)

    order = Order()
    keep, send = prepare(tokens, route_ids.T, gates.T, cotangent, replica.astype(jnp.int32).reshape(1), groups)
    beside = order(swap_cores(keep))
    first = jnp.concatenate([keep, beside], axis=0)
    second = jnp.concatenate([order(swap_pair(send)), order(swap_both(send))], axis=0)
    chunks = [products([first, second])]

    def wait_for(number):
        chunks[number][4] = order(chunks[number][4], chunks[-1][0][2])

    lead = steps // 2
    first_next = order(ring(first, 1))
    for step in range(1, steps + 1):
        first = first_next
        if step == 2 or step == steps:
            wait_for(step - 2)
        if step > lead + 1:
            first = order(ring(first, step), chunks[-1][0][2])
        if 3 <= step < steps:
            wait_for(step - 2)
        second = order(ring(second, step), chunks[-1][0][2])
        first_next = order(ring(first, step + 1)) if step <= lead else first
        first_other, second_other = swap_cores(first), order(swap_cores(second))
        chunks.append(products([first, first_other, second, second_other]))

    terms, grads, swapped = ([], []), [], []
    for number, ((x_rows, grad_rows, gate), own, _, places, came) in enumerate(chunks):
        if number == steps:
            came = order(came)
        elif number == steps - 1:
            came = order(came, flag, chunks[-1][0][2])
        elif number == steps - 2:
            came = after(came, flag, chunks[-1][0][2])
        elif number:
            came = after(came, flag)
        hidden, pair_grad, flag, out = expert_rows(own, came, gate, places, weight_in, weight_out, expert, groups)
        for stream in range(2):
            terms[stream].append([out[stream]])
        if number:
            swapped.append(swap_cores(out[2]))
        grads.append((x_rows, pair_grad, grad_rows, hidden))

    for number, other in enumerate(swapped, 1):
        half_way = other.shape[0] // 2
        terms[0][number].append(other[:half_way])
        terms[1][number].append(after(other[half_way:], flag))

    def pop_term(stream):
        return sum(term.astype(F32) for term in terms[stream].pop())

    totals = [pop_term(0), pop_term(1)]
    for step in reversed(range(steps)):
        for stream in (1, 0):
            came = lax.ppermute(totals[stream].astype(BF16), "expert", backward)
            if step == steps - 3 and stream == 1:
                came = after(came, grad_gate_up, grad_down)
            if step == steps - 2 and stream == 1:
                grads[0] = tuple(after(array, came) for array in grads[0])
                grad_gate_up, grad_down = outer_products(grads, 0, 1), outer_products(grads, 2, 3)
            base = pop_term(stream)
            if came.shape[0] < unit:
                totals[stream] = jnp.concatenate([base[:tok_dev] + came.astype(F32), base[tok_dev:]], axis=0)
            else:
                totals[stream] = base + came.astype(F32)

    there = totals[1][:, : 2 * half].astype(BF16)
    kept = totals[0][:tok_dev], swap_cores(totals[0][tok_dev:].astype(BF16))
    scores = kept[0][:, 2 * half :] + kept[1][:, 2 * half :].astype(F32)
    scores = scores[:, :groups] + scores[:, groups : 2 * groups]
    named = route_ids[:, :, None] == jnp.arange(groups, dtype=jnp.int32)[None, None, :]
    grad_gates = jnp.sum(jnp.where(named, scores[:, None, :], 0.0), axis=2)
    other = swap_pair(there[:tok_dev]), after(swap_both(there[tok_dev:]), scores)
    mixed, grad_tokens = join_halves(kept, other, half, replica.astype(jnp.int32).reshape(1))
    return (mixed, grad_tokens, grad_gates, grad_gate_up, grad_down)


def join_halves(kept, other, half, replica):
    rows = kept[0].shape[0]

    def kernel(replica_ref, mine_ref, beside_ref, across_ref, diagonal_ref, *outs):
        low = replica_ref[0] == 0
        for number, out in enumerate(outs):
            at = slice(number * half, (number + 1) * half)
            here = mine_ref[:, at] + beside_ref[:, at].astype(F32)
            there = across_ref[:, at].astype(F32) + diagonal_ref[:, at].astype(F32)
            out[:, :half] = jnp.where(low, here, there).astype(BF16)
            out[:, half:] = jnp.where(low, there, here).astype(BF16)

    out = jax.ShapeDtypeStruct((rows, 2 * half), BF16)
    return run(kernel, [out, out], [replica, *kept, *other], 1)


def outer_products(chunks, left, right):
    left = jnp.concatenate([chunk[left] for chunk in chunks])
    right = jnp.concatenate([chunk[right] for chunk in chunks])
    return lax.dot_general(left, right, (((0,), (0,)), ((), ())), preferred_element_type=F32).astype(BF16)[None]


def slot_capacity(tok_dev, top_count, experts):
    assignments = tok_dev * top_count
    return min(tok_dev, max(2, assignments // experts + max(1, assignments // (3 * experts))))


def body(tokens, route_ids, gates, cotangent, w_gate_up, w_down):
    groups, replicas = lax.axis_size("expert"), lax.axis_size("dp")
    gathered = 2 * groups * tokens.shape[0] * replicas * w_gate_up.shape[1] * 2
    small = gathered <= 8 * 1024 * 1024 and 3 * groups <= 128 and groups % 4 == 0 and groups >= 16
    if replicas == 2 and w_gate_up.shape[0] == 1 and small:
        return body_by_width(tokens, route_ids, gates, cotangent, w_gate_up, w_down)
    return body_by_slots(tokens, route_ids, gates, cotangent, w_gate_up, w_down)


def solution(mesh):
    placed = (
        P(("expert", "dp"), None),
        P(("expert", "dp"), None),
        P(("expert", "dp"), None),
        P(("expert", "dp"), None),
        P("expert", "dp", None),
        P("expert", "dp", None),
    )
    return jax.shard_map(
        body,
        mesh=mesh,
        in_specs=placed,
        out_specs=(
            P(("expert", "dp"), None),
            P(("expert", "dp"), None),
            P(("expert", "dp"), None),
            P("expert", "dp", None),
            P("expert", "dp", None),
        ),
        check_vma=False,
    )
```
